32 devices in a mesh: groups: 2 (over x), gx: 16 (over z, y, core).
Axes of the slice: x: 2, y: 2, z: 4, core: 2. Of those that a mesh axis runs over, the one named last changes fastest.
Arguments:
- tokens: bfloat16 [256, 8192], P(('groups', 'gx')), parts along dimension 0, may hold values from -6 to 6
- gate_weight: bfloat16 [8192, 3584], P(None, 'gx'), may hold values from -0.0625 to 0.0625
- up_weight: bfloat16 [8192, 3584], P(None, 'gx'), may hold values from -0.0625 to 0.0625
- down_weight: bfloat16 [3584, 8192], P('gx'), may hold values from -0.09375 to 0.09375
- sign_pattern: int32 [8192], replicated, may hold values from -1 to 1, as said below
Outputs:
- mixed: bfloat16 [256, 8192], P(('groups', 'gx')), parts along dimension 0
The draws below stay inside these ranges and needn't reach their ends.
There are 2 independent parts, one for each index of `groups`. The reference program is written for one: setup_inputs(seed, part) draws one part's arguments, and reference() takes and returns one part's arrays. A program takes and returns all parts, laid end to end along the dimension named above; an argument that names none is the same for every part. Nothing has to cross between parts.
Inputs may be any that keep to these rules, and one draw needn't show every extreme that they name: `sign_pattern`: each entry is -1 or 1.
All inputs are finite; a program needn't handle non-finite values.
Results may differ from the reference program's by a relative error of at most 0.0052.
Values may be sent and summed in bfloat16 or wider, within the bound.
No kernel may reach another device: no remote copies, remote signals or barrier semaphores. Data moves between devices by JAX's collectives and lax.ppermute only.
A program may use at most 128 MiB of HBM per device.

```python
import jax
import jax.numpy as jnp
from jax import lax

D = 8192
BLOCK = 128
NB = 64
FF = 3584
ROWS = 128


def draw_sign_pattern(key, part):
    key = jax.random.fold_in(key, 7)
    flips = jax.random.randint(key, (D,), 0, 2, dtype=jnp.int32)
    return 2 * flips - 1


def block_levels(rng, extent, shards, low, top_value):
    level = 1.0
    for position, parts in shards:
        draws = jax.random.uniform(jax.random.fold_in(jax.random.fold_in(rng, 6), position), (parts,), jnp.float32, low / len(shards), top_value / len(shards))
        level = level * jnp.repeat(jnp.exp(draws), extent[position] // parts).reshape((-1,) + (1,) * (len(extent) - 1 - position))
    return level


def scatter_about(key, extent, scale, reach, pieces=(), kind=jnp.bfloat16):
    factor_of = block_levels(key, extent, pieces, -0.22, 0.18) if pieces else 1.0
    array = jax.random.normal(key, extent, jnp.float32) * scale * factor_of
    return jnp.minimum(jnp.maximum(array, -reach), reach).astype(kind)


def setup_inputs(seed: int = 0, part: int = 0) -> dict:
    arg_keys = jax.random.split(jax.random.key(seed), 6)
    part_splits = jax.random.split(jax.random.fold_in(arg_keys[5], part), 6)
    tokens = scatter_about(part_splits[0], (ROWS, D), 1.0, 6.0, ((0, 16),))
    gate_weight = scatter_about(arg_keys[1], (D, FF), D ** -0.5, 0.0625, ((1, 16),))
    up_weight = scatter_about(arg_keys[2], (D, FF), D ** -0.5, 0.0625, ((1, 16),))
    down_weight = scatter_about(arg_keys[3], (FF, D), FF ** -0.5, 0.09375, ((0, 16),))
    sign_pattern = draw_sign_pattern(jax.random.fold_in(arg_keys[5], 71), part)
    return dict(tokens=tokens, gate_weight=gate_weight, up_weight=up_weight, down_weight=down_weight, sign_pattern=sign_pattern)


def hadamard_table(order):
    row_index = jnp.arange(order, dtype=jnp.int32)[:, None]
    col_index = jnp.arange(order, dtype=jnp.int32)[None, :]
    common = jnp.bitwise_and(row_index, col_index)
    parity = jnp.zeros((order, order), jnp.int32)
    for shift_bit in range(order.bit_length() - 1):
        parity = parity + jnp.bitwise_and(jnp.right_shift(common, shift_bit), 1)
    values = 1.0 - 2.0 * jnp.remainder(parity, 2).astype(jnp.float32)
    return values / jnp.sqrt(jnp.float32(order))

def reference(tokens, gate_weight, up_weight, down_weight, sign_pattern):
    gate = jnp.dot(tokens, gate_weight, preferred_element_type=jnp.float32)
    up = jnp.dot(tokens, up_weight, preferred_element_type=jnp.float32)
    hidden = (jax.nn.silu(gate) * up).astype(jnp.bfloat16)
    projected = jnp.dot(hidden, down_weight, preferred_element_type=jnp.float32)
    rotation = hadamard_table(BLOCK)
    sign_blocks = sign_pattern.astype(jnp.float32).reshape(NB, BLOCK)
    blocks = projected.reshape(ROWS, NB, BLOCK) * sign_blocks
    rotated = jnp.einsum('rbk,kl->rbl', blocks, rotation, precision=lax.Precision.HIGHEST)
    return rotated.reshape(ROWS, D).astype(jnp.bfloat16)
```

```python
import jax
import jax.numpy as jnp
from jax import lax
from jax.sharding import PartitionSpec as P


def hadamard_table(order):
    row_index = jnp.arange(order, dtype=jnp.int32)[:, None]
    col_index = jnp.arange(order, dtype=jnp.int32)[None, :]
    common = jnp.bitwise_and(row_index, col_index)
    parity = jnp.zeros((order, order), jnp.int32)
    for shift_bit in range(order.bit_length() - 1):
        parity = parity + jnp.bitwise_and(jnp.right_shift(common, shift_bit), 1)
    values = 1.0 - 2.0 * jnp.remainder(parity, 2).astype(jnp.float32)
    return values / jnp.sqrt(jnp.float32(order))


def rotate_rows(values, sign_blocks, rotation):
    count, features = values.shape
    blocks = values.reshape(count, features // 128, 128) * sign_blocks
    rotated = jnp.einsum("rbk,kl->rbl", blocks, rotation, precision=lax.Precision.HIGHEST)
    return rotated.reshape(count, features)


def solution(mesh):
    members = mesh.shape["gx"]
    assert members & (members - 1) == 0 and members >= 4

    def swap(value, mask):
        return lax.ppermute(value, "gx", [(i, i ^ mask) for i in range(members)])

    def on_device(tokens, gate_weight, up_weight, down_weight, sign_pattern):
        rows, features = tokens.shape
        rotation = hadamard_table(128)
        sign_blocks = sign_pattern.astype(jnp.float32).reshape(features // 128, 128)
        column = jnp.concatenate([tokens] + [swap(tokens, m) for m in range(4, members, 4)])
        plane = jnp.concatenate([column, swap(column, 2)])
        gathered = jnp.concatenate([plane, swap(plane, 1)])
        gate = jnp.dot(gathered, gate_weight, preferred_element_type=jnp.float32)
        up = jnp.dot(gathered, up_weight, preferred_element_type=jnp.float32)
        hidden = (jax.nn.silu(gate) * up).astype(jnp.bfloat16)
        total = jnp.dot(hidden, down_weight, preferred_element_type=jnp.float32)
        for mask in (1, 2):
            half = total.shape[0] // 2
            total = total[:half] + swap(total[half:].astype(jnp.bfloat16), mask).astype(jnp.float32)
        arrived = [
            swap(total[m // 4 * rows : (m // 4 + 1) * rows].astype(jnp.bfloat16), m)
            for m in range(4, members, 4)
        ]
        summed = total[:rows]
        for block in arrived:
            summed = summed + block.astype(jnp.float32)
        return rotate_rows(summed, sign_blocks, rotation).astype(jnp.bfloat16)

    placed = (P(("groups", "gx"), None), P(None, "gx"), P(None, "gx"), P("gx", None), P())
    return jax.shard_map(
        on_device, mesh=mesh, in_specs=placed, out_specs=P(("groups", "gx"), None), check_vma=False
    )
```

```python
import jax
import jax.numpy as jnp
from jax import lax
from jax.sharding import PartitionSpec as P


def hadamard_table(order):
    row_index = jnp.arange(order, dtype=jnp.int32)[:, None]
    col_index = jnp.arange(order, dtype=jnp.int32)[None, :]
    common = jnp.bitwise_and(row_index, col_index)
    parity = jnp.zeros((order, order), jnp.int32)
    for shift_bit in range(order.bit_length() - 1):
        parity = parity + jnp.bitwise_and(jnp.right_shift(common, shift_bit), 1)
    values = 1.0 - 2.0 * jnp.remainder(parity, 2).astype(jnp.float32)
    return values / jnp.sqrt(jnp.float32(order))


def rotate_rows(values, sign_blocks, rotation):
    count, features = values.shape
    blocks = values.reshape(count, features // 128, 128) * sign_blocks
    rotated = jnp.einsum("rbk,kl->rbl", blocks, rotation, precision=lax.Precision.HIGHEST)
    return rotated.reshape(count, features)


def solution(mesh):
    members = mesh.shape["gx"]
    assert members & (members - 1) == 0 and members >= 4

    def swap(value, mask):
        return lax.ppermute(value, "gx", [(i, i ^ mask) for i in range(members)])

    lines = [list(range(first, members, 4)) for first in range(4)]

    def along_z(value):
        return lax.all_to_all(value, "gx", 0, 0, axis_index_groups=lines)

    def on_device(tokens, gate_weight, up_weight, down_weight, sign_pattern):
        rows, features = tokens.shape
        rotation = hadamard_table(128)
        sign_blocks = sign_pattern.astype(jnp.float32).reshape(features // 128, 128)
        column = jnp.broadcast_to(tokens[None], (members // 4, rows, features))
        column = along_z(column).reshape(members // 4 * rows, features)
        plane = jnp.concatenate([column, swap(column, 2)])
        gathered = jnp.concatenate([plane, swap(plane, 1)])
        gate = jnp.dot(gathered, gate_weight, preferred_element_type=jnp.float32)
        up = jnp.dot(gathered, up_weight, preferred_element_type=jnp.float32)
        hidden = (jax.nn.silu(gate) * up).astype(jnp.bfloat16)
        total = jnp.dot(hidden, down_weight, preferred_element_type=jnp.float32)
        for mask in (1, 2):
            half = total.shape[0] // 2
            total = total[:half] + swap(total[half:].astype(jnp.bfloat16), mask).astype(jnp.float32)
        arrived = along_z(total.astype(jnp.bfloat16).reshape(members // 4, rows, features))
        summed = jnp.sum(arrived.astype(jnp.float32), axis=0)
        return rotate_rows(summed, sign_blocks, rotation).astype(jnp.bfloat16)

    placed = (P(("groups", "gx"), None), P(None, "gx"), P(None, "gx"), P("gx", None), P())
    return jax.shard_map(
        on_device, mesh=mesh, in_specs=placed, out_specs=P(("groups", "gx"), None), check_vma=False
    )
```

```python
import jax
import jax.numpy as jnp
from jax import lax
from jax.sharding import PartitionSpec as P


def hadamard_table(order):
    row_index = jnp.arange(order, dtype=jnp.int32)[:, None]
    col_index = jnp.arange(order, dtype=jnp.int32)[None, :]
    common = jnp.bitwise_and(row_index, col_index)
    parity = jnp.zeros((order, order), jnp.int32)
    for shift_bit in range(order.bit_length() - 1):
        parity = parity + jnp.bitwise_and(jnp.right_shift(common, shift_bit), 1)
    values = 1.0 - 2.0 * jnp.remainder(parity, 2).astype(jnp.float32)
    return values / jnp.sqrt(jnp.float32(order))


def rotate_rows(values, sign_blocks, rotation):
    count, features = values.shape
    blocks = values.reshape(count, features // 128, 128) * sign_blocks
    rotated = jnp.einsum("rbk,kl->rbl", blocks, rotation, precision=lax.Precision.HIGHEST)
    return rotated.reshape(count, features)


def solution(mesh):
    members = mesh.shape["gx"]
    assert members & (members - 1) == 0 and members >= 8

    steps = []
    mask = members // 2
    while mask > 4:
        steps.append((mask, mask))
        mask //= 2
    steps += [(4, 2), (2, 4), (1, 1)]

    def swap(value, masks):
        return lax.ppermute(value, "gx", [(i, i ^ masks[i % 2]) for i in range(members)])

    def on_device(tokens, gate_weight, up_weight, down_weight, sign_pattern):
        rows, features = tokens.shape
        rotation = hadamard_table(128)
        sign_blocks = sign_pattern.astype(jnp.float32).reshape(features // 128, 128)
        gathered = tokens
        for masks in steps:
            gathered = jnp.concatenate([gathered, swap(gathered, masks)])
        gate = jnp.dot(gathered, gate_weight, preferred_element_type=jnp.float32)
        up = jnp.dot(gathered, up_weight, preferred_element_type=jnp.float32)
        hidden = (jax.nn.silu(gate) * up).astype(jnp.bfloat16)
        total = jnp.dot(hidden, down_weight, preferred_element_type=jnp.float32)
        for masks in reversed(steps):
            half = total.shape[0] // 2
            total = total[:half] + swap(total[half:].astype(jnp.bfloat16), masks).astype(jnp.float32)
        return rotate_rows(total, sign_blocks, rotation).astype(jnp.bfloat16)

    placed = (P(("groups", "gx"), None), P(None, "gx"), P(None, "gx"), P("gx", None), P())
    return jax.shard_map(
        on_device, mesh=mesh, in_specs=placed, out_specs=P(("groups", "gx"), None), check_vma=False
    )
```

```python
import functools
import math

import jax
import jax.numpy as jnp
from jax import lax
from jax.experimental import pallas as pl
from jax.experimental.pallas import tpu as pltpu
from jax.sharding import PartitionSpec as P

CHUNKS = 2
BLOCK = 128
NT = (((1,), (1,)), ((), ()))


def vmem():
    return pl.BlockSpec(memory_space=pltpu.VMEM)


def gate_up_kernel(start, width, has_sum, last, *refs):
    gate_w, up_w, *refs = refs
    pieces, refs = refs[:4], refs[4:]
    if has_sum:
        gate_in, up_in, *refs = refs
    if last:
        hidden_ref, gate_sum, up_sum = refs
    else:
        gate_sum, up_sum = refs
    if has_sum:
        gate_sum[...] = gate_in[...]
        up_sum[...] = up_in[...]
    else:
        gate_sum[...] = jnp.zeros_like(gate_sum)
        up_sum[...] = jnp.zeros_like(up_sum)
    tile = math.gcd(width, 1024)

    def step(index, carry):
        here = pl.ds(pl.multiple_of(index * tile, tile), tile)
        there = pl.ds(pl.multiple_of(start + index * tile, tile), tile)
        rows = jnp.concatenate([piece[:, here] for piece in pieces])
        gate_sum[...] += lax.dot_general(gate_w[:, there], rows, NT, preferred_element_type=jnp.float32)
        up_sum[...] += lax.dot_general(up_w[:, there], rows, NT, preferred_element_type=jnp.float32)
        return carry

    lax.fori_loop(0, width // tile, step, 0)
    if last:
        gate = gate_sum[...]
        hidden = gate / (1.0 + jnp.exp(-gate)) * up_sum[...]
        hidden_ref[...] = hidden.T.astype(jnp.bfloat16)


def gate_up(gate_w, up_w, pieces, sums, start, last):
    units, rows, width = gate_w.shape[0], sum(p.shape[0] for p in pieces), pieces[0].shape[1]
    total = jax.ShapeDtypeStruct((units, rows), jnp.float32)
    return pl.pallas_call(
        functools.partial(gate_up_kernel, start, width, bool(sums), last),
        out_shape=jax.ShapeDtypeStruct((rows, units), jnp.bfloat16) if last else (total, total),
        in_specs=[vmem()] * (6 + len(sums)),
        out_specs=vmem() if last else (vmem(), vmem()),
        scratch_shapes=[pltpu.VMEM((units, rows), jnp.float32)] * 2 if last else [],
        cost_estimate=pl.CostEstimate(
            flops=4 * units * rows * width, bytes_accessed=4 * units * width, transcendentals=0
        ),
        compiler_params=pltpu.CompilerParams(vmem_limit_bytes=40 << 20),
    )(gate_w, up_w, *pieces, *sums)


def down_kernel(start, hidden_ref, down_ref, keep_ref, send_ref):
    half, width = keep_ref.shape
    tile = math.gcd(width, 512)

    def step(index, carry):
        here = pl.ds(pl.multiple_of(index * tile, tile), tile)
        there = pl.ds(pl.multiple_of(start + index * tile, tile), tile)
        part = jnp.dot(hidden_ref[...], down_ref[:, there], preferred_element_type=jnp.float32)
        keep_ref[:, here] = part[:half]
        send_ref[:, here] = part[half:].astype(jnp.bfloat16)
        return carry

    lax.fori_loop(0, width // tile, step, 0)


def down(hidden, down_w, start, width):
    rows, units = hidden.shape
    return pl.pallas_call(
        functools.partial(down_kernel, start),
        out_shape=(
            jax.ShapeDtypeStruct((rows // 2, width), jnp.float32),
            jax.ShapeDtypeStruct((rows // 2, width), jnp.bfloat16),
        ),
        in_specs=[vmem()] * 2,
        out_specs=(vmem(), vmem()),
        cost_estimate=pl.CostEstimate(
            flops=2 * units * rows * width, bytes_accessed=2 * units * width, transcendentals=0
        ),
        compiler_params=pltpu.CompilerParams(vmem_limit_bytes=40 << 20),
    )(hidden, down_w)


def rotate_kernel(count, *refs):
    sums, arrived = refs[:count], refs[count : 2 * count]
    sign_ref, out_ref = refs[2 * count :]
    rows, width = sums[0].shape
    common = lax.broadcasted_iota(jnp.int32, (BLOCK, BLOCK), 0) & lax.broadcasted_iota(
        jnp.int32, (BLOCK, BLOCK), 1
    )
    for shift in (4, 2, 1):
        common = common ^ (common >> shift)
    flips = (1 - 2 * (common & 1)).astype(jnp.float32).astype(jnp.bfloat16)
    scale = 1.0 / math.sqrt(BLOCK)
    for c in range(count):
        value = (sums[c][...] + arrived[c][...].astype(jnp.float32)) * sign_ref[
            :, c * width : (c + 1) * width
        ].astype(jnp.float32)
        value = jnp.concatenate([value[:, b : b + BLOCK] for b in range(0, width, BLOCK)])
        high = value.astype(jnp.bfloat16)
        low = (value - high.astype(jnp.float32)).astype(jnp.bfloat16)
        turned = jnp.dot(high, flips, preferred_element_type=jnp.float32)
        turned = (turned + jnp.dot(low, flips, preferred_element_type=jnp.float32)) * scale
        for b in range(width // BLOCK):
            first = c * width + b * BLOCK
            out_ref[:, first : first + BLOCK] = turned[b * rows : (b + 1) * rows].astype(jnp.bfloat16)


def rotate(sums, arrived, signs):
    rows, width = sums[0].shape
    features = signs.shape[0]
    return pl.pallas_call(
        functools.partial(rotate_kernel, len(sums)),
        out_shape=jax.ShapeDtypeStruct((rows, features), jnp.bfloat16),
        in_specs=[vmem()] * (2 * len(sums) + 1),
        out_specs=vmem(),
        compiler_params=pltpu.CompilerParams(vmem_limit_bytes=16 << 20),
    )(*sums, *arrived, signs.reshape(1, features))


def solution(mesh):
    members = mesh.shape["gx"]
    assert members & (members - 1) == 0 and members >= 8

    far = []
    mask = members // 2
    while mask > 4:
        far.append((mask, mask))
        mask //= 2
    near = [(4, 2), (2, 4)]
    core = (1, 1)

    def swap(value, masks):
        return lax.ppermute(value, "gx", [(i, i ^ masks[i % 2]) for i in range(members)])

    def halve(total, arrived):
        total = total + arrived.astype(jnp.float32)
        half = total.shape[0] // 2
        return total[:half], total[half:].astype(jnp.bfloat16)

    def on_device(tokens, gate_weight, up_weight, down_weight, sign_pattern):
        features = tokens.shape[1]
        width = features // CHUNKS
        gate_w, up_w = gate_weight.T, up_weight.T

        wide = tokens
        for masks in far:
            wide = jnp.concatenate([wide, swap(wide, masks)])
        sums = ()
        for c in range(CHUNKS):
            part = wide[:, c * width : (c + 1) * width]
            part = jnp.concatenate([part, swap(part, near[0])])
            there = swap(part, near[1])
            pieces = (part, there, swap(part, core), swap(there, core))
            sums = gate_up(gate_w, up_w, pieces, sums, c * width, c == CHUNKS - 1)
        hidden = sums

        totals, arrived = [], []
        for c in range(CHUNKS):
            total, send = down(hidden, down_weight, c * width, width)
            for masks in [core] + near[::-1] + far[::-1]:
                total, send = halve(total, swap(send, masks)) if masks != far[0] else (total, swap(send, masks))
            totals.append(total)
            arrived.append(send)
        return rotate(totals, arrived, sign_pattern)

    placed = (P(("groups", "gx"), None), P(None, "gx"), P(None, "gx"), P("gx", None), P())
    return jax.shard_map(
        on_device, mesh=mesh, in_specs=placed, out_specs=P(("groups", "gx"), None), check_vma=False
    )
```

```python
import functools
import math

import jax
import jax.numpy as jnp
from jax import lax
from jax.experimental import pallas as pl
from jax.experimental.pallas import tpu as pltpu
from jax.sharding import PartitionSpec as P

BLOCK = 128
NT = (((1,), (1,)), ((), ()))


def vmem():
    return pl.BlockSpec(memory_space=pltpu.VMEM)


def fetch_kernel(gate_hbm, up_hbm, down_hbm, gate_up_ref, down_ref, sems):
    units = gate_hbm.shape[0]
    copies = [
        pltpu.make_async_copy(gate_hbm, gate_up_ref.at[:units], sems.at[0]),
        pltpu.make_async_copy(up_hbm, gate_up_ref.at[units:], sems.at[1]),
        pltpu.make_async_copy(down_hbm, down_ref, sems.at[2]),
    ]
    for copy in copies:
        copy.start()
    for copy in copies:
        copy.wait()


def fetch(gate_w, up_w, down_w):
    units, features = gate_w.shape
    return pl.pallas_call(
        fetch_kernel,
        out_shape=(
            jax.ShapeDtypeStruct((2 * units, features), gate_w.dtype),
            jax.ShapeDtypeStruct(down_w.shape, down_w.dtype),
        ),
        in_specs=[pl.BlockSpec(memory_space=pltpu.HBM)] * 3,
        out_specs=(vmem(), vmem()),
        scratch_shapes=[pltpu.SemaphoreType.DMA((3,))],
        cost_estimate=pl.CostEstimate(flops=0, bytes_accessed=6 * units * features, transcendentals=0),
        compiler_params=pltpu.CompilerParams(vmem_limit_bytes=24 << 20),
    )(*(pltpu.with_memory_space_constraint(w, pltpu.HBM) for w in (gate_w, up_w, down_w)))


def hidden_kernel(weights_ref, rows_ref, hidden_ref, sums):
    units, features = sums.shape[0] // 2, rows_ref.shape[1]
    tile = math.gcd(features, 1024)
    sums[...] = jnp.zeros_like(sums)

    def step(index, carry):
        here = pl.ds(pl.multiple_of(index * tile, tile), tile)
        sums[...] += lax.dot_general(
            weights_ref[:, here], rows_ref[:, here], NT, preferred_element_type=jnp.float32
        )
        return carry

    lax.fori_loop(0, features // tile, step, 0)
    gate = sums[:units]
    hidden = gate / (1.0 + jnp.exp(-gate)) * sums[units:]
    hidden_ref[...] = hidden.T.astype(jnp.bfloat16)


def hidden_units(weights, rows):
    units, count = weights.shape[0] // 2, rows.shape[0]
    return pl.pallas_call(
        hidden_kernel,
        out_shape=jax.ShapeDtypeStruct((count, units), jnp.bfloat16),
        in_specs=[vmem()] * 2,
        out_specs=vmem(),
        scratch_shapes=[pltpu.VMEM((2 * units, count), jnp.float32)],
        cost_estimate=pl.CostEstimate(
            flops=4 * units * rows.size, bytes_accessed=2 * weights.size, transcendentals=0
        ),
        compiler_params=pltpu.CompilerParams(vmem_limit_bytes=24 << 20),
    )(weights, rows)


def down_kernel(own, other, hidden_ref, down_ref, keep_ref, send_ref):
    count, features = keep_ref.shape
    tile = math.gcd(features, 512)
    hidden = jnp.concatenate([hidden_ref[own : own + count], hidden_ref[other : other + count]])

    def step(index, carry):
        here = pl.ds(pl.multiple_of(index * tile, tile), tile)
        part = jnp.dot(hidden, down_ref[:, here], preferred_element_type=jnp.float32)
        keep_ref[:, here] = part[:count]
        send_ref[:, here] = part[count:].astype(jnp.bfloat16)
        return carry

    lax.fori_loop(0, features // tile, step, 0)


def down(hidden, down_w, own, other, count):
    units, features = down_w.shape
    return pl.pallas_call(
        functools.partial(down_kernel, own, other),
        out_shape=(
            jax.ShapeDtypeStruct((count, features), jnp.float32),
            jax.ShapeDtypeStruct((count, features), jnp.bfloat16),
        ),
        in_specs=[vmem()] * 2,
        out_specs=(vmem(), vmem()),
        cost_estimate=pl.CostEstimate(
            flops=4 * count * down_w.size, bytes_accessed=2 * down_w.size, transcendentals=0
        ),
        compiler_params=pltpu.CompilerParams(vmem_limit_bytes=24 << 20),
    )(hidden, down_w)


def rotate_kernel(count, *refs):
    total_ref, *arrived = refs[: count + 1]
    sign_ref, out_ref = refs[count + 1 :]
    rows, features = total_ref.shape
    common = lax.broadcasted_iota(jnp.int32, (BLOCK, BLOCK), 0) & lax.broadcasted_iota(
        jnp.int32, (BLOCK, BLOCK), 1
    )
    for shift in (4, 2, 1):
        common = common ^ (common >> shift)
    flips = (1 - 2 * (common & 1)).astype(jnp.float32).astype(jnp.bfloat16)
    scale = 1.0 / math.sqrt(BLOCK)
    value = total_ref[...]
    for piece in arrived:
        value = value + piece[...].astype(jnp.float32)
    value = value * sign_ref[...].astype(jnp.float32)
    value = jnp.concatenate([value[:, b : b + BLOCK] for b in range(0, features, BLOCK)])
    high = value.astype(jnp.bfloat16)
    low = (value - high.astype(jnp.float32)).astype(jnp.bfloat16)
    turned = jnp.dot(high, flips, preferred_element_type=jnp.float32)
    turned = (turned + jnp.dot(low, flips, preferred_element_type=jnp.float32)) * scale
    for b in range(features // BLOCK):
        out_ref[:, b * BLOCK : (b + 1) * BLOCK] = turned[b * rows : (b + 1) * rows].astype(jnp.bfloat16)


def rotate(total, arrived, signs):
    features = signs.shape[0]
    return pl.pallas_call(
        functools.partial(rotate_kernel, len(arrived)),
        out_shape=jax.ShapeDtypeStruct(total.shape, jnp.bfloat16),
        in_specs=[vmem()] * (len(arrived) + 2),
        out_specs=vmem(),
        compiler_params=pltpu.CompilerParams(vmem_limit_bytes=16 << 20),
    )(total, *arrived, signs.reshape(1, features))


def solution(mesh):
    members = mesh.shape["gx"]
    assert members & (members - 1) == 0 and members >= 16

    square = (4, 2, 6)
    far = []
    mask = members // 2
    while mask > 4:
        far.append(mask)
        mask //= 2
    others = members // 8 - 1

    def swap(value, mask):
        return lax.ppermute(value, "gx", [(i, i ^ mask) for i in range(members)])

    def on_device(tokens, gate_weight, up_weight, down_weight, sign_pattern):
        rows = tokens.shape[0]
        gate_up_w, down_w = fetch(gate_weight.T, up_weight.T, down_weight)

        away = []
        for mask in far:
            away.append(swap(jnp.concatenate([tokens] + away), mask))
        away = jnp.concatenate(away)
        own_there = jnp.concatenate([swap(tokens, m) for m in square])
        away_there = jnp.concatenate([swap(away, m) for m in square])
        pieces = [tokens, own_there, away, away_there]
        gathered = jnp.concatenate(pieces + [swap(piece, 1) for piece in pieces])
        hidden = hidden_units(gate_up_w, gathered)

        near, half = 4 * rows, members // 2 * rows
        away_keep, away_send = down(hidden, down_w, near, half + near, 4 * others * rows)
        own_keep, own_send = down(hidden, down_w, 0, half, near)

        def scatter(keep, send, count):
            total = keep + swap(send, 1).astype(jnp.float32)
            leave = total[count:].astype(jnp.bfloat16)
            arrived = [swap(leave[k * count : (k + 1) * count], m) for k, m in enumerate(square)]
            return total[:count], arrived

        total, arrived = scatter(away_keep, away_send, others * rows)
        for piece in arrived:
            total = total + piece.astype(jnp.float32)
        own, arrived = scatter(own_keep, own_send, rows)
        for mask in reversed(far):
            split = total.shape[0] // 2 // rows * rows
            piece = swap(total[split:].astype(jnp.bfloat16), mask)
            arrived.append(piece[:rows])
            total = total[:split] + piece[rows:].astype(jnp.float32)
        return rotate(own, arrived, sign_pattern)

    placed = (P(("groups", "gx"), None), P(None, "gx"), P(None, "gx"), P("gx", None), P())
    return jax.shard_map(
        on_device, mesh=mesh, in_specs=placed, out_specs=P(("groups", "gx"), None), check_vma=False
    )
```

```python
import functools
import math

import jax
import jax.numpy as jnp
from jax import lax
from jax.experimental import pallas as pl
from jax.experimental.pallas import tpu as pltpu
from jax.sharding import PartitionSpec as P

BLOCK = 128
NT = (((1,), (1,)), ((), ()))


def vmem():
    return pl.BlockSpec(memory_space=pltpu.VMEM)


def fetch_kernel(gate_hbm, up_hbm, down_hbm, _, gate_up_ref, down_ref, sems):
    units = gate_hbm.shape[0]
    copies = [
        pltpu.make_async_copy(gate_hbm, gate_up_ref.at[:units], sems.at[0]),
        pltpu.make_async_copy(up_hbm, gate_up_ref.at[units:], sems.at[1]),
        pltpu.make_async_copy(down_hbm, down_ref, sems.at[2]),
    ]
    for copy in copies:
        copy.start()
    for copy in copies:
        copy.wait()


def fetch(gate_w, up_w, down_w, after):
    units, features = gate_w.shape
    return pl.pallas_call(
        fetch_kernel,
        out_shape=(
            jax.ShapeDtypeStruct((2 * units, features), gate_w.dtype),
            jax.ShapeDtypeStruct(down_w.shape, down_w.dtype),
        ),
        in_specs=[pl.BlockSpec(memory_space=pltpu.HBM)] * 3 + [pl.BlockSpec(memory_space=pl.ANY)],
        out_specs=(vmem(),) * 2,
        scratch_shapes=[pltpu.SemaphoreType.DMA((3,))],
        cost_estimate=pl.CostEstimate(flops=0, bytes_accessed=6 * units * features, transcendentals=0),
        compiler_params=pltpu.CompilerParams(vmem_limit_bytes=24 << 20),
    )(*(pltpu.with_memory_space_constraint(w, pltpu.HBM) for w in (gate_w, up_w, down_w)), after)


def product(weights_ref, start, here_ref, there_ref):
    width = here_ref.shape[1]
    tile = math.gcd(width, 1024)
    total = None
    for first in range(0, width, tile):
        rows = jnp.concatenate([here_ref[:, first : first + tile], there_ref[:, first : first + tile]])
        span = weights_ref[:, start + first : start + first + tile]
        part = lax.dot_general(rows, span, NT, preferred_element_type=jnp.float32)
        total = part if total is None else total + part
    return total


def sums_kernel(weights_ref, here_ref, there_ref, sums_ref):
    sums_ref[...] = product(weights_ref, 0, here_ref, there_ref)


def hidden_kernel(weights_ref, here_ref, there_ref, sums_ref, hidden_ref):
    total = sums_ref[...] + product(weights_ref, here_ref.shape[1], here_ref, there_ref)
    units = total.shape[1] // 2
    gate = total[:, :units]
    hidden_ref[...] = (gate / (1.0 + jnp.exp(-gate)) * total[:, units:]).astype(jnp.bfloat16)


def hidden_units(weights, halves):
    units, width = weights.shape[0] // 2, halves[0][0].shape[1]
    count = 2 * halves[0][0].shape[0]
    cost = pl.CostEstimate(
        flops=4 * units * count * width, bytes_accessed=4 * units * width, transcendentals=0
    )
    params = pltpu.CompilerParams(vmem_limit_bytes=24 << 20)
    sums = pl.pallas_call(
        sums_kernel,
        out_shape=jax.ShapeDtypeStruct((count, 2 * units), jnp.float32),
        in_specs=[vmem()] * 3,
        out_specs=vmem(),
        cost_estimate=cost,
        compiler_params=params,
    )(weights, *halves[0])
    return pl.pallas_call(
        hidden_kernel,
        out_shape=jax.ShapeDtypeStruct((count, units), jnp.bfloat16),
        in_specs=[vmem()] * 4,
        out_specs=vmem(),
        cost_estimate=cost,
        compiler_params=params,
    )(weights, *halves[1], sums)


def down_kernel(hidden_ref, down_ref, keep_ref, near_ref, far_ref):
    half, features = keep_ref.shape
    near = near_ref.shape[0]
    tile = math.gcd(features, 512)
    for first in range(0, features, tile):
        here = slice(first, first + tile)
        part = jnp.dot(hidden_ref[...], down_ref[:, here], preferred_element_type=jnp.float32)
        keep_ref[:, here] = part[:half]
        near_ref[:, here] = part[half : half + near].astype(jnp.bfloat16)
        far_ref[:, here] = part[half + near :].astype(jnp.bfloat16)


def down(hidden, down_w, near):
    units, features = down_w.shape
    count = hidden.shape[0]
    half = count // 2
    return pl.pallas_call(
        down_kernel,
        out_shape=(
            jax.ShapeDtypeStruct((half, features), jnp.float32),
            jax.ShapeDtypeStruct((near, features), jnp.bfloat16),
            jax.ShapeDtypeStruct((half - near, features), jnp.bfloat16),
        ),
        in_specs=[vmem()] * 2,
        out_specs=(vmem(),) * 3,
        cost_estimate=pl.CostEstimate(
            flops=2 * count * units * features, bytes_accessed=2 * units * features, transcendentals=0
        ),
        compiler_params=pltpu.CompilerParams(vmem_limit_bytes=24 << 20),
    )(hidden, down_w)


def rotate_kernel(count, *refs):
    total_ref, *arrived = refs[: count + 1]
    sign_ref, out_ref = refs[count + 1 :]
    rows, features = total_ref.shape
    common = lax.broadcasted_iota(jnp.int32, (BLOCK, BLOCK), 0) & lax.broadcasted_iota(
        jnp.int32, (BLOCK, BLOCK), 1
    )
    for shift in (4, 2, 1):
        common = common ^ (common >> shift)
    flips = (1 - 2 * (common & 1)).astype(jnp.float32).astype(jnp.bfloat16)
    scale = 1.0 / math.sqrt(BLOCK)
    value = total_ref[...]
    for piece in arrived:
        value = value + piece[...].astype(jnp.float32)
    value = value * sign_ref[...].astype(jnp.float32)
    value = jnp.concatenate([value[:, b : b + BLOCK] for b in range(0, features, BLOCK)])
    high = value.astype(jnp.bfloat16)
    low = (value - high.astype(jnp.float32)).astype(jnp.bfloat16)
    turned = jnp.dot(high, flips, preferred_element_type=jnp.float32)
    turned = (turned + jnp.dot(low, flips, preferred_element_type=jnp.float32)) * scale
    for b in range(features // BLOCK):
        out_ref[:, b * BLOCK : (b + 1) * BLOCK] = turned[b * rows : (b + 1) * rows].astype(jnp.bfloat16)


def rotate(total, arrived, signs):
    features = signs.shape[0]
    return pl.pallas_call(
        functools.partial(rotate_kernel, len(arrived)),
        out_shape=jax.ShapeDtypeStruct(total.shape, jnp.bfloat16),
        in_specs=[vmem()] * (len(arrived) + 2),
        out_specs=vmem(),
        compiler_params=pltpu.CompilerParams(vmem_limit_bytes=16 << 20),
    )(total, *arrived, signs.reshape(1, features))


def solution(mesh):
    members = mesh.shape["gx"]
    assert members & (members - 1) == 0 and members >= 16

    square = ((4, 2), (2, 4), (6, 6))
    far = []
    mask = members // 2
    while mask > 4:
        far.append((mask, mask))
        mask //= 2
    others = members // 8 - 1

    def swap(value, masks):
        return lax.ppermute(value, "gx", [(i, i ^ masks[i % 2]) for i in range(members)])

    def on_device(tokens, gate_weight, up_weight, down_weight, sign_pattern):
        rows, features = tokens.shape

        away = []
        for masks in far:
            away.append(swap(jnp.concatenate([tokens] + away), masks))
        away = jnp.concatenate(away)
        first = [swap(tokens, m) for m in square] + [away]
        second = [swap(away, m) for m in square[::-1]]
        gate_up_w, down_w = fetch(gate_weight.T, up_weight.T, down_weight, away)
        gate_up_w, *gathered = lax.optimization_barrier((gate_up_w, *first, *second))
        gathered = [tokens, *gathered]
        halves = []
        for part in (slice(None, features // 2), slice(features // 2, None)):
            half = jnp.concatenate([piece[:, part] for piece in gathered])
            halves.append((half, swap(half, (1, 1))))
        hidden = hidden_units(gate_up_w, halves)

        near = 4 * rows
        keep, near_send, far_send = down(hidden, down_w, near)

        far_there, near_send = lax.optimization_barrier((swap(far_send, (1, 1)), near_send))
        near_there = swap(near_send, (1, 1))
        total = keep[near:] + far_there.astype(jnp.float32)
        count = others * rows
        leave = total[count:].astype(jnp.bfloat16)
        arrived = [swap(leave[k * count : (k + 1) * count], m) for k, m in enumerate(square[::-1])]
        near_there, arrived[0] = lax.optimization_barrier((near_there, arrived[0]))
        total = total[:count]
        for piece in arrived:
            total = total + piece.astype(jnp.float32)
        arrived = []
        for masks in reversed(far):
            split = total.shape[0] // 2 // rows * rows
            piece = swap(total[split:].astype(jnp.bfloat16), masks)
            arrived.append(piece[:rows])
            total = total[:split] + piece[rows:].astype(jnp.float32)

        total = keep[:near] + near_there.astype(jnp.float32)
        total = total[: 2 * rows] + swap(total[2 * rows :].astype(jnp.bfloat16), square[1]).astype(jnp.float32)
        arrived.append(swap(total[rows:].astype(jnp.bfloat16), square[0]))
        return rotate(total[:rows], arrived, sign_pattern)

    placed = (P(("groups", "gx"), None), P(None, "gx"), P(None, "gx"), P("gx", None), P())
    return jax.shard_map(
        on_device, mesh=mesh, in_specs=placed, out_specs=P(("groups", "gx"), None), check_vma=False
    )
```

```python
import functools
import math

import jax
import jax.numpy as jnp
from jax import lax
from jax.experimental import pallas as pl
from jax.experimental.pallas import tpu as pltpu
from jax.sharding import PartitionSpec as P

BLOCK = 128
PIECES = 4
SPANS = 4
NT = (((1,), (1,)), ((), ()))


def vmem():
    return pl.BlockSpec(memory_space=pltpu.VMEM)


def fetch_kernel(gate_hbm, up_hbm, down_hbm, _, gate_up_ref, down_ref, sems):
    units = gate_hbm.shape[0]
    copies = [
        pltpu.make_async_copy(gate_hbm, gate_up_ref.at[:units], sems.at[0]),
        pltpu.make_async_copy(up_hbm, gate_up_ref.at[units:], sems.at[1]),
        pltpu.make_async_copy(down_hbm, down_ref, sems.at[2]),
    ]
    for copy in copies:
        copy.start()
    for copy in copies:
        copy.wait()


def fetch(gate_w, up_w, down_w, after):
    units, features = gate_w.shape
    return pl.pallas_call(
        fetch_kernel,
        out_shape=(
            jax.ShapeDtypeStruct((2 * units, features), gate_w.dtype),
            jax.ShapeDtypeStruct(down_w.shape, down_w.dtype),
        ),
        in_specs=[pl.BlockSpec(memory_space=pltpu.HBM)] * 3 + [pl.BlockSpec(memory_space=pl.ANY)],
        out_specs=(vmem(),) * 2,
        scratch_shapes=[pltpu.SemaphoreType.DMA((3,))],
        cost_estimate=pl.CostEstimate(flops=0, bytes_accessed=6 * units * features, transcendentals=0),
        compiler_params=pltpu.CompilerParams(vmem_limit_bytes=24 << 20),
    )(*(pltpu.with_memory_space_constraint(w, pltpu.HBM) for w in (gate_w, up_w, down_w)), after)


def hidden_kernel(start, last, weights_ref, here_ref, there_ref, *refs):
    *sums, out_ref = refs
    width = here_ref.shape[1]
    tile = math.gcd(width, 1024)
    total = sums[0][...] if sums else None
    for first in range(0, width, tile):
        rows = jnp.concatenate([here_ref[:, first : first + tile], there_ref[:, first : first + tile]])
        span = weights_ref[:, start + first : start + first + tile]
        part = lax.dot_general(rows, span, NT, preferred_element_type=jnp.float32)
        total = part if total is None else total + part
    if last:
        units = total.shape[1] // 2
        gate = total[:, :units]
        total = gate / (1.0 + jnp.exp(-gate)) * total[:, units:]
    out_ref[...] = total.astype(out_ref.dtype)


def hidden_units(weights, spans):
    units, width = weights.shape[0] // 2, spans[0][0].shape[1]
    count = 2 * spans[0][0].shape[0]
    sums = ()
    for k, span in enumerate(spans):
        last = k == len(spans) - 1
        shape = ((count, units), jnp.bfloat16) if last else ((count, 2 * units), jnp.float32)
        sums = (
            pl.pallas_call(
                functools.partial(hidden_kernel, k * width, last),
                out_shape=jax.ShapeDtypeStruct(*shape),
                in_specs=[vmem()] * (3 + len(sums)),
                out_specs=vmem(),
                cost_estimate=pl.CostEstimate(
                    flops=4 * units * count * width, bytes_accessed=4 * units * width, transcendentals=0
                ),
                compiler_params=pltpu.CompilerParams(vmem_limit_bytes=24 << 20),
            )(weights, *span, *sums),
        )
    return sums[0]


def down_kernel(hidden_ref, down_ref, *outs):
    features = down_ref.shape[1]
    tile = math.gcd(features, 512)
    for first in range(0, features, tile):
        here = slice(first, first + tile)
        part = jnp.dot(hidden_ref[...], down_ref[:, here], preferred_element_type=jnp.float32)
        row = 0
        for out in outs:
            out[:, here] = part[row : row + out.shape[0]].astype(out.dtype)
            row += out.shape[0]


def down(hidden, down_w, counts):
    units, features = down_w.shape
    return pl.pallas_call(
        down_kernel,
        out_shape=[jax.ShapeDtypeStruct((count, features), jnp.float32) for count in counts]
        + [jax.ShapeDtypeStruct((count, features), jnp.bfloat16) for count in counts],
        in_specs=[vmem()] * 2,
        out_specs=[vmem()] * (2 * len(counts)),
        cost_estimate=pl.CostEstimate(
            flops=2 * hidden.size * features, bytes_accessed=2 * units * features, transcendentals=0
        ),
        compiler_params=pltpu.CompilerParams(vmem_limit_bytes=24 << 20),
    )(hidden, down_w)


def rotate_kernel(count, *refs):
    total_ref, *arrived = refs[: count + 1]
    sign_ref, out_ref, turned_ref, sems = refs[count + 1 :]
    rows, features = total_ref.shape
    common = lax.broadcasted_iota(jnp.int32, (BLOCK, BLOCK), 0) & lax.broadcasted_iota(
        jnp.int32, (BLOCK, BLOCK), 1
    )
    for shift in (4, 2, 1):
        common = common ^ (common >> shift)
    flips = (1 - 2 * (common & 1)).astype(jnp.float32).astype(jnp.bfloat16)
    scale = 1.0 / math.sqrt(BLOCK)
    width = features // PIECES
    copies = []
    for k in range(PIECES):
        here = slice(k * width, (k + 1) * width)
        value = total_ref[:, here]
        for piece in arrived:
            value = value + piece[:, here].astype(jnp.float32)
        value = value * sign_ref[:, here].astype(jnp.float32)
        value = jnp.concatenate([value[:, b : b + BLOCK] for b in range(0, width, BLOCK)])
        high = value.astype(jnp.bfloat16)
        low = (value - high.astype(jnp.float32)).astype(jnp.bfloat16)
        turned = jnp.dot(high, flips, preferred_element_type=jnp.float32)
        turned = (turned + jnp.dot(low, flips, preferred_element_type=jnp.float32)) * scale
        for b in range(width // BLOCK):
            first = k * width + b * BLOCK
            turned_ref[:, first : first + BLOCK] = turned[b * rows : (b + 1) * rows].astype(jnp.bfloat16)
        copies.append(pltpu.make_async_copy(turned_ref.at[:, here], out_ref.at[:, here], sems.at[k]))
        copies[-1].start()
    for copy in copies:
        copy.wait()


def rotate(total, arrived, signs):
    features = signs.shape[0]
    return pl.pallas_call(
        functools.partial(rotate_kernel, len(arrived)),
        out_shape=jax.ShapeDtypeStruct(total.shape, jnp.bfloat16),
        in_specs=[vmem()] * (len(arrived) + 2),
        out_specs=pl.BlockSpec(memory_space=pl.ANY),
        scratch_shapes=[pltpu.VMEM(total.shape, jnp.bfloat16), pltpu.SemaphoreType.DMA((PIECES,))],
        compiler_params=pltpu.CompilerParams(vmem_limit_bytes=16 << 20),
    )(total, *arrived, signs.reshape(1, features))


def solution(mesh):
    members = mesh.shape["gx"]
    assert members & (members - 1) == 0 and members >= 16

    square = ((4, 2), (2, 4), (6, 6))
    far = []
    mask = members // 2
    while mask > 4:
        far.append((mask, mask))
        mask //= 2
    others = members // 8 - 1

    def swap(value, masks):
        return lax.ppermute(value, "gx", [(i, i ^ masks[i % 2]) for i in range(members)])

    def on_device(tokens, gate_weight, up_weight, down_weight, sign_pattern):
        rows, features = tokens.shape

        away = []
        for masks in far:
            away.append(swap(jnp.concatenate([tokens] + away), masks))
        away = jnp.concatenate(away)
        near = [swap(tokens, m) for m in square]
        there = [swap(away, m) for m in square]
        gate_up_w, down_w = fetch(gate_weight.T, up_weight.T, down_weight, away)
        gate_up_w, *near, there[0], there[1], there[2] = lax.optimization_barrier((gate_up_w, *near, *there))
        gathered = [tokens, *near, there[2], away, *there[:2]]
        spans = []
        width = features // SPANS
        for k in range(SPANS):
            span = jnp.concatenate([piece[:, k * width : (k + 1) * width] for piece in gathered])
            spans.append((span, swap(span, (1, 1))))
        hidden = hidden_units(gate_up_w, spans)

        count = others * rows
        own, diagonal, rest, *sends = down(hidden, down_w, (4 * rows, count, 3 * count))
        diagonal = diagonal + swap(sends[1], (1, 1)).astype(jnp.float32)
        diagonal = swap(diagonal.astype(jnp.bfloat16), square[2])
        rest_there, sends[0] = lax.optimization_barrier((swap(sends[2], (1, 1)), sends[0]))
        rest = rest + rest_there.astype(jnp.float32)
        leave = rest[count:].astype(jnp.bfloat16)
        total = rest[:count]
        for piece in (diagonal, swap(leave[:count], square[0]), swap(leave[count:], square[1])):
            total = total + piece.astype(jnp.float32)
        arrived = []
        for masks in reversed(far):
            split = total.shape[0] // 2 // rows * rows
            piece = swap(total[split:].astype(jnp.bfloat16), masks)
            arrived.append(piece[:rows])
            total = total[:split] + piece[rows:].astype(jnp.float32)

        own = own + swap(sends[0], (1, 1)).astype(jnp.float32)
        own = own[: 2 * rows] + swap(own[2 * rows :].astype(jnp.bfloat16), square[1]).astype(jnp.float32)
        arrived.append(swap(own[rows:].astype(jnp.bfloat16), square[0]))
        return rotate(own[:rows], arrived, sign_pattern)

    placed = (P(("groups", "gx"), None), P(None, "gx"), P(None, "gx"), P("gx", None), P())
    return jax.shard_map(
        on_device, mesh=mesh, in_specs=placed, out_specs=P(("groups", "gx"), None), check_vma=False
    )
```

```python
import functools
import math

import jax
import jax.numpy as jnp
from jax import lax
from jax.experimental import pallas as pl
from jax.experimental.pallas import tpu as pltpu
from jax.sharding import PartitionSpec as P

BLOCK = 128
PIECES = 2
SPANS = (6, 5, 5)
NT = (((1,), (1,)), ((), ()))


def vmem():
    return pl.BlockSpec(memory_space=pltpu.VMEM)


def fetch_kernel(gate_hbm, up_hbm, down_hbm, _, gate_up_ref, down_ref, sems):
    units = gate_hbm.shape[0]
    copies = [
        pltpu.make_async_copy(gate_hbm, gate_up_ref.at[:units], sems.at[0]),
        pltpu.make_async_copy(up_hbm, gate_up_ref.at[units:], sems.at[1]),
        pltpu.make_async_copy(down_hbm, down_ref, sems.at[2]),
    ]
    for copy in copies:
        copy.start()
    for copy in copies:
        copy.wait()


def fetch(gate_w, up_w, down_w, after):
    units, features = gate_w.shape
    return pl.pallas_call(
        fetch_kernel,
        out_shape=(
            jax.ShapeDtypeStruct((2 * units, features), gate_w.dtype),
            jax.ShapeDtypeStruct(down_w.shape, down_w.dtype),
        ),
        in_specs=[pl.BlockSpec(memory_space=pltpu.HBM)] * 3 + [pl.BlockSpec(memory_space=pl.ANY)],
        out_specs=(vmem(),) * 2,
        scratch_shapes=[pltpu.SemaphoreType.DMA((3,))],
        cost_estimate=pl.CostEstimate(flops=0, bytes_accessed=6 * units * features, transcendentals=0),
        compiler_params=pltpu.CompilerParams(vmem_limit_bytes=24 << 20),
    )(*(pltpu.with_memory_space_constraint(w, pltpu.HBM) for w in (gate_w, up_w, down_w)), after)


def hidden_kernel(start, last, weights_ref, here_ref, there_ref, *refs):
    *sums, out_ref = refs
    width = here_ref.shape[1]
    tile = math.gcd(width, 512)
    total = sums[0][...] if sums else None
    for first in range(0, width, tile):
        rows = jnp.concatenate([here_ref[:, first : first + tile], there_ref[:, first : first + tile]])
        span = weights_ref[:, start + first : start + first + tile]
        part = lax.dot_general(rows, span, NT, preferred_element_type=jnp.float32)
        total = part if total is None else total + part
    if last:
        units = total.shape[1] // 2
        gate = total[:, :units]
        total = gate / (1.0 + jnp.exp(-gate)) * total[:, units:]
    out_ref[...] = total.astype(out_ref.dtype)


def hidden_units(weights, spans):
    units, features = weights.shape[0] // 2, weights.shape[1]
    count = 2 * spans[0][0].shape[0]
    sums, start = (), 0
    for span in spans:
        width = span[0].shape[1]
        last = start + width == features
        shape = ((count, units), jnp.bfloat16) if last else ((count, 2 * units), jnp.float32)
        sums = (
            pl.pallas_call(
                functools.partial(hidden_kernel, start, last),
                out_shape=jax.ShapeDtypeStruct(*shape),
                in_specs=[vmem()] * (3 + len(sums)),
                out_specs=vmem(),
                cost_estimate=pl.CostEstimate(
                    flops=4 * units * count * width, bytes_accessed=4 * units * width, transcendentals=0
                ),
                compiler_params=pltpu.CompilerParams(vmem_limit_bytes=24 << 20),
            )(weights, *span, *sums),
        )
        start += width
    return sums[0]


def down_kernel(hidden_ref, down_ref, *outs):
    features = down_ref.shape[1]
    tile = math.gcd(features, 512)
    for first in range(0, features, tile):
        here = slice(first, first + tile)
        part = jnp.dot(hidden_ref[...], down_ref[:, here], preferred_element_type=jnp.float32)
        row = 0
        for out in outs:
            out[:, here] = part[row : row + out.shape[0]].astype(out.dtype)
            row += out.shape[0]


def down(hidden, down_w, counts):
    units, features = down_w.shape
    return pl.pallas_call(
        down_kernel,
        out_shape=[jax.ShapeDtypeStruct((count, features), jnp.float32) for count in counts]
        + [jax.ShapeDtypeStruct((count, features), jnp.bfloat16) for count in counts],
        in_specs=[vmem()] * 2,
        out_specs=[vmem()] * (2 * len(counts)),
        cost_estimate=pl.CostEstimate(
            flops=2 * hidden.size * features, bytes_accessed=2 * units * features, transcendentals=0
        ),
        compiler_params=pltpu.CompilerParams(vmem_limit_bytes=24 << 20),
    )(hidden, down_w)


def signs_twice():
    index = jnp.arange(BLOCK, dtype=jnp.int32)
    common = index[:, None] & index[None, :]
    for shift in (4, 2, 1):
        common = common ^ (common >> shift)
    signs = (1 - 2 * (common & 1)).astype(jnp.bfloat16)
    return jnp.concatenate([signs, signs])


def rotate_kernel(count, *refs):
    total_ref, *arrived = refs[: count + 1]
    sign_ref, matrix_ref, out_ref, turned_ref, sems = refs[count + 1 :]
    rows, features = total_ref.shape
    scale = 1.0 / math.sqrt(BLOCK)
    width = features // PIECES
    copies = []
    for k in range(PIECES):
        here = slice(k * width, (k + 1) * width)
        value = total_ref[:, here]
        for piece in arrived:
            value = value + piece[:, here].astype(jnp.float32)
        value = value * sign_ref[:, here].astype(jnp.float32)
        value = jnp.concatenate([value[:, b : b + BLOCK] for b in range(0, width, BLOCK)])
        high = value.astype(jnp.bfloat16)
        low = (value - high.astype(jnp.float32)).astype(jnp.bfloat16)
        both = jnp.concatenate([high, low], axis=1)
        turned = jnp.dot(both, matrix_ref[...], preferred_element_type=jnp.float32) * scale
        for b in range(width // BLOCK):
            first = k * width + b * BLOCK
            turned_ref[:, first : first + BLOCK] = turned[b * rows : (b + 1) * rows].astype(jnp.bfloat16)
        copies.append(pltpu.make_async_copy(turned_ref.at[:, here], out_ref.at[:, here], sems.at[k]))
        copies[-1].start()
    for copy in copies:
        copy.wait()


def rotate(total, arrived, signs):
    return pl.pallas_call(
        functools.partial(rotate_kernel, len(arrived)),
        out_shape=jax.ShapeDtypeStruct(total.shape, jnp.bfloat16),
        in_specs=[vmem()] * (len(arrived) + 3),
        out_specs=pl.BlockSpec(memory_space=pl.ANY),
        scratch_shapes=[pltpu.VMEM(total.shape, jnp.bfloat16), pltpu.SemaphoreType.DMA((PIECES,))],
        compiler_params=pltpu.CompilerParams(vmem_limit_bytes=16 << 20),
    )(total, *arrived, signs.reshape(1, -1), signs_twice())


def solution(mesh):
    members = mesh.shape["gx"]
    assert members & (members - 1) == 0 and members >= 16

    square = ((4, 2), (2, 4), (6, 6))
    far = []
    mask = members // 2
    while mask > 4:
        far.append((mask, mask))
        mask //= 2
    others = members // 8 - 1

    def swap(value, masks):
        return lax.ppermute(value, "gx", [(i, i ^ masks[i % 2]) for i in range(members)])

    def on_device(tokens, gate_weight, up_weight, down_weight, sign_pattern):
        rows, features = tokens.shape

        away = []
        for masks in far:
            away.append(swap(jnp.concatenate([tokens] + away), masks))
        away = jnp.concatenate(away)
        near = [swap(tokens, m) for m in square]
        there = [swap(away, m) for m in square]
        gate_up_w, down_w = fetch(gate_weight.T, up_weight.T, down_weight, away)
        gate_up_w, *near, there[0], there[1], there[2] = lax.optimization_barrier((gate_up_w, *near, *there))
        gathered = [tokens, near[1], near[0], near[2], there[2], away, *there[:2]]
        spans, start = [], 0
        for share in SPANS:
            end = start + features * share // sum(SPANS)
            span = jnp.concatenate([piece[:, start:end] for piece in gathered])
            spans.append((span, swap(span, (1, 1))))
            start = end
        hidden = hidden_units(gate_up_w, spans)

        count = others * rows
        own, diagonal, rest, *sends = down(hidden, down_w, (4 * rows, count, 3 * count))
        there, sends[2] = lax.optimization_barrier((swap(sends[1], (1, 1)), sends[2]))
        diagonal = diagonal + there.astype(jnp.float32)
        diagonal = swap(diagonal.astype(jnp.bfloat16), square[2])
        rest_there, sends[0] = lax.optimization_barrier((swap(sends[2], (1, 1)), sends[0]))
        rest = rest + rest_there.astype(jnp.float32)
        leave = rest[count:].astype(jnp.bfloat16)
        total = rest[:count]
        for piece in (diagonal, swap(leave[:count], square[0]), swap(leave[count:], square[1])):
            total = total + piece.astype(jnp.float32)
        arrived = []
        for masks in reversed(far):
            split = total.shape[0] // 2 // rows * rows
            piece = swap(total[split:].astype(jnp.bfloat16), masks)
            arrived.append(piece[:rows])
            total = total[:split] + piece[rows:].astype(jnp.float32)

        own = own + swap(sends[0], (1, 1)).astype(jnp.float32)
        own = own[: 2 * rows] + swap(own[2 * rows :].astype(jnp.bfloat16), square[0]).astype(jnp.float32)
        arrived.append(swap(own[rows:].astype(jnp.bfloat16), square[1]))
        return rotate(own[:rows], arrived, sign_pattern)

    placed = (P(("groups", "gx"), None), P(None, "gx"), P(None, "gx"), P("gx", None), P())
    return jax.shard_map(
        on_device, mesh=mesh, in_specs=placed, out_specs=P(("groups", "gx"), None), check_vma=False
    )
```

```python
import functools
import math

import jax
import jax.numpy as jnp
from jax import lax
from jax.experimental import pallas as pl
from jax.experimental.pallas import tpu as pltpu
from jax.sharding import PartitionSpec as P

BLOCK = 128
PIECES = 2
SPANS = (6, 5, 5)
NT = (((1,), (1,)), ((), ()))


def vmem():
    return pl.BlockSpec(memory_space=pltpu.VMEM)


def fetch_kernel(gate_hbm, up_hbm, down_hbm, _, gate_up_ref, down_ref, sems):
    units = gate_hbm.shape[0]
    copies = [
        pltpu.make_async_copy(gate_hbm, gate_up_ref.at[:units], sems.at[0]),
        pltpu.make_async_copy(up_hbm, gate_up_ref.at[units:], sems.at[1]),
        pltpu.make_async_copy(down_hbm, down_ref, sems.at[2]),
    ]
    for copy in copies:
        copy.start()
    for copy in copies:
        copy.wait()


def fetch(gate_w, up_w, down_w, after):
    units, features = gate_w.shape
    return pl.pallas_call(
        fetch_kernel,
        out_shape=(
            jax.ShapeDtypeStruct((2 * units, features), gate_w.dtype),
            jax.ShapeDtypeStruct(down_w.shape, down_w.dtype),
        ),
        in_specs=[pl.BlockSpec(memory_space=pltpu.HBM)] * 3 + [pl.BlockSpec(memory_space=pl.ANY)],
        out_specs=(vmem(),) * 2,
        scratch_shapes=[pltpu.SemaphoreType.DMA((3,))],
        cost_estimate=pl.CostEstimate(flops=0, bytes_accessed=6 * units * features, transcendentals=0),
        compiler_params=pltpu.CompilerParams(vmem_limit_bytes=24 << 20),
    )(*(pltpu.with_memory_space_constraint(w, pltpu.HBM) for w in (gate_w, up_w, down_w)), after)


def hidden_kernel(start, last, weights_ref, rows_ref, *refs):
    *sums, out_ref = refs
    width = rows_ref.shape[1]
    tile = math.gcd(width, 512)
    total = sums[0][...] if sums else None
    for first in range(0, width, tile):
        span = weights_ref[:, start + first : start + first + tile]
        part = lax.dot_general(rows_ref[:, first : first + tile], span, NT, preferred_element_type=jnp.float32)
        total = part if total is None else total + part
    if last:
        units = total.shape[1] // 2
        gate = total[:, :units]
        total = gate / (1.0 + jnp.exp(-gate)) * total[:, units:]
    out_ref[...] = total.astype(out_ref.dtype)


def hidden_units(weights, spans):
    units, features = weights.shape[0] // 2, weights.shape[1]
    count = spans[0].shape[0]
    sums, start = (), 0
    for span in spans:
        width = span.shape[1]
        last = start + width == features
        shape = ((count, units), jnp.bfloat16) if last else ((count, 2 * units), jnp.float32)
        sums = (
            pl.pallas_call(
                functools.partial(hidden_kernel, start, last),
                out_shape=jax.ShapeDtypeStruct(*shape),
                in_specs=[vmem()] * (2 + len(sums)),
                out_specs=vmem(),
                cost_estimate=pl.CostEstimate(
                    flops=4 * units * count * width, bytes_accessed=4 * units * width, transcendentals=0
                ),
                compiler_params=pltpu.CompilerParams(vmem_limit_bytes=24 << 20),
            )(weights, span, *sums),
        )
        start += width
    return sums[0]


def down_kernel(here_ref, there_ref, down_ref, *outs):
    features = down_ref.shape[1]
    hidden = jnp.concatenate([here_ref[...], there_ref[...]])
    tile = math.gcd(features, 512)
    for first in range(0, features, tile):
        here = slice(first, first + tile)
        part = jnp.dot(hidden, down_ref[:, here], preferred_element_type=jnp.float32)
        row = 0
        for out in outs:
            out[:, here] = part[row : row + out.shape[0]].astype(out.dtype)
            row += out.shape[0]


def down(here, there, down_w, counts):
    units, features = down_w.shape
    return pl.pallas_call(
        down_kernel,
        out_shape=[jax.ShapeDtypeStruct((count, features), jnp.float32) for count in counts]
        + [jax.ShapeDtypeStruct((count, features), jnp.bfloat16) for count in counts],
        in_specs=[vmem()] * 3,
        out_specs=[vmem()] * (2 * len(counts)),
        cost_estimate=pl.CostEstimate(
            flops=4 * here.size * features, bytes_accessed=2 * units * features, transcendentals=0
        ),
        compiler_params=pltpu.CompilerParams(vmem_limit_bytes=24 << 20),
    )(here, there, down_w)


def signs_twice():
    index = jnp.arange(BLOCK, dtype=jnp.int32)
    common = index[:, None] & index[None, :]
    for shift in (4, 2, 1):
        common = common ^ (common >> shift)
    signs = (1 - 2 * (common & 1)).astype(jnp.bfloat16)
    return jnp.concatenate([signs, signs])


def rotate_kernel(count, *refs):
    total_ref, *arrived = refs[: count + 1]
    sign_ref, matrix_ref, out_ref, turned_ref, sems = refs[count + 1 :]
    rows, features = total_ref.shape
    scale = 1.0 / math.sqrt(BLOCK)
    width = features // PIECES
    copies = []
    for k in range(PIECES):
        here = slice(k * width, (k + 1) * width)
        value = total_ref[:, here]
        for piece in arrived:
            value = value + piece[:, here].astype(jnp.float32)
        value = value * sign_ref[:, here].astype(jnp.float32)
        value = jnp.concatenate([value[:, b : b + BLOCK] for b in range(0, width, BLOCK)])
        high = value.astype(jnp.bfloat16)
        low = (value - high.astype(jnp.float32)).astype(jnp.bfloat16)
        both = jnp.concatenate([high, low], axis=1)
        turned = jnp.dot(both, matrix_ref[...], preferred_element_type=jnp.float32) * scale
        for b in range(width // BLOCK):
            first = k * width + b * BLOCK
            turned_ref[:, first : first + BLOCK] = turned[b * rows : (b + 1) * rows].astype(jnp.bfloat16)
        copies.append(pltpu.make_async_copy(turned_ref.at[:, here], out_ref.at[:, here], sems.at[k]))
        copies[-1].start()
    for copy in copies:
        copy.wait()


def rotate(total, arrived, signs):
    return pl.pallas_call(
        functools.partial(rotate_kernel, len(arrived)),
        out_shape=jax.ShapeDtypeStruct(total.shape, jnp.bfloat16),
        in_specs=[vmem()] * (len(arrived) + 3),
        out_specs=pl.BlockSpec(memory_space=pl.ANY),
        scratch_shapes=[pltpu.VMEM(total.shape, jnp.bfloat16), pltpu.SemaphoreType.DMA((PIECES,))],
        compiler_params=pltpu.CompilerParams(vmem_limit_bytes=16 << 20),
    )(total, *arrived, signs.reshape(1, -1), signs_twice())


def solution(mesh):
    members = mesh.shape["gx"]
    assert members & (members - 1) == 0 and members >= 16

    square = ((4, 2), (2, 4), (6, 6))
    far = []
    mask = members // 2
    while mask > 4:
        far.append((mask, mask))
        mask //= 2
    others = members // 8 - 1

    def swap(value, masks):
        return lax.ppermute(value, "gx", [(i, i ^ masks[i % 2]) for i in range(members)])

    def on_device(tokens, gate_weight, up_weight, down_weight, sign_pattern):
        rows, features = tokens.shape

        away = []
        for masks in far:
            away.append(swap(jnp.concatenate([tokens] + away), masks))
        away = jnp.concatenate(away)
        near = [swap(tokens, m) for m in square]
        there = [swap(away, m) for m in square]
        gate_up_w, down_w = fetch(gate_weight.T, up_weight.T, down_weight, away)
        gate_up_w, *near, there[0], there[1], there[2] = lax.optimization_barrier((gate_up_w, *near, *there))
        gathered = [tokens, near[1], near[0], near[2], there[2], away, *there[:2]]
        spans, start = [], 0
        for share in SPANS:
            end = start + features * share // sum(SPANS)
            span = jnp.concatenate([piece[:, start:end] for piece in gathered])
            spans.append(span)
            start = end
        here = hidden_units(gate_up_w, spans)
        there = hidden_units(gate_up_w, [swap(span, (1, 1)) for span in spans])

        count = others * rows
        own, diagonal, rest, *sends = down(here, there, down_w, (4 * rows, count, 3 * count))
        diagonal = diagonal + swap(sends[1], (1, 1)).astype(jnp.float32)
        diagonal = swap(diagonal.astype(jnp.bfloat16), square[2])
        rest_there, sends[0] = lax.optimization_barrier((swap(sends[2], (1, 1)), sends[0]))
        rest = rest + rest_there.astype(jnp.float32)
        leave = rest[count:].astype(jnp.bfloat16)
        total = rest[:count]
        for piece in (diagonal, swap(leave[:count], square[0]), swap(leave[count:], square[1])):
            total = total + piece.astype(jnp.float32)
        arrived = []
        for masks in reversed(far):
            split = total.shape[0] // 2 // rows * rows
            piece = swap(total[split:].astype(jnp.bfloat16), masks)
            arrived.append(piece[:rows])
            total = total[:split] + piece[rows:].astype(jnp.float32)

        own = own + swap(sends[0], (1, 1)).astype(jnp.float32)
        own = own[: 2 * rows] + swap(own[2 * rows :].astype(jnp.bfloat16), square[0]).astype(jnp.float32)
        arrived.append(swap(own[rows:].astype(jnp.bfloat16), square[1]))
        return rotate(own[:rows], arrived, sign_pattern)

    placed = (P(("groups", "gx"), None), P(None, "gx"), P(None, "gx"), P("gx", None), P())
    return jax.shard_map(
        on_device, mesh=mesh, in_specs=placed, out_specs=P(("groups", "gx"), None), check_vma=False
    )
```

```python
import functools
import math

import jax
import jax.numpy as jnp
from jax import lax
from jax.experimental import pallas as pl
from jax.experimental.pallas import tpu as pltpu
from jax.sharding import PartitionSpec as P

BLOCK = 128
PIECES = 2
SPANS = 2
TURNS = 8
NT = (((1,), (1,)), ((), ()))


def vmem():
    return pl.BlockSpec(memory_space=pltpu.VMEM)


def turn_kernel(gate_hbm, up_hbm, _, gate_ref, up_ref, staged, sems):
    tile = staged.shape[2] // sems.shape[1]
    copies = []
    for k in range(sems.shape[1]):
        here = slice(k * tile, (k + 1) * tile)
        for j, source in enumerate((gate_hbm, up_hbm)):
            copies.append(
                pltpu.make_async_copy(source.at[:, here], staged.at[j, :, here], sems.at[j, k])
            )
            copies[-1].start()
    for k in range(sems.shape[1]):
        here = slice(k * tile, (k + 1) * tile)
        for j, out in enumerate((gate_ref, up_ref)):
            copies[2 * k + j].wait()
            out[here, :] = staged[j, :, here].T


def turn(gate_w, up_w, after):
    units, features = gate_w.shape
    shape = jax.ShapeDtypeStruct((features, units), gate_w.dtype)
    return pl.pallas_call(
        turn_kernel,
        out_shape=(shape, shape),
        in_specs=[pl.BlockSpec(memory_space=pltpu.HBM)] * 2 + [pl.BlockSpec(memory_space=pl.ANY)],
        out_specs=(vmem(), vmem()),
        scratch_shapes=[
            pltpu.VMEM((2, units, features), gate_w.dtype),
            pltpu.SemaphoreType.DMA((2, TURNS)),
        ],
        cost_estimate=pl.CostEstimate(flops=0, bytes_accessed=4 * units * features, transcendentals=0),
        compiler_params=pltpu.CompilerParams(vmem_limit_bytes=24 << 20),
    )(*(pltpu.with_memory_space_constraint(w, pltpu.HBM) for w in (gate_w, up_w)), after)


def fetch_kernel(down_hbm, down_ref, sem):
    copy = pltpu.make_async_copy(down_hbm, down_ref, sem)
    copy.start()
    copy.wait()


def fetch(down_w):
    return pl.pallas_call(
        fetch_kernel,
        out_shape=jax.ShapeDtypeStruct(down_w.shape, down_w.dtype),
        in_specs=[pl.BlockSpec(memory_space=pltpu.HBM)],
        out_specs=vmem(),
        scratch_shapes=[pltpu.SemaphoreType.DMA],
        cost_estimate=pl.CostEstimate(flops=0, bytes_accessed=2 * down_w.size, transcendentals=0),
        compiler_params=pltpu.CompilerParams(vmem_limit_bytes=4 << 20),
    )(pltpu.with_memory_space_constraint(down_w, pltpu.HBM))


def hidden_kernel(start, last, *refs):
    gate_ref, up_ref, near_here, near_there, far_here, far_there, *refs = refs
    sums, outs = refs[: len(refs) - (1 if last else 2)], refs[-1 if last else -2 :]
    width = far_here.shape[1]
    tile = math.gcd(width, 1024)
    gate, up = (ref[...] for ref in sums) if sums else (0.0, 0.0)
    for first in range(0, width, tile):
        here, there = slice(first, first + tile), slice(start + first, start + first + tile)
        rows = jnp.concatenate([near_here[:, there], far_here[:, here], near_there[:, there], far_there[:, here]])
        gate = gate + jnp.dot(rows, gate_ref[there, :], preferred_element_type=jnp.float32)
        up = up + jnp.dot(rows, up_ref[there, :], preferred_element_type=jnp.float32)
    if last:
        outs[0][...] = (gate / (1.0 + jnp.exp(-gate)) * up).astype(jnp.bfloat16)
    else:
        outs[0][...], outs[1][...] = gate, up


def hidden_units(gate_w, up_w, near, spans):
    features, units = gate_w.shape
    count = 2 * (near[0].shape[0] + spans[0][0].shape[0])
    sums, start = (), 0
    for span in spans:
        width = span[0].shape[1]
        last = start + width == features
        total = jax.ShapeDtypeStruct((count, units), jnp.float32)
        sums = pl.pallas_call(
            functools.partial(hidden_kernel, start, last),
            out_shape=(jax.ShapeDtypeStruct((count, units), jnp.bfloat16),) if last else (total, total),
            in_specs=[vmem()] * (6 + len(sums)),
            out_specs=(vmem(),) * (1 if last else 2),
            cost_estimate=pl.CostEstimate(
                flops=4 * units * count * width, bytes_accessed=4 * units * width, transcendentals=0
            ),
            compiler_params=pltpu.CompilerParams(vmem_limit_bytes=24 << 20),
        )(gate_w, up_w, *near, *span, *sums)
        start += width
    return sums[0]


def down_kernel(hidden_ref, down_ref, *outs):
    features = down_ref.shape[1]
    tile = math.gcd(features, 512)
    for first in range(0, features, tile):
        here = slice(first, first + tile)
        part = jnp.dot(hidden_ref[...], down_ref[:, here], preferred_element_type=jnp.float32)
        row = 0
        for out in outs:
            out[:, here] = part[row : row + out.shape[0]].astype(out.dtype)
            row += out.shape[0]


def down(hidden, down_w, counts):
    units, features = down_w.shape
    return pl.pallas_call(
        down_kernel,
        out_shape=[jax.ShapeDtypeStruct((count, features), jnp.float32) for count in counts]
        + [jax.ShapeDtypeStruct((count, features), jnp.bfloat16) for count in counts],
        in_specs=[vmem()] * 2,
        out_specs=[vmem()] * (2 * len(counts)),
        cost_estimate=pl.CostEstimate(
            flops=2 * hidden.size * features, bytes_accessed=2 * units * features, transcendentals=0
        ),
        compiler_params=pltpu.CompilerParams(vmem_limit_bytes=24 << 20),
    )(hidden, down_w)


def signs_twice():
    index = jnp.arange(BLOCK, dtype=jnp.int32)
    common = index[:, None] & index[None, :]
    for shift in (4, 2, 1):
        common = common ^ (common >> shift)
    signs = (1 - 2 * (common & 1)).astype(jnp.bfloat16)
    return jnp.concatenate([signs, signs])


def rotate_kernel(count, *refs):
    total_ref, *arrived = refs[: count + 1]
    sign_ref, matrix_ref, out_ref, turned_ref, sems = refs[count + 1 :]
    rows, features = total_ref.shape
    scale = 1.0 / math.sqrt(BLOCK)
    width = features // PIECES
    copies = []
    for k in range(PIECES):
        here = slice(k * width, (k + 1) * width)
        value = total_ref[:, here]
        for piece in arrived:
            value = value + piece[:, here].astype(jnp.float32)
        value = value * sign_ref[:, here].astype(jnp.float32)
        value = jnp.concatenate([value[:, b : b + BLOCK] for b in range(0, width, BLOCK)])
        high = value.astype(jnp.bfloat16)
        low = (value - high.astype(jnp.float32)).astype(jnp.bfloat16)
        both = jnp.concatenate([high, low], axis=1)
        turned = jnp.dot(both, matrix_ref[...], preferred_element_type=jnp.float32) * scale
        for b in range(width // BLOCK):
            first = k * width + b * BLOCK
            turned_ref[:, first : first + BLOCK] = turned[b * rows : (b + 1) * rows].astype(jnp.bfloat16)
        copies.append(pltpu.make_async_copy(turned_ref.at[:, here], out_ref.at[:, here], sems.at[k]))
        copies[-1].start()
    for copy in copies:
        copy.wait()


def rotate(total, arrived, signs):
    return pl.pallas_call(
        functools.partial(rotate_kernel, len(arrived)),
        out_shape=jax.ShapeDtypeStruct(total.shape, jnp.bfloat16),
        in_specs=[vmem()] * (len(arrived) + 3),
        out_specs=pl.BlockSpec(memory_space=pl.ANY),
        scratch_shapes=[pltpu.VMEM(total.shape, jnp.bfloat16), pltpu.SemaphoreType.DMA((PIECES,))],
        compiler_params=pltpu.CompilerParams(vmem_limit_bytes=16 << 20),
    )(total, *arrived, signs.reshape(1, -1), signs_twice())


def solution(mesh):
    members = mesh.shape["gx"]
    assert members & (members - 1) == 0 and members >= 16

    square = ((4, 2), (2, 4), (6, 6))
    far = []
    mask = members // 2
    while mask > 4:
        far.append((mask, mask))
        mask //= 2
    others = members // 8 - 1

    def swap(value, masks):
        return lax.ppermute(value, "gx", [(i, i ^ masks[i % 2]) for i in range(members)])

    def on_device(tokens, gate_weight, up_weight, down_weight, sign_pattern):
        rows, features = tokens.shape

        away = []
        for masks in far:
            away.append(swap(jnp.concatenate([tokens] + away), masks))
        away = jnp.concatenate(away)
        near = [swap(tokens, m) for m in square]
        down_w = fetch(down_weight)
        away, down_w = lax.optimization_barrier((away, down_w))
        there = [swap(away, m) for m in square[:2]]
        away, near[0] = lax.optimization_barrier((away, near[0]))
        there.append(swap(away, square[2]))
        gate_w, up_w = turn(gate_weight.T, up_weight.T, away)
        there[0], *near = lax.optimization_barrier((there[0], *near))
        near = jnp.concatenate([tokens, near[1], near[0], near[2]])
        near_there = swap(near, (1, 1))
        gate_w, up_w, near, *there[1:] = lax.optimization_barrier((gate_w, up_w, near, *there[1:]))
        far_rows = [there[2], away, *there[:2]]
        spans = []
        width = features // SPANS
        for k in range(SPANS):
            span = jnp.concatenate([piece[:, k * width : (k + 1) * width] for piece in far_rows])
            spans.append((span, swap(span, (1, 1))))
        hidden = hidden_units(gate_w, up_w, (near, near_there), spans)

        count = others * rows
        own, diagonal, rest, *sends = down(hidden, down_w, (4 * rows, count, 3 * count))
        diagonal = diagonal + swap(sends[1], (1, 1)).astype(jnp.float32)
        diagonal = swap(diagonal.astype(jnp.bfloat16), square[2])
        rest_there, sends[0] = lax.optimization_barrier((swap(sends[2], (1, 1)), sends[0]))
        rest = rest + rest_there.astype(jnp.float32)
        leave = rest[count:].astype(jnp.bfloat16)
        total = rest[:count]
        for piece in (diagonal, swap(leave[:count], square[0]), swap(leave[count:], square[1])):
            total = total + piece.astype(jnp.float32)
        arrived = []
        for masks in reversed(far):
            split = total.shape[0] // 2 // rows * rows
            piece = swap(total[split:].astype(jnp.bfloat16), masks)
            arrived.append(piece[:rows])
            total = total[:split] + piece[rows:].astype(jnp.float32)

        own = own + swap(sends[0], (1, 1)).astype(jnp.float32)
        own = own[: 2 * rows] + swap(own[2 * rows :].astype(jnp.bfloat16), square[0]).astype(jnp.float32)
        arrived.append(swap(own[rows:].astype(jnp.bfloat16), square[1]))
        return rotate(own[:rows], arrived, sign_pattern)

    placed = (P(("groups", "gx"), None), P(None, "gx"), P(None, "gx"), P("gx", None), P())
    return jax.shard_map(
        on_device, mesh=mesh, in_specs=placed, out_specs=P(("groups", "gx"), None), check_vma=False
    )
```

```python
import functools
import math

import jax
import jax.numpy as jnp
from jax import lax
from jax.experimental import pallas as pl
from jax.experimental.pallas import tpu as pltpu
from jax.sharding import PartitionSpec as P

BLOCK = 128
PIECES = 2
SPANS = 2
TURNS = 8
NT = (((1,), (1,)), ((), ()))


def vmem():
    return pl.BlockSpec(memory_space=pltpu.VMEM)


def load_kernel(gate_hbm, up_hbm, down_hbm, _, gate_ref, up_ref, down_ref, staged, sems, down_sem):
    tile = staged.shape[2] // sems.shape[1]
    copies = []
    for k in range(sems.shape[1]):
        here = slice(k * tile, (k + 1) * tile)
        for j, source in enumerate((gate_hbm, up_hbm)):
            copies.append(
                pltpu.make_async_copy(source.at[:, here], staged.at[j, :, here], sems.at[j, k])
            )
            copies[-1].start()
    down_copy = pltpu.make_async_copy(down_hbm, down_ref, down_sem)
    down_copy.start()
    for k in range(sems.shape[1]):
        here = slice(k * tile, (k + 1) * tile)
        for j, out in enumerate((gate_ref, up_ref)):
            copies[2 * k + j].wait()
            out[here, :] = staged[j, :, here].T
    down_copy.wait()


def load(gate_w, up_w, down_w, after):
    units, features = gate_w.shape
    shape = jax.ShapeDtypeStruct((features, units), gate_w.dtype)
    return pl.pallas_call(
        load_kernel,
        out_shape=(shape, shape, jax.ShapeDtypeStruct(down_w.shape, down_w.dtype)),
        in_specs=[pl.BlockSpec(memory_space=pltpu.HBM)] * 3 + [pl.BlockSpec(memory_space=pl.ANY)],
        out_specs=(vmem(),) * 3,
        scratch_shapes=[
            pltpu.VMEM((2, units, features), gate_w.dtype),
            pltpu.SemaphoreType.DMA((2, TURNS)),
            pltpu.SemaphoreType.DMA,
        ],
        cost_estimate=pl.CostEstimate(flops=0, bytes_accessed=6 * units * features, transcendentals=0),
        compiler_params=pltpu.CompilerParams(vmem_limit_bytes=24 << 20),
    )(*(pltpu.with_memory_space_constraint(w, pltpu.HBM) for w in (gate_w, up_w, down_w)), after)


def hidden_kernel(start, last, *refs):
    gate_ref, up_ref, near_here, near_there, far_here, far_there, *refs = refs
    sums, outs = refs[: len(refs) - (1 if last else 2)], refs[-1 if last else -2 :]
    width = far_here.shape[1]
    tile = math.gcd(width, 1024)
    gate, up = (ref[...] for ref in sums) if sums else (0.0, 0.0)
    for first in range(0, width, tile):
        here, there = slice(first, first + tile), slice(start + first, start + first + tile)
        rows = jnp.concatenate([near_here[:, there], far_here[:, here], near_there[:, there], far_there[:, here]])
        gate = gate + jnp.dot(rows, gate_ref[there, :], preferred_element_type=jnp.float32)
        up = up + jnp.dot(rows, up_ref[there, :], preferred_element_type=jnp.float32)
    if last:
        outs[0][...] = (gate / (1.0 + jnp.exp(-gate)) * up).astype(jnp.bfloat16)
    else:
        outs[0][...], outs[1][...] = gate, up


def hidden_units(gate_w, up_w, near, spans):
    features, units = gate_w.shape
    count = 2 * (near[0].shape[0] + spans[0][0].shape[0])
    sums, start = (), 0
    for span in spans:
        width = span[0].shape[1]
        last = start + width == features
        total = jax.ShapeDtypeStruct((count, units), jnp.float32)
        sums = pl.pallas_call(
            functools.partial(hidden_kernel, start, last),
            out_shape=(jax.ShapeDtypeStruct((count, units), jnp.bfloat16),) if last else (total, total),
            in_specs=[vmem()] * (6 + len(sums)),
            out_specs=(vmem(),) * (1 if last else 2),
            cost_estimate=pl.CostEstimate(
                flops=4 * units * count * width, bytes_accessed=4 * units * width, transcendentals=0
            ),
            compiler_params=pltpu.CompilerParams(vmem_limit_bytes=24 << 20),
        )(gate_w, up_w, *near, *span, *sums)
        start += width
    return sums[0]


def down_kernel(spans, hidden_ref, down_ref, *outs):
    half, features = hidden_ref.shape[0] // 2, down_ref.shape[1]
    tile = math.gcd(features, 512)
    for first in range(0, features, tile):
        here = slice(first, first + tile)
        part = jnp.dot(hidden_ref[...], down_ref[:, here], preferred_element_type=jnp.float32)
        for k, out in enumerate(outs):
            begin = 0 if k < len(spans) else half
            rows = [part[begin + first : begin + last] for first, last in spans[k % len(spans)]]
            out[:, here] = jnp.concatenate(rows).astype(out.dtype)


def down(hidden, down_w, spans):
    units, features = down_w.shape
    counts = [sum(last - first for first, last in span) for span in spans]
    return pl.pallas_call(
        functools.partial(down_kernel, spans),
        out_shape=[jax.ShapeDtypeStruct((count, features), jnp.float32) for count in counts]
        + [jax.ShapeDtypeStruct((count, features), jnp.bfloat16) for count in counts],
        in_specs=[vmem()] * 2,
        out_specs=[vmem()] * (2 * len(counts)),
        cost_estimate=pl.CostEstimate(
            flops=2 * hidden.size * features, bytes_accessed=2 * units * features, transcendentals=0
        ),
        compiler_params=pltpu.CompilerParams(vmem_limit_bytes=24 << 20),
    )(hidden, down_w)


def signs_twice():
    index = jnp.arange(BLOCK, dtype=jnp.int32)
    common = index[:, None] & index[None, :]
    for shift in (4, 2, 1):
        common = common ^ (common >> shift)
    signs = (1 - 2 * (common & 1)).astype(jnp.bfloat16)
    return jnp.concatenate([signs, signs])


def rotate_kernel(count, *refs):
    total_ref, *arrived = refs[: count + 1]
    sign_ref, matrix_ref, out_ref, turned_ref, sems = refs[count + 1 :]
    rows, features = total_ref.shape
    scale = 1.0 / math.sqrt(BLOCK)
    width = features // PIECES
    copies = []
    for k in range(PIECES):
        here = slice(k * width, (k + 1) * width)
        value = total_ref[:, here]
        for piece in arrived:
            value = value + piece[:, here].astype(jnp.float32)
        value = value * sign_ref[:, here].astype(jnp.float32)
        value = jnp.concatenate([value[:, b : b + BLOCK] for b in range(0, width, BLOCK)])
        high = value.astype(jnp.bfloat16)
        low = (value - high.astype(jnp.float32)).astype(jnp.bfloat16)
        both = jnp.concatenate([high, low], axis=1)
        turned = jnp.dot(both, matrix_ref[...], preferred_element_type=jnp.float32) * scale
        for b in range(width // BLOCK):
            first = k * width + b * BLOCK
            turned_ref[:, first : first + BLOCK] = turned[b * rows : (b + 1) * rows].astype(jnp.bfloat16)
        copies.append(pltpu.make_async_copy(turned_ref.at[:, here], out_ref.at[:, here], sems.at[k]))
        copies[-1].start()
    for copy in copies:
        copy.wait()


def rotate(total, arrived, signs):
    return pl.pallas_call(
        functools.partial(rotate_kernel, len(arrived)),
        out_shape=jax.ShapeDtypeStruct(total.shape, jnp.bfloat16),
        in_specs=[vmem()] * (len(arrived) + 3),
        out_specs=pl.BlockSpec(memory_space=pl.ANY),
        scratch_shapes=[pltpu.VMEM(total.shape, jnp.bfloat16), pltpu.SemaphoreType.DMA((PIECES,))],
        compiler_params=pltpu.CompilerParams(vmem_limit_bytes=16 << 20),
    )(total, *arrived, signs.reshape(1, -1), signs_twice())


def solution(mesh):
    members = mesh.shape["gx"]
    assert members & (members - 1) == 0 and members >= 16

    square = ((4, 2), (2, 4), (6, 6))
    far = []
    mask = members // 2
    while mask > 4:
        far.append((mask, mask))
        mask //= 2
    others = members // 8 - 1

    def swap(value, masks):
        return lax.ppermute(value, "gx", [(i, i ^ masks[i % 2]) for i in range(members)])

    def on_device(tokens, gate_weight, up_weight, down_weight, sign_pattern):
        rows, features = tokens.shape

        away = []
        for masks in far:
            away.append(swap(jnp.concatenate([tokens] + away), masks))
        away = jnp.concatenate(away)
        near = [swap(tokens, m) for m in square[:2]]
        gate_w, up_w, down_w = load(gate_weight.T, up_weight.T, down_weight, away)
        first = swap(away, square[0])
        both = swap(jnp.concatenate([away, near[0]]), square[1])
        diagonal = swap(away, square[2])
        first, *near = lax.optimization_barrier((first, *near))
        early = jnp.concatenate([tokens, near[1], near[0], away])
        early_there = swap(early, (1, 1))
        gate_w, up_w, early, both, diagonal = lax.optimization_barrier((gate_w, up_w, early, both, diagonal))
        count = others * rows
        late = [both[count:], diagonal, first, both[:count]]
        spans = []
        width = features // SPANS
        for k in range(SPANS):
            span = jnp.concatenate([piece[:, k * width : (k + 1) * width] for piece in late])
            spans.append((span, swap(span, (1, 1))))
        hidden = hidden_units(gate_w, up_w, (early, early_there), spans)

        a, b = 3 * rows, 3 * rows + count
        own_rows = ((0, a), (b, b + rows))
        rest_rows = ((a, b), (b + rows + count, b + rows + 3 * count))
        own, diagonal, rest, *sends = down(
            hidden, down_w, (own_rows, ((b + rows, b + rows + count),), rest_rows)
        )
        diagonal = diagonal + swap(sends[1], (1, 1)).astype(jnp.float32)
        diagonal = swap(diagonal.astype(jnp.bfloat16), square[2])
        rest_there, sends[0] = lax.optimization_barrier((swap(sends[2], (1, 1)), sends[0]))
        rest = rest + rest_there.astype(jnp.float32)
        leave = rest[count:].astype(jnp.bfloat16)
        total = rest[:count]
        for piece in (diagonal, swap(leave[:count], square[0]), swap(leave[count:], square[1])):
            total = total + piece.astype(jnp.float32)
        arrived = []
        for masks in reversed(far):
            split = total.shape[0] // 2 // rows * rows
            piece = swap(total[split:].astype(jnp.bfloat16), masks)
            arrived.append(piece[:rows])
            total = total[:split] + piece[rows:].astype(jnp.float32)

        own = own + swap(sends[0], (1, 1)).astype(jnp.float32)
        own = own[: 2 * rows] + swap(own[2 * rows :].astype(jnp.bfloat16), square[0]).astype(jnp.float32)
        arrived.append(swap(own[rows:].astype(jnp.bfloat16), square[1]))
        return rotate(own[:rows], arrived, sign_pattern)

    placed = (P(("groups", "gx"), None), P(None, "gx"), P(None, "gx"), P("gx", None), P())
    return jax.shard_map(
        on_device, mesh=mesh, in_specs=placed, out_specs=P(("groups", "gx"), None), check_vma=False
    )
```

```python
import functools
import math

import jax
import jax.numpy as jnp
from jax import lax
from jax.experimental import pallas as pl
from jax.experimental.pallas import tpu as pltpu
from jax.sharding import PartitionSpec as P

BLOCK = 128
PIECES = 2
SPANS = 2
TURNS = 8
NT = (((1,), (1,)), ((), ()))


def vmem():
    return pl.BlockSpec(memory_space=pltpu.VMEM)


def load_kernel(gate_hbm, up_hbm, down_hbm, _, gate_ref, up_ref, down_ref, staged, sems, down_sem):
    tile = staged.shape[2] // sems.shape[1]
    copies = []
    for k in range(sems.shape[1]):
        here = slice(k * tile, (k + 1) * tile)
        for j, source in enumerate((gate_hbm, up_hbm)):
            copies.append(
                pltpu.make_async_copy(source.at[:, here], staged.at[j, :, here], sems.at[j, k])
            )
            copies[-1].start()
    down_copy = pltpu.make_async_copy(down_hbm, down_ref, down_sem)
    down_copy.start()
    for k in range(sems.shape[1]):
        here = slice(k * tile, (k + 1) * tile)
        for j, out in enumerate((gate_ref, up_ref)):
            copies[2 * k + j].wait()
            out[here, :] = staged[j, :, here].T
    down_copy.wait()


def load(gate_w, up_w, down_w, after):
    units, features = gate_w.shape
    shape = jax.ShapeDtypeStruct((features, units), gate_w.dtype)
    return pl.pallas_call(
        load_kernel,
        out_shape=(shape, shape, jax.ShapeDtypeStruct(down_w.shape, down_w.dtype)),
        in_specs=[pl.BlockSpec(memory_space=pltpu.HBM)] * 3 + [pl.BlockSpec(memory_space=pl.ANY)],
        out_specs=(vmem(),) * 3,
        scratch_shapes=[
            pltpu.VMEM((2, units, features), gate_w.dtype),
            pltpu.SemaphoreType.DMA((2, TURNS)),
            pltpu.SemaphoreType.DMA,
        ],
        cost_estimate=pl.CostEstimate(flops=0, bytes_accessed=6 * units * features, transcendentals=0),
        compiler_params=pltpu.CompilerParams(vmem_limit_bytes=24 << 20),
    )(*(pltpu.with_memory_space_constraint(w, pltpu.HBM) for w in (gate_w, up_w, down_w)), after)


def hidden_kernel(start, last, *refs):
    gate_ref, up_ref, near_here, near_there, far_here, far_there, *refs = refs
    sums, outs = refs[:-2], refs[-2:]
    width = far_here.shape[1]
    tile = math.gcd(width, 1024)
    gate, up = (ref[...] for ref in sums) if sums else (0.0, 0.0)
    for first in range(0, width, tile):
        here, there = slice(first, first + tile), slice(start + first, start + first + tile)
        rows = jnp.concatenate([near_here[:, there], far_here[:, here], near_there[:, there], far_there[:, here]])
        gate = gate + jnp.dot(rows, gate_ref[there, :], preferred_element_type=jnp.float32)
        up = up + jnp.dot(rows, up_ref[there, :], preferred_element_type=jnp.float32)
    if last:
        hidden = (gate / (1.0 + jnp.exp(-gate)) * up).astype(jnp.bfloat16)
        half = outs[0].shape[0]
        outs[0][...], outs[1][...] = hidden[:half], hidden[half:]
    else:
        outs[0][...], outs[1][...] = gate, up


def hidden_units(gate_w, up_w, near, spans):
    features, units = gate_w.shape
    count = 2 * (near[0].shape[0] + spans[0][0].shape[0])
    sums, start = (), 0
    for span in spans:
        width = span[0].shape[1]
        last = start + width == features
        out = ((count // 2, units), jnp.bfloat16) if last else ((count, units), jnp.float32)
        sums = pl.pallas_call(
            functools.partial(hidden_kernel, start, last),
            out_shape=(jax.ShapeDtypeStruct(*out),) * 2,
            in_specs=[vmem()] * (6 + len(sums)),
            out_specs=(vmem(),) * 2,
            cost_estimate=pl.CostEstimate(
                flops=4 * units * count * width, bytes_accessed=4 * units * width, transcendentals=0
            ),
            compiler_params=pltpu.CompilerParams(vmem_limit_bytes=24 << 20),
        )(gate_w, up_w, *near, *span, *sums)
        start += width
    return sums


def down_kernel(count, hidden_ref, down_ref, *refs):
    before, outs = refs[:count], refs[count:]
    features = down_ref.shape[1]
    tile = math.gcd(features, 512)
    for first in range(0, features, tile):
        here = slice(first, first + tile)
        part = jnp.dot(hidden_ref[...], down_ref[:, here], preferred_element_type=jnp.float32)
        row = 0
        for k, out in enumerate(outs):
            rows = part[row : row + out.shape[0]]
            row += out.shape[0]
            out[:, here] = (before[k][:, here] + rows if before else rows).astype(out.dtype)


def down(hidden, down_w, outs, before=()):
    units, features = down_w.shape
    return pl.pallas_call(
        functools.partial(down_kernel, len(before)),
        out_shape=[jax.ShapeDtypeStruct((count, features), kind) for count, kind in outs],
        in_specs=[vmem()] * (2 + len(before)),
        out_specs=[vmem()] * len(outs),
        cost_estimate=pl.CostEstimate(
            flops=2 * hidden.size * features, bytes_accessed=2 * units * features, transcendentals=0
        ),
        compiler_params=pltpu.CompilerParams(vmem_limit_bytes=24 << 20),
    )(hidden, down_w, *before)


def signs_twice():
    index = jnp.arange(BLOCK, dtype=jnp.int32)
    common = index[:, None] & index[None, :]
    for shift in (4, 2, 1):
        common = common ^ (common >> shift)
    signs = (1 - 2 * (common & 1)).astype(jnp.bfloat16)
    return jnp.concatenate([signs, signs])


def rotate_kernel(count, *refs):
    total_ref, *arrived = refs[: count + 1]
    sign_ref, matrix_ref, out_ref, turned_ref, sems = refs[count + 1 :]
    rows, features = total_ref.shape
    scale = 1.0 / math.sqrt(BLOCK)
    width = features // PIECES
    copies = []
    for k in range(PIECES):
        here = slice(k * width, (k + 1) * width)
        value = total_ref[:, here]
        for piece in arrived:
            value = value + piece[:, here].astype(jnp.float32)
        value = value * sign_ref[:, here].astype(jnp.float32)
        value = jnp.concatenate([value[:, b : b + BLOCK] for b in range(0, width, BLOCK)])
        high = value.astype(jnp.bfloat16)
        low = (value - high.astype(jnp.float32)).astype(jnp.bfloat16)
        both = jnp.concatenate([high, low], axis=1)
        turned = jnp.dot(both, matrix_ref[...], preferred_element_type=jnp.float32) * scale
        for b in range(width // BLOCK):
            first = k * width + b * BLOCK
            turned_ref[:, first : first + BLOCK] = turned[b * rows : (b + 1) * rows].astype(jnp.bfloat16)
        copies.append(pltpu.make_async_copy(turned_ref.at[:, here], out_ref.at[:, here], sems.at[k]))
        copies[-1].start()
    for copy in copies:
        copy.wait()


def rotate(total, arrived, signs):
    return pl.pallas_call(
        functools.partial(rotate_kernel, len(arrived)),
        out_shape=jax.ShapeDtypeStruct(total.shape, jnp.bfloat16),
        in_specs=[vmem()] * (len(arrived) + 3),
        out_specs=pl.BlockSpec(memory_space=pl.ANY),
        scratch_shapes=[pltpu.VMEM(total.shape, jnp.bfloat16), pltpu.SemaphoreType.DMA((PIECES,))],
        compiler_params=pltpu.CompilerParams(vmem_limit_bytes=16 << 20),
    )(total, *arrived, signs.reshape(1, -1), signs_twice())


def solution(mesh):
    members = mesh.shape["gx"]
    assert members & (members - 1) == 0 and members >= 16

    square = ((4, 2), (2, 4), (6, 6))
    far = []
    mask = members // 2
    while mask > 4:
        far.append((mask, mask))
        mask //= 2
    others = members // 8 - 1

    def swap(value, masks):
        return lax.ppermute(value, "gx", [(i, i ^ masks[i % 2]) for i in range(members)])

    def on_device(tokens, gate_weight, up_weight, down_weight, sign_pattern):
        rows, features = tokens.shape

        away = []
        for masks in far:
            away.append(swap(jnp.concatenate([tokens] + away), masks))
        away = jnp.concatenate(away)
        near = [swap(tokens, m) for m in square]
        there = [None] * 3
        for k, arrived in ((1, None), (2, 1), (0, 0)):
            if arrived is not None:
                away, near[arrived] = lax.optimization_barrier((away, near[arrived]))
            there[k] = swap(away, square[k])
        down_there = swap(down_weight, (1, 1))
        gate_w, up_w, down_w = load(gate_weight.T, up_weight.T, down_weight, away)
        there[1], *near = lax.optimization_barrier((there[1], *near))
        near = jnp.concatenate([tokens, near[1], near[0], near[2]])
        near_there = swap(near, (1, 1))
        gate_w, up_w, near, there[0], there[2] = lax.optimization_barrier((gate_w, up_w, near, there[0], there[2]))
        far_rows = [there[2], away, *there[:2]]
        spans = []
        width = features // SPANS
        for k in range(SPANS):
            span = jnp.concatenate([piece[:, k * width : (k + 1) * width] for piece in far_rows])
            spans.append((span, swap(span, (1, 1))))
        mine, theirs = hidden_units(gate_w, up_w, (near, near_there), spans)

        count = others * rows
        wide, narrow = jnp.float32, jnp.bfloat16
        counts = (4 * rows, count, count, count, count)
        sums = down(mine, down_w, [(n, wide) for n in counts])
        kinds = (wide, narrow, wide, narrow, narrow)
        own, diagonal, total, *leave = down(swap(theirs, (1, 1)), down_there, list(zip(counts, kinds)), sums)
        for piece in (swap(diagonal, square[2]), swap(leave[0], square[0]), swap(leave[1], square[1])):
            total = total + piece.astype(jnp.float32)
        arrived = []
        for masks in reversed(far):
            split = total.shape[0] // 2 // rows * rows
            piece = swap(total[split:].astype(jnp.bfloat16), masks)
            arrived.append(piece[:rows])
            total = total[:split] + piece[rows:].astype(jnp.float32)

        own = own[: 2 * rows] + swap(own[2 * rows :].astype(jnp.bfloat16), square[0]).astype(jnp.float32)
        arrived.append(swap(own[rows:].astype(jnp.bfloat16), square[1]))
        return rotate(own[:rows], arrived, sign_pattern)

    placed = (P(("groups", "gx"), None), P(None, "gx"), P(None, "gx"), P("gx", None), P())
    return jax.shard_map(
        on_device, mesh=mesh, in_specs=placed, out_specs=P(("groups", "gx"), None), check_vma=False
    )
```

```python
import functools
import math

import jax
import jax.numpy as jnp
from jax import lax
from jax.experimental import pallas as pl
from jax.experimental.pallas import tpu as pltpu
from jax.sharding import PartitionSpec as P

BLOCK = 128
PIECES = 2
SPANS = 2
TURNS = 8
FIRST, SECOND, THIRD = (8, 4), (4, 2), (2, 8)
NT = (((1,), (1,)), ((), ()))


def vmem():
    return pl.BlockSpec(memory_space=pltpu.VMEM)


def load_kernel(turned, *refs):
    count = len(turned)
    sources, outs = refs[:count], refs[count + 1 : 2 * count + 1]
    staged, sems = refs[2 * count + 1 :]
    tile = staged.shape[1] // (sems.shape[0] - 1)
    copies = []
    for source, out, turn in zip(sources, outs, turned):
        if not turn:
            continue
        for k in range(sems.shape[0] - 1):
            here = slice(k * tile, (k + 1) * tile)
            copies.append((pltpu.make_async_copy(source.at[:, here], staged.at[:, here], sems.at[k]), out, here))
    others = [
        pltpu.make_async_copy(source, out, sems.at[sems.shape[0] - 1])
        for source, out, turn in zip(sources, outs, turned)
        if not turn
    ]
    for copy, _, _ in copies:
        copy.start()
    for copy in others:
        copy.start()
    for copy, out, here in copies:
        copy.wait()
        out[here, :] = staged[:, here].T
    for copy in others:
        copy.wait()


def load(weights, turned, after):
    shapes = [w.shape[::-1] if turn else w.shape for w, turn in zip(weights, turned)]
    size = sum(w.size for w in weights)
    return pl.pallas_call(
        functools.partial(load_kernel, turned),
        out_shape=[jax.ShapeDtypeStruct(shape, weights[0].dtype) for shape in shapes],
        in_specs=[pl.BlockSpec(memory_space=pltpu.HBM)] * len(weights) + [pl.BlockSpec(memory_space=pl.ANY)],
        out_specs=[vmem()] * len(weights),
        scratch_shapes=[
            pltpu.VMEM(weights[0].shape, weights[0].dtype),
            pltpu.SemaphoreType.DMA((TURNS + 1,)),
        ],
        cost_estimate=pl.CostEstimate(flops=0, bytes_accessed=4 * size, transcendentals=0),
        compiler_params=pltpu.CompilerParams(vmem_limit_bytes=16 << 20),
    )(*(pltpu.with_memory_space_constraint(w, pltpu.HBM) for w in weights), after)


def hidden_kernel(start, last, *refs):
    gate_ref, up_ref, near_here, near_there, far_here, far_there, *refs = refs
    sums, outs = refs[: len(refs) - (1 if last else 2)], refs[-1 if last else -2 :]
    width = far_here.shape[1]
    tile = math.gcd(width, 1024)
    gate, up = (ref[...] for ref in sums) if sums else (0.0, 0.0)
    for first in range(0, width, tile):
        here, there = slice(first, first + tile), slice(start + first, start + first + tile)
        rows = jnp.concatenate([near_here[:, there], far_here[:, here], near_there[:, there], far_there[:, here]])
        gate = gate + jnp.dot(rows, gate_ref[there, :], preferred_element_type=jnp.float32)
        up = up + jnp.dot(rows, up_ref[there, :], preferred_element_type=jnp.float32)
    if last:
        outs[0][...] = (gate / (1.0 + jnp.exp(-gate)) * up).astype(jnp.bfloat16)
    else:
        outs[0][...], outs[1][...] = gate, up


def hidden_units(gate_w, up_w, near, spans):
    features, units = gate_w.shape
    count = 2 * (near[0].shape[0] + spans[0][0].shape[0])
    sums, start = (), 0
    for span in spans:
        width = span[0].shape[1]
        last = start + width == features
        total = jax.ShapeDtypeStruct((count, units), jnp.float32)
        sums = pl.pallas_call(
            functools.partial(hidden_kernel, start, last),
            out_shape=(jax.ShapeDtypeStruct((count, units), jnp.bfloat16),) if last else (total, total),
            in_specs=[vmem()] * (6 + len(sums)),
            out_specs=(vmem(),) * (1 if last else 2),
            cost_estimate=pl.CostEstimate(
                flops=4 * units * count * width, bytes_accessed=4 * units * width, transcendentals=0
            ),
            compiler_params=pltpu.CompilerParams(vmem_limit_bytes=24 << 20),
        )(gate_w, up_w, *near, *span, *sums)
        start += width
    return sums[0]


def down_kernel(hidden_ref, down_ref, *outs):
    features = down_ref.shape[1]
    tile = math.gcd(features, 512)
    for first in range(0, features, tile):
        here = slice(first, first + tile)
        part = jnp.dot(hidden_ref[...], down_ref[:, here], preferred_element_type=jnp.float32)
        row = 0
        for out in outs:
            out[:, here] = part[row : row + out.shape[0]].astype(out.dtype)
            row += out.shape[0]


def down(hidden, down_w, counts):
    units, features = down_w.shape
    return pl.pallas_call(
        down_kernel,
        out_shape=[jax.ShapeDtypeStruct((count, features), jnp.float32) for count in counts]
        + [jax.ShapeDtypeStruct((count, features), jnp.bfloat16) for count in counts],
        in_specs=[vmem()] * 2,
        out_specs=[vmem()] * (2 * len(counts)),
        cost_estimate=pl.CostEstimate(
            flops=2 * hidden.size * features, bytes_accessed=2 * units * features, transcendentals=0
        ),
        compiler_params=pltpu.CompilerParams(vmem_limit_bytes=24 << 20),
    )(hidden, down_w)


def signs_twice():
    index = jnp.arange(BLOCK, dtype=jnp.int32)
    common = index[:, None] & index[None, :]
    for shift in (4, 2, 1):
        common = common ^ (common >> shift)
    signs = (1 - 2 * (common & 1)).astype(jnp.bfloat16)
    return jnp.concatenate([signs, signs])


def rotate_kernel(count, *refs):
    total_ref, *arrived = refs[: count + 1]
    sign_ref, matrix_ref, out_ref, turned_ref, sems = refs[count + 1 :]
    rows, features = total_ref.shape
    scale = 1.0 / math.sqrt(BLOCK)
    width = features // PIECES
    copies = []
    for k in range(PIECES):
        here = slice(k * width, (k + 1) * width)
        value = total_ref[:, here]
        for piece in arrived:
            value = value + piece[:, here].astype(jnp.float32)
        value = value * sign_ref[:, here].astype(jnp.float32)
        value = jnp.concatenate([value[:, b : b + BLOCK] for b in range(0, width, BLOCK)])
        high = value.astype(jnp.bfloat16)
        low = (value - high.astype(jnp.float32)).astype(jnp.bfloat16)
        both = jnp.concatenate([high, low], axis=1)
        turned = jnp.dot(both, matrix_ref[...], preferred_element_type=jnp.float32) * scale
        for b in range(width // BLOCK):
            first = k * width + b * BLOCK
            turned_ref[:, first : first + BLOCK] = turned[b * rows : (b + 1) * rows].astype(jnp.bfloat16)
        copies.append(pltpu.make_async_copy(turned_ref.at[:, here], out_ref.at[:, here], sems.at[k]))
        copies[-1].start()
    for copy in copies:
        copy.wait()


def rotate(total, arrived, signs):
    return pl.pallas_call(
        functools.partial(rotate_kernel, len(arrived)),
        out_shape=jax.ShapeDtypeStruct(total.shape, jnp.bfloat16),
        in_specs=[vmem()] * (len(arrived) + 3),
        out_specs=pl.BlockSpec(memory_space=pl.ANY),
        scratch_shapes=[pltpu.VMEM(total.shape, jnp.bfloat16), pltpu.SemaphoreType.DMA((PIECES,))],
        compiler_params=pltpu.CompilerParams(vmem_limit_bytes=16 << 20),
    )(total, *arrived, signs.reshape(1, -1), signs_twice())


def solution(mesh):
    members = mesh.shape["gx"]
    assert members & (members - 1) == 0 and members >= 16

    wide = []
    mask = members // 2
    while mask > 8:
        wide.append((mask, mask))
        mask //= 2

    def swap(value, masks):
        pairs = [(i, i ^ masks[i % 2]) for i in range(members) if masks[i % 2] is not None]
        return lax.ppermute(value, "gx", pairs)

    def narrow(value):
        return value.astype(jnp.bfloat16)

    def on_device(tokens, gate_weight, up_weight, down_weight, sign_pattern):
        features = tokens.shape[1]
        own = tokens
        for masks in wide:
            own = jnp.concatenate([own, swap(own, masks)])
        rows = own.shape[0]

        one, two, three = swap(own, FIRST), swap(own, SECOND), swap(own, THIRD)
        four, five, six = swap(one, (4, 2)), swap(one, (2, None)), swap(one, (6, None))
        beside = swap(two, (2, None))
        (gate_w,) = load((gate_weight.T,), (True,), one)
        gate_w, three, four, five, six, beside = lax.optimization_barrier((gate_w, three, four, five, six, beside))
        seven, eight, nine = swap(three, (None, 4)), swap(three, (None, 2)), swap(three, (None, 6))
        up_w, down_w = load((up_weight.T, down_weight), (True, False), three)
        up_w, beside, seven, eight, nine = lax.optimization_barrier((up_w, beside, seven, eight, nine))
        early = jnp.concatenate([own, one, two, three])
        early_there = swap(early, (1, 1))
        spans = []
        width = features // SPANS
        for k in range(SPANS):
            here = slice(k * width, (k + 1) * width)
            pieces = [five[:, here] + eight[:, here], six[:, here] + nine[:, here], beside[:, here] + seven[:, here]]
            span = jnp.concatenate([four[:, here]] + pieces)
            spans.append((span, swap(span, (1, 1))))
        hidden = hidden_units(gate_w, up_w, (early, early_there), spans)

        near, last, rest, *sends = down(hidden, down_w, (4 * rows, rows, 3 * rows))
        last = narrow(last + swap(sends[1], (1, 1)).astype(jnp.float32))
        rest_there, sends[0] = lax.optimization_barrier((swap(sends[2], (1, 1)), sends[0]))
        rest = narrow(rest + rest_there.astype(jnp.float32))
        both, diagonal, seven = (rest[k * rows : (k + 1) * rows] for k in range(3))
        near_there = swap(sends[0], (1, 1))
        a, b, c, g = swap(last, (4, 2)), swap(both, (2, None)), swap(diagonal, (6, None)), swap(seven, (2, None))
        e = swap(both, (None, 2))
        a, diagonal = lax.optimization_barrier((a, diagonal))
        f = swap(diagonal, (None, 6))
        b, seven = lax.optimization_barrier((b, seven))
        d = swap(seven, (None, 4))
        near = near + near_there.astype(jnp.float32)
        one = near[rows : 2 * rows]
        for piece in (a, b, c):
            one = one + piece.astype(jnp.float32)
        one, near = lax.optimization_barrier((narrow(one), near))
        own, _, two, three = (near[k * rows : (k + 1) * rows] for k in range(4))
        for piece in (d, e, f):
            three = three + piece.astype(jnp.float32)
        three, g = lax.optimization_barrier((narrow(three), g))
        two = narrow(two + g.astype(jnp.float32))
        arrived = [swap(one, FIRST), swap(two, SECOND), swap(three, THIRD)]
        for k in (2, 0):
            own, arrived[k] = lax.optimization_barrier((own, arrived[k]))
            own = own + arrived[k].astype(jnp.float32)
        own, *arrived = lax.optimization_barrier((own, arrived[1]))
        if wide:
            own = own + arrived.pop().astype(jnp.float32)
        for masks in reversed(wide):
            half = own.shape[0] // 2
            own = own[:half] + swap(narrow(own[half:]), masks).astype(jnp.float32)
        return rotate(own, arrived, sign_pattern)

    placed = (P(("groups", "gx"), None), P(None, "gx"), P(None, "gx"), P("gx", None), P())
    return jax.shard_map(
        on_device, mesh=mesh, in_specs=placed, out_specs=P(("groups", "gx"), None), check_vma=False
    )
```

```python
import functools
import math

import jax
import jax.numpy as jnp
from jax import lax
from jax.experimental import pallas as pl
from jax.experimental.pallas import tpu as pltpu
from jax.sharding import PartitionSpec as P

BLOCK = 128
PIECES = 2
SPANS = 2
TURNS = 8
FIRST, SECOND, THIRD = (8, 4), (4, 2), (2, 8)
NT = (((1,), (1,)), ((), ()))


def vmem():
    return pl.BlockSpec(memory_space=pltpu.VMEM)


def load_kernel(turned, *refs):
    count = len(turned)
    sources, outs = refs[:count], refs[count + 1 : 2 * count + 1]
    staged, sems = refs[2 * count + 1 :]
    tile = staged.shape[1] // (sems.shape[0] - 1)
    copies = []
    for source, out, turn in zip(sources, outs, turned):
        if not turn:
            continue
        for k in range(sems.shape[0] - 1):
            here = slice(k * tile, (k + 1) * tile)
            copies.append((pltpu.make_async_copy(source.at[:, here], staged.at[:, here], sems.at[k]), out, here))
    others = [
        pltpu.make_async_copy(source, out, sems.at[sems.shape[0] - 1])
        for source, out, turn in zip(sources, outs, turned)
        if not turn
    ]
    for copy, _, _ in copies:
        copy.start()
    for copy in others:
        copy.start()
    for copy, out, here in copies:
        copy.wait()
        out[here, :] = staged[:, here].T
    for copy in others:
        copy.wait()


def load(weights, turned, after):
    shapes = [w.shape[::-1] if turn else w.shape for w, turn in zip(weights, turned)]
    size = sum(w.size for w in weights)
    return pl.pallas_call(
        functools.partial(load_kernel, turned),
        out_shape=[jax.ShapeDtypeStruct(shape, weights[0].dtype) for shape in shapes],
        in_specs=[pl.BlockSpec(memory_space=pltpu.HBM)] * len(weights) + [pl.BlockSpec(memory_space=pl.ANY)],
        out_specs=[vmem()] * len(weights),
        scratch_shapes=[
            pltpu.VMEM(weights[0].shape, weights[0].dtype),
            pltpu.SemaphoreType.DMA((TURNS + 1,)),
        ],
        cost_estimate=pl.CostEstimate(flops=0, bytes_accessed=4 * size, transcendentals=0),
        compiler_params=pltpu.CompilerParams(vmem_limit_bytes=16 << 20),
    )(*(pltpu.with_memory_space_constraint(w, pltpu.HBM) for w in weights), after)


def hidden_kernel(start, last, *refs):
    gate_ref, up_ref, near_here, near_there, far_here, far_there, *refs = refs
    sums, outs = refs[: len(refs) - (1 if last else 2)], refs[-1 if last else -2 :]
    width = far_here.shape[1]
    tile = math.gcd(width, 1024)
    gate, up = (ref[...] for ref in sums) if sums else (0.0, 0.0)
    for first in range(0, width, tile):
        here, there = slice(first, first + tile), slice(start + first, start + first + tile)
        rows = jnp.concatenate([near_here[:, there], far_here[:, here], near_there[:, there], far_there[:, here]])
        gate = gate + jnp.dot(rows, gate_ref[there, :], preferred_element_type=jnp.float32)
        up = up + jnp.dot(rows, up_ref[there, :], preferred_element_type=jnp.float32)
    if last:
        outs[0][...] = (gate / (1.0 + jnp.exp(-gate)) * up).astype(jnp.bfloat16)
    else:
        outs[0][...], outs[1][...] = gate, up


def hidden_units(gate_w, up_w, near, spans):
    features, units = gate_w.shape
    count = 2 * (near[0].shape[0] + spans[0][0].shape[0])
    sums, start = (), 0
    for span in spans:
        width = span[0].shape[1]
        last = start + width == features
        total = jax.ShapeDtypeStruct((count, units), jnp.float32)
        sums = pl.pallas_call(
            functools.partial(hidden_kernel, start, last),
            out_shape=(jax.ShapeDtypeStruct((count, units), jnp.bfloat16),) if last else (total, total),
            in_specs=[vmem()] * (6 + len(sums)),
            out_specs=(vmem(),) * (1 if last else 2),
            cost_estimate=pl.CostEstimate(
                flops=4 * units * count * width, bytes_accessed=4 * units * width, transcendentals=0
            ),
            compiler_params=pltpu.CompilerParams(vmem_limit_bytes=24 << 20),
        )(gate_w, up_w, *near, *span, *sums)
        start += width
    return sums[0]


def down_kernel(hidden_ref, down_ref, *outs):
    features = down_ref.shape[1]
    tile = math.gcd(features, 512)
    for first in range(0, features, tile):
        here = slice(first, first + tile)
        part = jnp.dot(hidden_ref[...], down_ref[:, here], preferred_element_type=jnp.float32)
        row = 0
        for out in outs:
            out[:, here] = part[row : row + out.shape[0]].astype(out.dtype)
            row += out.shape[0]


def down(hidden, down_w, counts):
    units, features = down_w.shape
    return pl.pallas_call(
        down_kernel,
        out_shape=[jax.ShapeDtypeStruct((count, features), jnp.float32) for count in counts]
        + [jax.ShapeDtypeStruct((count, features), jnp.bfloat16) for count in counts],
        in_specs=[vmem()] * 2,
        out_specs=[vmem()] * (2 * len(counts)),
        cost_estimate=pl.CostEstimate(
            flops=2 * hidden.size * features, bytes_accessed=2 * units * features, transcendentals=0
        ),
        compiler_params=pltpu.CompilerParams(vmem_limit_bytes=24 << 20),
    )(hidden, down_w)


def signs_twice():
    index = jnp.arange(BLOCK, dtype=jnp.int32)
    common = index[:, None] & index[None, :]
    for shift in (4, 2, 1):
        common = common ^ (common >> shift)
    signs = (1 - 2 * (common & 1)).astype(jnp.bfloat16)
    return jnp.concatenate([signs, signs])


def rotate_kernel(count, *refs):
    total_ref, *arrived = refs[: count + 1]
    sign_ref, matrix_ref, out_ref, turned_ref, sems = refs[count + 1 :]
    rows, features = total_ref.shape
    scale = 1.0 / math.sqrt(BLOCK)
    width = features // PIECES
    copies = []
    for k in range(PIECES):
        here = slice(k * width, (k + 1) * width)
        value = total_ref[:, here]
        for piece in arrived:
            value = value + piece[:, here].astype(jnp.float32)
        value = value * sign_ref[:, here].astype(jnp.float32)
        value = jnp.concatenate([value[:, b : b + BLOCK] for b in range(0, width, BLOCK)])
        high = value.astype(jnp.bfloat16)
        low = (value - high.astype(jnp.float32)).astype(jnp.bfloat16)
        both = jnp.concatenate([high, low], axis=1)
        turned = jnp.dot(both, matrix_ref[...], preferred_element_type=jnp.float32) * scale
        for b in range(width // BLOCK):
            first = k * width + b * BLOCK
            turned_ref[:, first : first + BLOCK] = turned[b * rows : (b + 1) * rows].astype(jnp.bfloat16)
        copies.append(pltpu.make_async_copy(turned_ref.at[:, here], out_ref.at[:, here], sems.at[k]))
        copies[-1].start()
    for copy in copies:
        copy.wait()


def rotate(total, arrived, signs):
    return pl.pallas_call(
        functools.partial(rotate_kernel, len(arrived)),
        out_shape=jax.ShapeDtypeStruct(total.shape, jnp.bfloat16),
        in_specs=[vmem()] * (len(arrived) + 3),
        out_specs=pl.BlockSpec(memory_space=pl.ANY),
        scratch_shapes=[pltpu.VMEM(total.shape, jnp.bfloat16), pltpu.SemaphoreType.DMA((PIECES,))],
        compiler_params=pltpu.CompilerParams(vmem_limit_bytes=16 << 20),
    )(total, *arrived, signs.reshape(1, -1), signs_twice())


def solution(mesh):
    members = mesh.shape["gx"]
    assert members & (members - 1) == 0 and members >= 16

    wide = []
    mask = members // 2
    while mask > 8:
        wide.append((mask, mask))
        mask //= 2

    def swap(value, masks):
        return lax.ppermute(value, "gx", [(i, i ^ masks[i % 2]) for i in range(members)])

    def narrow(value):
        return value.astype(jnp.bfloat16)

    def on_device(tokens, gate_weight, up_weight, down_weight, sign_pattern):
        features = tokens.shape[1]
        even = lax.axis_index("gx") % 2 == 0
        own = tokens
        for masks in wide:
            own = jnp.concatenate([own, swap(own, masks)])
        rows = own.shape[0]

        one, two, three = swap(own, FIRST), swap(own, SECOND), swap(own, THIRD)
        four, five, six = swap(one, (4, 2)), swap(one, (2, 0)), swap(one, (6, 0))
        beside = swap(two, (2, 0))
        (gate_w,) = load((gate_weight.T,), (True,), one)
        gate_w, three, four, five, six, beside = lax.optimization_barrier((gate_w, three, four, five, six, beside))
        seven, eight, nine = swap(three, (0, 4)), swap(three, (0, 2)), swap(three, (0, 6))
        up_w, down_w = load((up_weight.T, down_weight), (True, False), three)
        up_w, beside, seven, eight, nine = lax.optimization_barrier((up_w, beside, seven, eight, nine))
        early = jnp.concatenate([own, one, two, three])
        early_there = swap(early, (1, 1))
        spans = []
        width = features // SPANS
        for k in range(SPANS):
            here = slice(k * width, (k + 1) * width)
            pairs = ((five, eight), (six, nine), (beside, seven))
            pieces = [jnp.where(even, a[:, here], b[:, here]) for a, b in pairs]
            span = jnp.concatenate([four[:, here]] + pieces)
            spans.append((span, swap(span, (1, 1))))
        hidden = hidden_units(gate_w, up_w, (early, early_there), spans)

        near, last, rest, *sends = down(hidden, down_w, (4 * rows, rows, 3 * rows))
        last = narrow(last + swap(sends[1], (1, 1)).astype(jnp.float32))
        rest_there, sends[0] = lax.optimization_barrier((swap(sends[2], (1, 1)), sends[0]))
        rest = narrow(rest + rest_there.astype(jnp.float32))
        both, diagonal, seven = (rest[k * rows : (k + 1) * rows] for k in range(3))
        near_there = swap(sends[0], (1, 1))
        a, b, c, g = swap(last, (4, 2)), swap(both, (2, 0)), swap(diagonal, (6, 0)), swap(seven, (2, 0))
        e = swap(both, (0, 2))
        a, diagonal = lax.optimization_barrier((a, diagonal))
        f = swap(diagonal, (0, 6))
        b, seven = lax.optimization_barrier((b, seven))
        d = swap(seven, (0, 4))
        near = near + near_there.astype(jnp.float32)
        one = near[rows : 2 * rows]
        one = one + a.astype(jnp.float32)
        one = one + jnp.where(even, b.astype(jnp.float32) + c.astype(jnp.float32), 0.0)
        one, near = lax.optimization_barrier((narrow(one), near))
        own, _, two, three = (near[k * rows : (k + 1) * rows] for k in range(4))
        there = d.astype(jnp.float32) + e.astype(jnp.float32) + f.astype(jnp.float32)
        three = three + jnp.where(even, 0.0, there)
        three, g = lax.optimization_barrier((narrow(three), g))
        two = narrow(two + jnp.where(even, g.astype(jnp.float32), 0.0))
        arrived = [swap(one, FIRST), swap(two, SECOND), swap(three, THIRD)]
        for k in (2, 0):
            own, arrived[k] = lax.optimization_barrier((own, arrived[k]))
            own = own + arrived[k].astype(jnp.float32)
        own, *arrived = lax.optimization_barrier((own, arrived[1]))
        if wide:
            own = own + arrived.pop().astype(jnp.float32)
        for masks in reversed(wide):
            half = own.shape[0] // 2
            own = own[:half] + swap(narrow(own[half:]), masks).astype(jnp.float32)
        return rotate(own, arrived, sign_pattern)

    placed = (P(("groups", "gx"), 0), P(0, "gx"), P(0, "gx"), P("gx", 0), P())
    return jax.shard_map(
        on_device, mesh=mesh, in_specs=placed, out_specs=P(("groups", "gx"), 0), check_vma=False
    )
```

```python
import functools
import math

import jax
import jax.numpy as jnp
from jax import lax
from jax.experimental import pallas as pl
from jax.experimental.pallas import tpu as pltpu
from jax.sharding import PartitionSpec as P

BLOCK = 128
PIECES = 2
SPANS = 2
TURNS = 8
NT = (((1,), (1,)), ((), ()))


def vmem():
    return pl.BlockSpec(memory_space=pltpu.VMEM)


def load_kernel(gate_hbm, up_hbm, down_hbm, _, gate_ref, up_ref, down_ref, staged, sems, down_sem):
    tile = staged.shape[2] // sems.shape[1]
    copies = []
    for k in range(sems.shape[1]):
        here = slice(k * tile, (k + 1) * tile)
        for j, source in enumerate((gate_hbm, up_hbm)):
            copies.append(
                pltpu.make_async_copy(source.at[:, here], staged.at[j, :, here], sems.at[j, k])
            )
            copies[-1].start()
    down_copy = pltpu.make_async_copy(down_hbm, down_ref, down_sem)
    down_copy.start()
    for k in range(sems.shape[1]):
        here = slice(k * tile, (k + 1) * tile)
        for j, out in enumerate((gate_ref, up_ref)):
            copies[2 * k + j].wait()
            out[here, :] = staged[j, :, here].T
    down_copy.wait()


def load(gate_w, up_w, down_w, after):
    units, features = gate_w.shape
    shape = jax.ShapeDtypeStruct((features, units), gate_w.dtype)
    return pl.pallas_call(
        load_kernel,
        out_shape=(shape, shape, jax.ShapeDtypeStruct(down_w.shape, down_w.dtype)),
        in_specs=[pl.BlockSpec(memory_space=pltpu.HBM)] * 3 + [pl.BlockSpec(memory_space=pl.ANY)],
        out_specs=(vmem(),) * 3,
        scratch_shapes=[
            pltpu.VMEM((2, units, features), gate_w.dtype),
            pltpu.SemaphoreType.DMA((2, TURNS)),
            pltpu.SemaphoreType.DMA,
        ],
        cost_estimate=pl.CostEstimate(flops=0, bytes_accessed=6 * units * features, transcendentals=0),
        compiler_params=pltpu.CompilerParams(vmem_limit_bytes=24 << 20),
    )(*(pltpu.with_memory_space_constraint(w, pltpu.HBM) for w in (gate_w, up_w, down_w)), after)


def hidden_kernel(start, last, *refs):
    gate_ref, up_ref, near_here, near_there, far_here, far_there, *refs = refs
    sums, outs = refs[: len(refs) - (1 if last else 2)], refs[-1 if last else -2 :]
    width = far_here.shape[1]
    tile = math.gcd(width, 1024)
    gate, up = (ref[...] for ref in sums) if sums else (0.0, 0.0)
    for first in range(0, width, tile):
        here, there = slice(first, first + tile), slice(start + first, start + first + tile)
        rows = jnp.concatenate([near_here[:, there], far_here[:, here], near_there[:, there], far_there[:, here]])
        gate = gate + jnp.dot(rows, gate_ref[there, :], preferred_element_type=jnp.float32)
        up = up + jnp.dot(rows, up_ref[there, :], preferred_element_type=jnp.float32)
    if last:
        outs[0][...] = (gate / (1.0 + jnp.exp(-gate)) * up).astype(jnp.bfloat16)
    else:
        outs[0][...], outs[1][...] = gate, up


def hidden_units(gate_w, up_w, near, spans):
    features, units = gate_w.shape
    count = 2 * (near[0].shape[0] + spans[0][0].shape[0])
    sums, start = (), 0
    for span in spans:
        width = span[0].shape[1]
        last = start + width == features
        total = jax.ShapeDtypeStruct((count, units), jnp.float32)
        sums = pl.pallas_call(
            functools.partial(hidden_kernel, start, last),
            out_shape=(jax.ShapeDtypeStruct((count, units), jnp.bfloat16),) if last else (total, total),
            in_specs=[vmem()] * (6 + len(sums)),
            out_specs=(vmem(),) * (1 if last else 2),
            cost_estimate=pl.CostEstimate(
                flops=4 * units * count * width, bytes_accessed=4 * units * width, transcendentals=0
            ),
            compiler_params=pltpu.CompilerParams(vmem_limit_bytes=24 << 20),
        )(gate_w, up_w, *near, *span, *sums)
        start += width
    return sums[0]


def down_kernel(hidden_ref, down_ref, *outs):
    features = down_ref.shape[1]
    tile = math.gcd(features, 512)
    for first in range(0, features, tile):
        here = slice(first, first + tile)
        part = jnp.dot(hidden_ref[...], down_ref[:, here], preferred_element_type=jnp.float32)
        row = 0
        for out in outs:
            out[:, here] = part[row : row + out.shape[0]].astype(out.dtype)
            row += out.shape[0]


def down(hidden, down_w, counts):
    units, features = down_w.shape
    return pl.pallas_call(
        down_kernel,
        out_shape=[jax.ShapeDtypeStruct((count, features), jnp.float32) for count in counts]
        + [jax.ShapeDtypeStruct((count, features), jnp.bfloat16) for count in counts],
        in_specs=[vmem()] * 2,
        out_specs=[vmem()] * (2 * len(counts)),
        cost_estimate=pl.CostEstimate(
            flops=2 * hidden.size * features, bytes_accessed=2 * units * features, transcendentals=0
        ),
        compiler_params=pltpu.CompilerParams(vmem_limit_bytes=24 << 20),
    )(hidden, down_w)


def signs_twice():
    index = jnp.arange(BLOCK, dtype=jnp.int32)
    common = index[:, None] & index[None, :]
    for shift in (4, 2, 1):
        common = common ^ (common >> shift)
    signs = (1 - 2 * (common & 1)).astype(jnp.bfloat16)
    return jnp.concatenate([signs, signs])


def rotate_kernel(count, *refs):
    total_ref, *arrived = refs[: count + 1]
    sign_ref, matrix_ref, out_ref, turned_ref, sems = refs[count + 1 :]
    rows, features = total_ref.shape
    scale = 1.0 / math.sqrt(BLOCK)
    width = features // PIECES
    copies = []
    for k in range(PIECES):
        here = slice(k * width, (k + 1) * width)
        value = total_ref[:, here]
        for piece in arrived:
            value = value + piece[:, here].astype(jnp.float32)
        value = value * sign_ref[:, here].astype(jnp.float32)
        value = jnp.concatenate([value[:, b : b + BLOCK] for b in range(0, width, BLOCK)])
        high = value.astype(jnp.bfloat16)
        low = (value - high.astype(jnp.float32)).astype(jnp.bfloat16)
        both = jnp.concatenate([high, low], axis=1)
        turned = jnp.dot(both, matrix_ref[...], preferred_element_type=jnp.float32) * scale
        for b in range(width // BLOCK):
            first = k * width + b * BLOCK
            turned_ref[:, first : first + BLOCK] = turned[b * rows : (b + 1) * rows].astype(jnp.bfloat16)
        copies.append(pltpu.make_async_copy(turned_ref.at[:, here], out_ref.at[:, here], sems.at[k]))
        copies[-1].start()
    for copy in copies:
        copy.wait()


def rotate(total, arrived, signs):
    return pl.pallas_call(
        functools.partial(rotate_kernel, len(arrived)),
        out_shape=jax.ShapeDtypeStruct(total.shape, jnp.bfloat16),
        in_specs=[vmem()] * (len(arrived) + 3),
        out_specs=pl.BlockSpec(memory_space=pl.ANY),
        scratch_shapes=[pltpu.VMEM(total.shape, jnp.bfloat16), pltpu.SemaphoreType.DMA((PIECES,))],
        compiler_params=pltpu.CompilerParams(vmem_limit_bytes=16 << 20),
    )(total, *arrived, signs.reshape(1, -1), signs_twice())


def solution(mesh):
    members = mesh.shape["gx"]
    assert members & (members - 1) == 0 and members >= 16

    far = []
    mask = members // 2
    while mask > 8:
        far.append((mask, mask))
        mask //= 2
    far.append((8, 4))
    square = ((4, 2), (2, 8), (6, 10))
    others = members // 8 - 1

    def swap(value, masks):
        return lax.ppermute(value, "gx", [(i, i ^ masks[i % 2]) for i in range(members)])

    def on_device(tokens, gate_weight, up_weight, down_weight, sign_pattern):
        rows, features = tokens.shape

        away = []
        for masks in far:
            away.append(swap(jnp.concatenate([tokens] + away), masks))
        away = jnp.concatenate(away)
        near = [swap(tokens, m) for m in square]
        there = [swap(away, m) for m in square[:2]]
        away, near[0] = lax.optimization_barrier((away, near[0]))
        there.append(swap(away, square[2]))
        gate_w, up_w, down_w = load(gate_weight.T, up_weight.T, down_weight, away)
        there[0], *near = lax.optimization_barrier((there[0], *near))
        near = jnp.concatenate([tokens, near[1], near[0], near[2]])
        near_there = swap(near, (1, 1))
        gate_w, up_w, near, *there[1:] = lax.optimization_barrier((gate_w, up_w, near, *there[1:]))
        far_rows = [there[2], away, *there[:2]]
        spans = []
        width = features // SPANS
        for k in range(SPANS):
            span = jnp.concatenate([piece[:, k * width : (k + 1) * width] for piece in far_rows])
            spans.append((span, swap(span, (1, 1))))
        hidden = hidden_units(gate_w, up_w, (near, near_there), spans)

        count = others * rows
        own, diagonal, rest, *sends = down(hidden, down_w, (4 * rows, count, 3 * count))
        diagonal = diagonal + swap(sends[1], (1, 1)).astype(jnp.float32)
        diagonal = swap(diagonal.astype(jnp.bfloat16), square[2])
        rest_there, sends[0] = lax.optimization_barrier((swap(sends[2], (1, 1)), sends[0]))
        rest = rest + rest_there.astype(jnp.float32)
        leave = rest[count:].astype(jnp.bfloat16)
        total = rest[:count]
        for piece in (diagonal, swap(leave[:count], square[0]), swap(leave[count:], square[1])):
            total = total + piece.astype(jnp.float32)
        arrived = []
        for masks in reversed(far):
            split = total.shape[0] // 2 // rows * rows
            piece = swap(total[split:].astype(jnp.bfloat16), masks)
            arrived.append(piece[:rows])
            total = total[:split] + piece[rows:].astype(jnp.float32)

        own = own + swap(sends[0], (1, 1)).astype(jnp.float32)
        own = own[: 2 * rows] + swap(own[2 * rows :].astype(jnp.bfloat16), square[0]).astype(jnp.float32)
        arrived.append(swap(own[rows:].astype(jnp.bfloat16), square[1]))
        return rotate(own[:rows], arrived, sign_pattern)

    placed = (P(("groups", "gx"), None), P(None, "gx"), P(None, "gx"), P("gx", None), P())
    return jax.shard_map(
        on_device, mesh=mesh, in_specs=placed, out_specs=P(("groups", "gx"), None), check_vma=False
    )
```

```python
import functools
import math

import jax
import jax.numpy as jnp
from jax import lax
from jax.experimental import pallas as pl
from jax.experimental.pallas import tpu as pltpu
from jax.sharding import PartitionSpec as P

BLOCK = 128
PIECES = 2
SPANS = 2
TURNS = 8
NT = (((1,), (1,)), ((), ()))


def vmem():
    return pl.BlockSpec(memory_space=pltpu.VMEM)


def load_kernel(gate_hbm, up_hbm, down_hbm, _, gate_ref, up_ref, down_ref, staged, sems, down_sem):
    tile = staged.shape[2] // sems.shape[1]
    copies = []
    for k in range(sems.shape[1]):
        here = slice(k * tile, (k + 1) * tile)
        for j, source in enumerate((gate_hbm, up_hbm)):
            copies.append(
                pltpu.make_async_copy(source.at[:, here], staged.at[j, :, here], sems.at[j, k])
            )
            copies[-1].start()
    down_copy = pltpu.make_async_copy(down_hbm, down_ref, down_sem)
    down_copy.start()
    for k in range(sems.shape[1]):
        here = slice(k * tile, (k + 1) * tile)
        for j, out in enumerate((gate_ref, up_ref)):
            copies[2 * k + j].wait()
            out[here, :] = staged[j, :, here].T
    down_copy.wait()


def load(gate_w, up_w, down_w, after):
    units, features = gate_w.shape
    shape = jax.ShapeDtypeStruct((features, units), gate_w.dtype)
    return pl.pallas_call(
        load_kernel,
        out_shape=(shape, shape, jax.ShapeDtypeStruct(down_w.shape, down_w.dtype)),
        in_specs=[pl.BlockSpec(memory_space=pltpu.HBM)] * 3 + [pl.BlockSpec(memory_space=pl.ANY)],
        out_specs=(vmem(),) * 3,
        scratch_shapes=[
            pltpu.VMEM((2, units, features), gate_w.dtype),
            pltpu.SemaphoreType.DMA((2, TURNS)),
            pltpu.SemaphoreType.DMA,
        ],
        cost_estimate=pl.CostEstimate(flops=0, bytes_accessed=6 * units * features, transcendentals=0),
        compiler_params=pltpu.CompilerParams(vmem_limit_bytes=24 << 20),
    )(*(pltpu.with_memory_space_constraint(w, pltpu.HBM) for w in (gate_w, up_w, down_w)), after)


def hidden_kernel(start, last, *refs):
    gate_ref, up_ref, near_here, near_there, far_here, far_there, *refs = refs
    sums, outs = refs[: len(refs) - (1 if last else 2)], refs[-1 if last else -2 :]
    width = far_here.shape[1]
    tile = math.gcd(width, 1024)
    gate, up = (ref[...] for ref in sums) if sums else (0.0, 0.0)
    for first in range(0, width, tile):
        here, there = slice(first, first + tile), slice(start + first, start + first + tile)
        rows = jnp.concatenate([near_here[:, there], far_here[:, here], near_there[:, there], far_there[:, here]])
        gate = gate + jnp.dot(rows, gate_ref[there, :], preferred_element_type=jnp.float32)
        up = up + jnp.dot(rows, up_ref[there, :], preferred_element_type=jnp.float32)
    if last:
        outs[0][...] = (gate / (1.0 + jnp.exp(-gate)) * up).astype(jnp.bfloat16)
    else:
        outs[0][...], outs[1][...] = gate, up


def hidden_units(gate_w, up_w, near, spans):
    features, units = gate_w.shape
    count = 2 * (near[0].shape[0] + spans[0][0].shape[0])
    sums, start = (), 0
    for span in spans:
        width = span[0].shape[1]
        last = start + width == features
        total = jax.ShapeDtypeStruct((count, units), jnp.float32)
        sums = pl.pallas_call(
            functools.partial(hidden_kernel, start, last),
            out_shape=(jax.ShapeDtypeStruct((count, units), jnp.bfloat16),) if last else (total, total),
            in_specs=[vmem()] * (6 + len(sums)),
            out_specs=(vmem(),) * (1 if last else 2),
            cost_estimate=pl.CostEstimate(
                flops=4 * units * count * width, bytes_accessed=4 * units * width, transcendentals=0
            ),
            compiler_params=pltpu.CompilerParams(vmem_limit_bytes=24 << 20),
        )(gate_w, up_w, *near, *span, *sums)
        start += width
    return sums[0]


def down_kernel(hidden_ref, down_ref, *outs):
    features = down_ref.shape[1]
    tile = math.gcd(features, 512)
    for first in range(0, features, tile):
        here = slice(first, first + tile)
        part = jnp.dot(hidden_ref[...], down_ref[:, here], preferred_element_type=jnp.float32)
        row = 0
        for out in outs:
            out[:, here] = part[row : row + out.shape[0]].astype(out.dtype)
            row += out.shape[0]


def down(hidden, down_w, counts):
    units, features = down_w.shape
    return pl.pallas_call(
        down_kernel,
        out_shape=[jax.ShapeDtypeStruct((count, features), jnp.float32) for count in counts]
        + [jax.ShapeDtypeStruct((count, features), jnp.bfloat16) for count in counts],
        in_specs=[vmem()] * 2,
        out_specs=[vmem()] * (2 * len(counts)),
        cost_estimate=pl.CostEstimate(
            flops=2 * hidden.size * features, bytes_accessed=2 * units * features, transcendentals=0
        ),
        compiler_params=pltpu.CompilerParams(vmem_limit_bytes=24 << 20),
    )(hidden, down_w)


def signs_twice():
    index = jnp.arange(BLOCK, dtype=jnp.int32)
    common = index[:, None] & index[None, :]
    for shift in (4, 2, 1):
        common = common ^ (common >> shift)
    signs = (1 - 2 * (common & 1)).astype(jnp.bfloat16)
    return jnp.concatenate([signs, signs])


def rotate_kernel(count, *refs):
    total_ref, *arrived = refs[: count + 1]
    sign_ref, matrix_ref, out_ref, turned_ref, sems = refs[count + 1 :]
    rows, features = total_ref.shape
    scale = 1.0 / math.sqrt(BLOCK)
    width = features // PIECES
    copies = []
    for k in range(PIECES):
        here = slice(k * width, (k + 1) * width)
        value = total_ref[:, here]
        for piece in arrived:
            value = value + piece[:, here].astype(jnp.float32)
        value = value * sign_ref[:, here].astype(jnp.float32)
        value = jnp.concatenate([value[:, b : b + BLOCK] for b in range(0, width, BLOCK)])
        high = value.astype(jnp.bfloat16)
        low = (value - high.astype(jnp.float32)).astype(jnp.bfloat16)
        both = jnp.concatenate([high, low], axis=1)
        turned = jnp.dot(both, matrix_ref[...], preferred_element_type=jnp.float32) * scale
        for b in range(width // BLOCK):
            first = k * width + b * BLOCK
            turned_ref[:, first : first + BLOCK] = turned[b * rows : (b + 1) * rows].astype(jnp.bfloat16)
        copies.append(pltpu.make_async_copy(turned_ref.at[:, here], out_ref.at[:, here], sems.at[k]))
        copies[-1].start()
    for copy in copies:
        copy.wait()


def rotate(total, arrived, signs):
    return pl.pallas_call(
        functools.partial(rotate_kernel, len(arrived)),
        out_shape=jax.ShapeDtypeStruct(total.shape, jnp.bfloat16),
        in_specs=[vmem()] * (len(arrived) + 3),
        out_specs=pl.BlockSpec(memory_space=pl.ANY),
        scratch_shapes=[pltpu.VMEM(total.shape, jnp.bfloat16), pltpu.SemaphoreType.DMA((PIECES,))],
        compiler_params=pltpu.CompilerParams(vmem_limit_bytes=16 << 20),
    )(total, *arrived, signs.reshape(1, -1), signs_twice())


def solution(mesh):
    members = mesh.shape["gx"]
    assert members & (members - 1) == 0 and members >= 16

    square = ((4, 2), (2, 4), (6, 6))
    far = []
    mask = members // 2
    while mask > 4:
        far.append((mask, mask))
        mask //= 2
    others = members // 8 - 1

    def swap(value, masks):
        return lax.ppermute(value, "gx", [(i, i ^ masks[i % 2]) for i in range(members)])

    def on_device(tokens, gate_weight, up_weight, down_weight, sign_pattern):
        rows, features = tokens.shape

        away = []
        for masks in far:
            away.append(swap(jnp.concatenate([tokens] + away), masks))
        away = jnp.concatenate(away)
        near = [swap(tokens, m) for m in square]
        away, sign_pattern = lax.optimization_barrier((away, sign_pattern))
        there = [swap(away, m) for m in square[:2]]
        away, near[0] = lax.optimization_barrier((away, near[0]))
        there.append(swap(away, square[2]))
        gate_w, up_w, down_w = load(gate_weight.T, up_weight.T, down_weight, away)
        there[0], *near = lax.optimization_barrier((there[0], *near))
        near = jnp.concatenate([tokens, near[1], near[0], near[2]])
        near_there = swap(near, (1, 1))
        gate_w, up_w, near, *there[1:] = lax.optimization_barrier((gate_w, up_w, near, *there[1:]))
        far_rows = [there[2], away, *there[:2]]
        spans = []
        width = features // SPANS
        for k in range(SPANS):
            span = jnp.concatenate([piece[:, k * width : (k + 1) * width] for piece in far_rows])
            spans.append((span, swap(span, (1, 1))))
        hidden = hidden_units(gate_w, up_w, (near, near_there), spans)

        count = others * rows
        own, diagonal, rest, *sends = down(hidden, down_w, (4 * rows, count, 3 * count))
        diagonal = diagonal + swap(sends[1], (1, 1)).astype(jnp.float32)
        diagonal = swap(diagonal.astype(jnp.bfloat16), square[2])
        rest_there, sends[0] = lax.optimization_barrier((swap(sends[2], (1, 1)), sends[0]))
        rest = rest + rest_there.astype(jnp.float32)
        leave = rest[count:].astype(jnp.bfloat16)
        total = rest[:count]
        for piece in (diagonal, swap(leave[:count], square[0]), swap(leave[count:], square[1])):
            total = total + piece.astype(jnp.float32)
        arrived = []
        for masks in reversed(far):
            split = total.shape[0] // 2 // rows * rows
            piece = swap(total[split:].astype(jnp.bfloat16), masks)
            arrived.append(piece[:rows])
            total = total[:split] + piece[rows:].astype(jnp.float32)

        own = own + swap(sends[0], (1, 1)).astype(jnp.float32)
        own = own[: 2 * rows] + swap(own[2 * rows :].astype(jnp.bfloat16), square[0]).astype(jnp.float32)
        arrived.append(swap(own[rows:].astype(jnp.bfloat16), square[1]))
        return rotate(own[:rows], arrived, sign_pattern)

    placed = (P(("groups", "gx"), None), P(None, "gx"), P(None, "gx"), P("gx", None), P())
    return jax.shard_map(
        on_device, mesh=mesh, in_specs=placed, out_specs=P(("groups", "gx"), None), check_vma=False
    )
```

```python
import functools
import math

import jax
import jax.numpy as jnp
from jax import lax
from jax.experimental import pallas as pl
from jax.experimental.pallas import tpu as pltpu
from jax.sharding import PartitionSpec as P

BLOCK = 128
PIECES = 2
SPANS = 2
TURNS = 8
NT = (((1,), (1,)), ((), ()))


def vmem():
    return pl.BlockSpec(memory_space=pltpu.VMEM)


def load_kernel(gate_hbm, up_hbm, down_hbm, _, gate_ref, up_ref, down_ref, staged, sems, down_sem):
    tile = staged.shape[2] // sems.shape[1]
    copies = []
    for k in range(sems.shape[1]):
        here = slice(k * tile, (k + 1) * tile)
        for j, source in enumerate((gate_hbm, up_hbm)):
            copies.append(
                pltpu.make_async_copy(source.at[:, here], staged.at[j, :, here], sems.at[j, k])
            )
            copies[-1].start()
    down_copy = pltpu.make_async_copy(down_hbm, down_ref, down_sem)
    down_copy.start()
    for k in range(sems.shape[1]):
        here = slice(k * tile, (k + 1) * tile)
        for j, out in enumerate((gate_ref, up_ref)):
            copies[2 * k + j].wait()
            out[here, :] = staged[j, :, here].T
    down_copy.wait()


def load(gate_w, up_w, down_w, after):
    units, features = gate_w.shape
    shape = jax.ShapeDtypeStruct((features, units), gate_w.dtype)
    return pl.pallas_call(
        load_kernel,
        out_shape=(shape, shape, jax.ShapeDtypeStruct(down_w.shape, down_w.dtype)),
        in_specs=[pl.BlockSpec(memory_space=pltpu.HBM)] * 3 + [pl.BlockSpec(memory_space=pl.ANY)],
        out_specs=(vmem(),) * 3,
        scratch_shapes=[
            pltpu.VMEM((2, units, features), gate_w.dtype),
            pltpu.SemaphoreType.DMA((2, TURNS)),
            pltpu.SemaphoreType.DMA,
        ],
        cost_estimate=pl.CostEstimate(flops=0, bytes_accessed=6 * units * features, transcendentals=0),
        compiler_params=pltpu.CompilerParams(vmem_limit_bytes=24 << 20),
    )(*(pltpu.with_memory_space_constraint(w, pltpu.HBM) for w in (gate_w, up_w, down_w)), after)


def hidden_kernel(start, last, *refs):
    gate_ref, up_ref, near_here, near_there, far_here, far_there, *refs = refs
    sums, outs = refs[: len(refs) - (1 if last else 2)], refs[-1 if last else -2 :]
    width = far_here.shape[1]
    tile = math.gcd(width, 1024)
    gate, up = (ref[...] for ref in sums) if sums else (0.0, 0.0)
    for first in range(0, width, tile):
        here, there = slice(first, first + tile), slice(start + first, start + first + tile)
        rows = jnp.concatenate([near_here[:, there], far_here[:, here], near_there[:, there], far_there[:, here]])
        gate = gate + jnp.dot(rows, gate_ref[there, :], preferred_element_type=jnp.float32)
        up = up + jnp.dot(rows, up_ref[there, :], preferred_element_type=jnp.float32)
    if last:
        outs[0][...] = (gate / (1.0 + jnp.exp(-gate)) * up).astype(jnp.bfloat16)
    else:
        outs[0][...], outs[1][...] = gate, up


def hidden_units(gate_w, up_w, near, spans):
    features, units = gate_w.shape
    count = 2 * (near[0].shape[0] + spans[0][0].shape[0])
    sums, start = (), 0
    for span in spans:
        width = span[0].shape[1]
        last = start + width == features
        total = jax.ShapeDtypeStruct((count, units), jnp.float32)
        sums = pl.pallas_call(
            functools.partial(hidden_kernel, start, last),
            out_shape=(jax.ShapeDtypeStruct((count, units), jnp.bfloat16),) if last else (total, total),
            in_specs=[vmem()] * (6 + len(sums)),
            out_specs=(vmem(),) * (1 if last else 2),
            cost_estimate=pl.CostEstimate(
                flops=4 * units * count * width, bytes_accessed=4 * units * width, transcendentals=0
            ),
            compiler_params=pltpu.CompilerParams(vmem_limit_bytes=24 << 20),
        )(gate_w, up_w, *near, *span, *sums)
        start += width
    return sums[0]


def down_kernel(hidden_ref, down_ref, *outs):
    features = down_ref.shape[1]
    tile = math.gcd(features, 512)
    for first in range(0, features, tile):
        here = slice(first, first + tile)
        part = jnp.dot(hidden_ref[...], down_ref[:, here], preferred_element_type=jnp.float32)
        row = 0
        for out in outs:
            out[:, here] = part[row : row + out.shape[0]].astype(out.dtype)
            row += out.shape[0]


def down(hidden, down_w, counts):
    units, features = down_w.shape
    return pl.pallas_call(
        down_kernel,
        out_shape=[jax.ShapeDtypeStruct((count, features), jnp.float32) for count in counts]
        + [jax.ShapeDtypeStruct((count, features), jnp.bfloat16) for count in counts],
        in_specs=[vmem()] * 2,
        out_specs=[vmem()] * (2 * len(counts)),
        cost_estimate=pl.CostEstimate(
            flops=2 * hidden.size * features, bytes_accessed=2 * units * features, transcendentals=0
        ),
        compiler_params=pltpu.CompilerParams(vmem_limit_bytes=24 << 20),
    )(hidden, down_w)


def signs_twice():
    index = jnp.arange(BLOCK, dtype=jnp.int32)
    common = index[:, None] & index[None, :]
    for shift in (4, 2, 1):
        common = common ^ (common >> shift)
    signs = (1 - 2 * (common & 1)).astype(jnp.bfloat16)
    return jnp.concatenate([signs, signs])


def rotate_kernel(count, *refs):
    total_ref, *arrived = refs[: count + 1]
    sign_ref, matrix_ref, out_ref, turned_ref, sems = refs[count + 1 :]
    rows, features = total_ref.shape
    scale = 1.0 / math.sqrt(BLOCK)
    width = features // PIECES
    copies = []
    for k in range(PIECES):
        here = slice(k * width, (k + 1) * width)
        value = total_ref[:, here]
        for piece in arrived:
            value = value + piece[:, here].astype(jnp.float32)
        value = value * sign_ref[:, here].astype(jnp.float32)
        value = jnp.concatenate([value[:, b : b + BLOCK] for b in range(0, width, BLOCK)])
        high = value.astype(jnp.bfloat16)
        low = (value - high.astype(jnp.float32)).astype(jnp.bfloat16)
        both = jnp.concatenate([high, low], axis=1)
        turned = jnp.dot(both, matrix_ref[...], preferred_element_type=jnp.float32) * scale
        for b in range(width // BLOCK):
            first = k * width + b * BLOCK
            turned_ref[:, first : first + BLOCK] = turned[b * rows : (b + 1) * rows].astype(jnp.bfloat16)
        copies.append(pltpu.make_async_copy(turned_ref.at[:, here], out_ref.at[:, here], sems.at[k]))
        copies[-1].start()
    for copy in copies:
        copy.wait()


def rotate(total, arrived, signs):
    return pl.pallas_call(
        functools.partial(rotate_kernel, len(arrived)),
        out_shape=jax.ShapeDtypeStruct(total.shape, jnp.bfloat16),
        in_specs=[vmem()] * (len(arrived) + 3),
        out_specs=pl.BlockSpec(memory_space=pl.ANY),
        scratch_shapes=[pltpu.VMEM(total.shape, jnp.bfloat16), pltpu.SemaphoreType.DMA((PIECES,))],
        compiler_params=pltpu.CompilerParams(vmem_limit_bytes=16 << 20),
    )(total, *arrived, signs.reshape(1, -1), signs_twice())


def solution(mesh):
    members = mesh.shape["gx"]
    assert members & (members - 1) == 0 and members >= 16

    square = ((4, 2), (2, 4), (6, 6))
    far = []
    mask = members // 2
    while mask > 8:
        far.append((mask, mask))
        mask //= 2
    far.append((12, 8))
    others = members // 8 - 1

    def swap(value, masks):
        return lax.ppermute(value, "gx", [(i, i ^ masks[i % 2]) for i in range(members)])

    def swap_far(value, masks):
        firsts = range(0, mesh.shape["groups"] * members, members)
        pairs = [(g + i, g + (i ^ masks[g // members % 2])) for g in firsts for i in range(members)]
        return lax.ppermute(value, ("groups", "gx"), pairs)

    def on_device(tokens, gate_weight, up_weight, down_weight, sign_pattern):
        rows, features = tokens.shape

        away = []
        for masks in far:
            away.append(swap_far(jnp.concatenate([tokens] + away), masks))
        away = jnp.concatenate(away)
        near = [swap(tokens, m) for m in square]
        away, sign_pattern = lax.optimization_barrier((away, sign_pattern))
        there = [swap(away, m) for m in square[:2]]
        away, near[0] = lax.optimization_barrier((away, near[0]))
        there.append(swap(away, square[2]))
        gate_w, up_w, down_w = load(gate_weight.T, up_weight.T, down_weight, away)
        there[0], *near = lax.optimization_barrier((there[0], *near))
        near = jnp.concatenate([tokens, near[1], near[0], near[2]])
        near_there = swap(near, (1, 1))
        gate_w, up_w, near, *there[1:] = lax.optimization_barrier((gate_w, up_w, near, *there[1:]))
        far_rows = [there[2], away, *there[:2]]
        spans = []
        width = features // SPANS
        for k in range(SPANS):
            span = jnp.concatenate([piece[:, k * width : (k + 1) * width] for piece in far_rows])
            spans.append((span, swap(span, (1, 1))))
        hidden = hidden_units(gate_w, up_w, (near, near_there), spans)

        count = others * rows
        own, diagonal, rest, *sends = down(hidden, down_w, (4 * rows, count, 3 * count))
        diagonal = diagonal + swap(sends[1], (1, 1)).astype(jnp.float32)
        diagonal = swap(diagonal.astype(jnp.bfloat16), square[2])
        rest_there, sends[0] = lax.optimization_barrier((swap(sends[2], (1, 1)), sends[0]))
        rest = rest + rest_there.astype(jnp.float32)
        leave = rest[count:].astype(jnp.bfloat16)
        total = rest[:count]
        for piece in (diagonal, swap(leave[:count], square[0]), swap(leave[count:], square[1])):
            total = total + piece.astype(jnp.float32)
        arrived = []
        for masks in reversed(far):
            split = total.shape[0] // 2 // rows * rows
            piece = swap_far(total[split:].astype(jnp.bfloat16), masks)
            arrived.append(piece[:rows])
            total = total[:split] + piece[rows:].astype(jnp.float32)

        own = own + swap(sends[0], (1, 1)).astype(jnp.float32)
        own = own[: 2 * rows] + swap(own[2 * rows :].astype(jnp.bfloat16), square[0]).astype(jnp.float32)
        arrived.append(swap(own[rows:].astype(jnp.bfloat16), square[1]))
        return rotate(own[:rows], arrived, sign_pattern)

    placed = (P(("groups", "gx"), None), P(None, "gx"), P(None, "gx"), P("gx", None), P())
    return jax.shard_map(
        on_device, mesh=mesh, in_specs=placed, out_specs=P(("groups", "gx"), None), check_vma=False
    )
```

```python
import functools
import math

import jax
import jax.numpy as jnp
from jax import lax
from jax.experimental import pallas as pl
from jax.experimental.pallas import tpu as pltpu
from jax.sharding import PartitionSpec as P

BLOCK = 128
SPANS = 2
TURNS = 8
NT = (((1,), (1,)), ((), ()))


def vmem():
    return pl.BlockSpec(memory_space=pltpu.VMEM)


def load_kernel(gate_hbm, up_hbm, down_hbm, _, gate_ref, up_ref, down_ref, staged, sems, down_sem):
    tile = staged.shape[2] // sems.shape[1]
    copies = []
    for k in range(sems.shape[1]):
        here = slice(k * tile, (k + 1) * tile)
        for j, source in enumerate((gate_hbm, up_hbm)):
            copies.append(
                pltpu.make_async_copy(source.at[:, here], staged.at[j, :, here], sems.at[j, k])
            )
            copies[-1].start()
    down_copy = pltpu.make_async_copy(down_hbm, down_ref, down_sem)
    down_copy.start()
    for k in range(sems.shape[1]):
        here = slice(k * tile, (k + 1) * tile)
        for j, out in enumerate((gate_ref, up_ref)):
            copies[2 * k + j].wait()
            out[here, :] = staged[j, :, here].T
    down_copy.wait()


def load(gate_w, up_w, down_w, after):
    units, features = gate_w.shape
    shape = jax.ShapeDtypeStruct((features, units), gate_w.dtype)
    return pl.pallas_call(
        load_kernel,
        out_shape=(shape, shape, jax.ShapeDtypeStruct(down_w.shape, down_w.dtype)),
        in_specs=[pl.BlockSpec(memory_space=pltpu.HBM)] * 3 + [pl.BlockSpec(memory_space=pl.ANY)],
        out_specs=(vmem(),) * 3,
        scratch_shapes=[
            pltpu.VMEM((2, units, features), gate_w.dtype),
            pltpu.SemaphoreType.DMA((2, TURNS)),
            pltpu.SemaphoreType.DMA,
        ],
        cost_estimate=pl.CostEstimate(flops=0, bytes_accessed=6 * units * features, transcendentals=0),
        compiler_params=pltpu.CompilerParams(vmem_limit_bytes=24 << 20),
    )(*(pltpu.with_memory_space_constraint(w, pltpu.HBM) for w in (gate_w, up_w, down_w)), after)


def hidden_kernel(start, last, *refs):
    gate_ref, up_ref, near_here, near_there, far_here, far_there, *refs = refs
    sums, outs = refs[: len(refs) - (1 if last else 2)], refs[-1 if last else -2 :]
    width = far_here.shape[1]
    tile = math.gcd(width, 1024)
    gate, up = (ref[...] for ref in sums) if sums else (0.0, 0.0)
    for first in range(0, width, tile):
        here, there = slice(first, first + tile), slice(start + first, start + first + tile)
        rows = jnp.concatenate([near_here[:, there], far_here[:, here], near_there[:, there], far_there[:, here]])
        gate = gate + jnp.dot(rows, gate_ref[there, :], preferred_element_type=jnp.float32)
        up = up + jnp.dot(rows, up_ref[there, :], preferred_element_type=jnp.float32)
    if last:
        outs[0][...] = (gate / (1.0 + jnp.exp(-gate)) * up).astype(jnp.bfloat16)
    else:
        outs[0][...], outs[1][...] = gate, up


def hidden_units(gate_w, up_w, near, spans):
    features, units = gate_w.shape
    count = 2 * (near[0].shape[0] + spans[0][0].shape[0])
    sums, start = (), 0
    for span in spans:
        width = span[0].shape[1]
        last = start + width == features
        total = jax.ShapeDtypeStruct((count, units), jnp.float32)
        sums = pl.pallas_call(
            functools.partial(hidden_kernel, start, last),
            out_shape=(jax.ShapeDtypeStruct((count, units), jnp.bfloat16),) if last else (total, total),
            in_specs=[vmem()] * (6 + len(sums)),
            out_specs=(vmem(),) * (1 if last else 2),
            cost_estimate=pl.CostEstimate(
                flops=4 * units * count * width, bytes_accessed=4 * units * width, transcendentals=0
            ),
            compiler_params=pltpu.CompilerParams(vmem_limit_bytes=24 << 20),
        )(gate_w, up_w, *near, *span, *sums)
        start += width
    return sums[0]


def down_kernel(spans, hidden_ref, down_ref, *outs):
    half, features = hidden_ref.shape[0] // 2, down_ref.shape[1]
    tile = math.gcd(features, 512)
    for first in range(0, features, tile):
        here = slice(first, first + tile)
        part = jnp.dot(hidden_ref[...], down_ref[:, here], preferred_element_type=jnp.float32)
        for k, out in enumerate(outs):
            begin = 0 if k < len(spans) else half
            rows = [part[begin + first : begin + last] for first, last in spans[k % len(spans)]]
            out[:, here] = jnp.concatenate(rows).astype(out.dtype)


def down(hidden, down_w, spans):
    units, features = down_w.shape
    counts = [sum(last - first for first, last in span) for span in spans]
    return pl.pallas_call(
        functools.partial(down_kernel, spans),
        out_shape=[jax.ShapeDtypeStruct((count, features), jnp.float32) for count in counts]
        + [jax.ShapeDtypeStruct((count, features), jnp.bfloat16) for count in counts],
        in_specs=[vmem()] * 2,
        out_specs=[vmem()] * (2 * len(counts)),
        cost_estimate=pl.CostEstimate(
            flops=2 * hidden.size * features, bytes_accessed=2 * units * features, transcendentals=0
        ),
        compiler_params=pltpu.CompilerParams(vmem_limit_bytes=24 << 20),
    )(hidden, down_w)


def signs_twice():
    index = jnp.arange(BLOCK, dtype=jnp.int32)
    common = index[:, None] & index[None, :]
    for shift in (4, 2, 1):
        common = common ^ (common >> shift)
    signs = (1 - 2 * (common & 1)).astype(jnp.bfloat16)
    return jnp.concatenate([signs, signs])


def rotate_kernel(count, *refs):
    total_ref, *arrived = refs[: count + 1]
    sign_ref, matrix_ref, out_ref = refs[count + 1 :]
    rows, features = total_ref.shape
    value = total_ref[...]
    for piece in arrived:
        value = value + piece[...].astype(jnp.float32)
    value = value * sign_ref[...].astype(jnp.float32)
    value = jnp.concatenate([value[:, b : b + BLOCK] for b in range(0, features, BLOCK)])
    high = value.astype(jnp.bfloat16)
    low = (value - high.astype(jnp.float32)).astype(jnp.bfloat16)
    both = jnp.concatenate([high, low], axis=1)
    turned = jnp.dot(both, matrix_ref[...], preferred_element_type=jnp.float32) * (1.0 / math.sqrt(BLOCK))
    for b in range(features // BLOCK):
        out_ref[:, b * BLOCK : (b + 1) * BLOCK] = turned[b * rows : (b + 1) * rows].astype(jnp.bfloat16)


def rotate(total, arrived, signs):
    return pl.pallas_call(
        functools.partial(rotate_kernel, len(arrived)),
        out_shape=jax.ShapeDtypeStruct(total.shape, jnp.bfloat16),
        in_specs=[vmem()] * (len(arrived) + 3),
        out_specs=vmem(),
        compiler_params=pltpu.CompilerParams(vmem_limit_bytes=16 << 20),
    )(total, *arrived, signs.reshape(1, -1), signs_twice())


def solution(mesh):
    members = mesh.shape["gx"]
    assert members & (members - 1) == 0 and members >= 16

    square = ((4, 2), (2, 4), (6, 6))
    far = []
    mask = members // 2
    while mask > 4:
        far.append((mask, mask))
        mask //= 2
    others = members // 8 - 1

    def swap(value, masks):
        return lax.ppermute(value, "gx", [(i, i ^ masks[i % 2]) for i in range(members)])

    def on_device(tokens, gate_weight, up_weight, down_weight, sign_pattern):
        rows, features = tokens.shape

        away = []
        for masks in far:
            away.append(swap(jnp.concatenate([tokens] + away), masks))
        away = jnp.concatenate(away)
        near = [swap(tokens, m) for m in square]
        away, sign_pattern = lax.optimization_barrier((away, sign_pattern))
        there = [swap(away, m) for m in square[:2]]
        away, near[0] = lax.optimization_barrier((away, near[0]))
        there.append(swap(away, square[2]))
        gate_w, up_w, down_w = load(gate_weight.T, up_weight.T, down_weight, away)
        there[0], *near = lax.optimization_barrier((there[0], *near))
        early = jnp.concatenate([tokens, near[1], near[0], near[2], away, there[0]])
        early_there = swap(early, (1, 1))
        gate_w, up_w, early, *there[1:] = lax.optimization_barrier((gate_w, up_w, early, *there[1:]))
        spans = []
        width = features // SPANS
        for k in range(SPANS):
            span = jnp.concatenate([piece[:, k * width : (k + 1) * width] for piece in there[:0:-1]])
            spans.append((span, swap(span, (1, 1))))
        hidden = hidden_units(gate_w, up_w, (early, early_there), spans)

        count = others * rows
        ends = [4 * rows + k * count for k in range(5)]
        own, diagonal, rest, *sends = down(
            hidden,
            down_w,
            (((0, ends[0]),), ((ends[2], ends[3]),), ((ends[0], ends[2]), (ends[3], ends[4]))),
        )
        diagonal = diagonal + swap(sends[1], (1, 1)).astype(jnp.float32)
        diagonal = swap(diagonal.astype(jnp.bfloat16), square[2])
        rest_there, sends[0] = lax.optimization_barrier((swap(sends[2], (1, 1)), sends[0]))
        rest = rest + rest_there.astype(jnp.float32)
        leave = rest[count:].astype(jnp.bfloat16)
        total = rest[:count]
        for piece in (diagonal, swap(leave[:count], square[0]), swap(leave[count:], square[1])):
            total = total + piece.astype(jnp.float32)
        arrived = []
        for masks in reversed(far):
            split = total.shape[0] // 2 // rows * rows
            piece = swap(total[split:].astype(jnp.bfloat16), masks)
            arrived.append(piece[:rows])
            total = total[:split] + piece[rows:].astype(jnp.float32)

        own = own + swap(sends[0], (1, 1)).astype(jnp.float32)
        own = own[: 2 * rows] + swap(own[2 * rows :].astype(jnp.bfloat16), square[0]).astype(jnp.float32)
        arrived.append(swap(own[rows:].astype(jnp.bfloat16), square[1]))
        return rotate(own[:rows], arrived, sign_pattern)

    placed = (P(("groups", "gx"), None), P(None, "gx"), P(None, "gx"), P("gx", None), P())
    return jax.shard_map(
        on_device, mesh=mesh, in_specs=placed, out_specs=P(("groups", "gx"), None), check_vma=False
    )
```

```python
import functools
import math

import jax
import jax.numpy as jnp
from jax import lax
from jax.experimental import pallas as pl
from jax.experimental.pallas import tpu as pltpu
from jax.sharding import PartitionSpec as P

BLOCK = 128
PARTS = (9, 7)
SPANS = 2
TURNS = 8
NT = (((1,), (1,)), ((), ()))


def vmem():
    return pl.BlockSpec(memory_space=pltpu.VMEM)


def load_kernel(gate_hbm, up_hbm, down_hbm, _, gate_ref, up_ref, down_ref, staged, sems, down_sem):
    tile = staged.shape[2] // sems.shape[1]
    copies = []
    for k in range(sems.shape[1]):
        here = slice(k * tile, (k + 1) * tile)
        for j, source in enumerate((gate_hbm, up_hbm)):
            copies.append(
                pltpu.make_async_copy(source.at[:, here], staged.at[j, :, here], sems.at[j, k])
            )
            copies[-1].start()
    down_copy = pltpu.make_async_copy(down_hbm, down_ref, down_sem)
    down_copy.start()
    for k in range(sems.shape[1]):
        here = slice(k * tile, (k + 1) * tile)
        for j, out in enumerate((gate_ref, up_ref)):
            copies[2 * k + j].wait()
            out[here, :] = staged[j, :, here].T
    down_copy.wait()


def load(gate_w, up_w, down_w, after):
    units, features = gate_w.shape
    shape = jax.ShapeDtypeStruct((features, units), gate_w.dtype)
    return pl.pallas_call(
        load_kernel,
        out_shape=(shape, shape, jax.ShapeDtypeStruct(down_w.shape, down_w.dtype)),
        in_specs=[pl.BlockSpec(memory_space=pltpu.HBM)] * 3 + [pl.BlockSpec(memory_space=pl.ANY)],
        out_specs=(vmem(),) * 3,
        scratch_shapes=[
            pltpu.VMEM((2, units, features), gate_w.dtype),
            pltpu.SemaphoreType.DMA((2, TURNS)),
            pltpu.SemaphoreType.DMA,
        ],
        cost_estimate=pl.CostEstimate(flops=0, bytes_accessed=6 * units * features, transcendentals=0),
        compiler_params=pltpu.CompilerParams(vmem_limit_bytes=24 << 20),
    )(*(pltpu.with_memory_space_constraint(w, pltpu.HBM) for w in (gate_w, up_w, down_w)), after)


def hidden_kernel(start, last, *refs):
    gate_ref, up_ref, near_here, near_there, far_here, far_there, *refs = refs
    sums, outs = refs[: len(refs) - (1 if last else 2)], refs[-1 if last else -2 :]
    width = far_here.shape[1]
    tile = math.gcd(width, 1024)
    gate, up = (ref[...] for ref in sums) if sums else (0.0, 0.0)
    for first in range(0, width, tile):
        here, there = slice(first, first + tile), slice(start + first, start + first + tile)
        rows = jnp.concatenate([near_here[:, there], far_here[:, here], near_there[:, there], far_there[:, here]])
        gate = gate + jnp.dot(rows, gate_ref[there, :], preferred_element_type=jnp.float32)
        up = up + jnp.dot(rows, up_ref[there, :], preferred_element_type=jnp.float32)
    if last:
        outs[0][...] = (gate / (1.0 + jnp.exp(-gate)) * up).astype(jnp.bfloat16)
    else:
        outs[0][...], outs[1][...] = gate, up


def hidden_units(gate_w, up_w, near, spans):
    features, units = gate_w.shape
    count = 2 * (near[0].shape[0] + spans[0][0].shape[0])
    sums, start = (), 0
    for span in spans:
        width = span[0].shape[1]
        last = start + width == features
        total = jax.ShapeDtypeStruct((count, units), jnp.float32)
        sums = pl.pallas_call(
            functools.partial(hidden_kernel, start, last),
            out_shape=(jax.ShapeDtypeStruct((count, units), jnp.bfloat16),) if last else (total, total),
            in_specs=[vmem()] * (6 + len(sums)),
            out_specs=(vmem(),) * (1 if last else 2),
            cost_estimate=pl.CostEstimate(
                flops=4 * units * count * width, bytes_accessed=4 * units * width, transcendentals=0
            ),
            compiler_params=pltpu.CompilerParams(vmem_limit_bytes=24 << 20),
        )(gate_w, up_w, *near, *span, *sums)
        start += width
    return sums[0]


def down_kernel(hidden_ref, down_ref, *outs):
    features = down_ref.shape[1]
    tile = math.gcd(features, 512)
    for first in range(0, features, tile):
        here = slice(first, first + tile)
        part = jnp.dot(hidden_ref[...], down_ref[:, here], preferred_element_type=jnp.float32)
        row = 0
        for out in outs:
            out[:, here] = part[row : row + out.shape[0]].astype(out.dtype)
            row += out.shape[0]


def down(hidden, down_w, counts):
    units, features = down_w.shape
    return pl.pallas_call(
        down_kernel,
        out_shape=[jax.ShapeDtypeStruct((count, features), jnp.float32) for count in counts]
        + [jax.ShapeDtypeStruct((count, features), jnp.bfloat16) for count in counts],
        in_specs=[vmem()] * 2,
        out_specs=[vmem()] * (2 * len(counts)),
        cost_estimate=pl.CostEstimate(
            flops=2 * hidden.size * features, bytes_accessed=2 * units * features, transcendentals=0
        ),
        compiler_params=pltpu.CompilerParams(vmem_limit_bytes=24 << 20),
    )(hidden, down_w)


def signs_twice():
    index = jnp.arange(BLOCK, dtype=jnp.int32)
    common = index[:, None] & index[None, :]
    for shift in (4, 2, 1):
        common = common ^ (common >> shift)
    signs = (1 - 2 * (common & 1)).astype(jnp.bfloat16)
    return jnp.concatenate([signs, signs])


def rotate_kernel(counts, *refs):
    total_ref, *refs = refs
    value = total_ref[...]
    rows, features = value.shape
    for count in counts:
        parts, refs = refs[:count], refs[count:]
        value = value + jnp.concatenate([part[...] for part in parts], axis=1).astype(jnp.float32)
    sign_ref, matrix_ref, out_ref = refs
    value = value * sign_ref[...].astype(jnp.float32)
    value = jnp.concatenate([value[:, b : b + BLOCK] for b in range(0, features, BLOCK)])
    high = value.astype(jnp.bfloat16)
    low = (value - high.astype(jnp.float32)).astype(jnp.bfloat16)
    both = jnp.concatenate([high, low], axis=1)
    turned = jnp.dot(both, matrix_ref[...], preferred_element_type=jnp.float32) * (1.0 / math.sqrt(BLOCK))
    for b in range(features // BLOCK):
        out_ref[:, b * BLOCK : (b + 1) * BLOCK] = turned[b * rows : (b + 1) * rows].astype(jnp.bfloat16)


def rotate(total, arrived, signs):
    pieces = [piece for parts in arrived for piece in parts]
    return pl.pallas_call(
        functools.partial(rotate_kernel, [len(parts) for parts in arrived]),
        out_shape=jax.ShapeDtypeStruct(total.shape, jnp.bfloat16),
        in_specs=[vmem()] * (len(pieces) + 3),
        out_specs=vmem(),
        compiler_params=pltpu.CompilerParams(vmem_limit_bytes=16 << 20),
    )(total, *pieces, signs.reshape(1, -1), signs_twice())


def solution(mesh):
    members = mesh.shape["gx"]
    assert members & (members - 1) == 0 and members >= 16

    square = ((4, 2), (2, 4), (6, 6))
    far = []
    mask = members // 2
    while mask > 4:
        far.append((mask, mask))
        mask //= 2
    others = members // 8 - 1

    def swap(value, masks):
        return lax.ppermute(value, "gx", [(i, i ^ masks[i % 2]) for i in range(members)])

    def on_device(tokens, gate_weight, up_weight, down_weight, sign_pattern):
        rows, features = tokens.shape

        away = []
        for masks in far:
            away.append(swap(jnp.concatenate([tokens] + away), masks))
        away = jnp.concatenate(away)
        near = [swap(tokens, m) for m in square]
        away, sign_pattern = lax.optimization_barrier((away, sign_pattern))
        there = [swap(away, m) for m in square[:2]]
        away, near[0] = lax.optimization_barrier((away, near[0]))
        there.append(swap(away, square[2]))
        gate_w, up_w, down_w = load(gate_weight.T, up_weight.T, down_weight, away)
        there[0], *near = lax.optimization_barrier((there[0], *near))
        near = jnp.concatenate([tokens, near[1], near[0], near[2]])
        near_there = swap(near, (1, 1))
        gate_w, up_w, near, *there[1:] = lax.optimization_barrier((gate_w, up_w, near, *there[1:]))
        far_rows = [there[2], away, *there[:2]]
        spans = []
        width = features // SPANS
        for k in range(SPANS):
            span = jnp.concatenate([piece[:, k * width : (k + 1) * width] for piece in far_rows])
            spans.append((span, swap(span, (1, 1))))
        hidden = hidden_units(gate_w, up_w, (near, near_there), spans)

        count = others * rows
        own, diagonal, rest, *sends = down(hidden, down_w, (4 * rows, count, 3 * count))
        diagonal = diagonal + swap(sends[1], (1, 1)).astype(jnp.float32)
        diagonal = diagonal.astype(jnp.bfloat16)
        rest_there, sends[0] = lax.optimization_barrier((swap(sends[2], (1, 1)), sends[0]))
        rest = rest + rest_there.astype(jnp.float32)
        leave = rest[count:].astype(jnp.bfloat16)

        arrived, start = [], 0
        for share in PARTS:
            part = slice(start, start + features * share // sum(PARTS))
            start = part.stop
            total = rest[:count, part]
            for masks, piece in zip(square[::-1], (diagonal, leave[count:], leave[:count])):
                total = total + swap(piece[:, part], masks).astype(jnp.float32)
            arrived.append([])
            for masks in reversed(far):
                split = total.shape[0] // 2 // rows * rows
                piece = swap(total[split:].astype(jnp.bfloat16), masks)
                arrived[-1].append(piece[:rows])
                total = total[:split] + piece[rows:].astype(jnp.float32)
        arrived = list(zip(*arrived))

        own = own + swap(sends[0], (1, 1)).astype(jnp.float32)
        own = own[: 2 * rows] + swap(own[2 * rows :].astype(jnp.bfloat16), square[0]).astype(jnp.float32)
        arrived.append([swap(own[rows:].astype(jnp.bfloat16), square[1])])
        return rotate(own[:rows], arrived, sign_pattern)

    placed = (P(("groups", "gx"), None), P(None, "gx"), P(None, "gx"), P("gx", None), P())
    return jax.shard_map(
        on_device, mesh=mesh, in_specs=placed, out_specs=P(("groups", "gx"), None), check_vma=False
    )
```

```python
import functools
import math

import jax
import jax.numpy as jnp
from jax import lax
from jax.experimental import pallas as pl
from jax.experimental.pallas import tpu as pltpu
from jax.sharding import PartitionSpec as P

BLOCK = 128
SPANS = 2
TURNS = 8
NT = (((1,), (1,)), ((), ()))


def vmem():
    return pl.BlockSpec(memory_space=pltpu.VMEM)


def load_kernel(gate_hbm, up_hbm, down_hbm, _, gate_ref, up_ref, down_ref, staged, sems, down_sem):
    tile = staged.shape[2] // sems.shape[1]
    copies = []
    for k in range(sems.shape[1]):
        here = slice(k * tile, (k + 1) * tile)
        for j, source in enumerate((gate_hbm, up_hbm)):
            copies.append(
                pltpu.make_async_copy(source.at[:, here], staged.at[j, :, here], sems.at[j, k])
            )
            copies[-1].start()
    down_copy = pltpu.make_async_copy(down_hbm, down_ref, down_sem)
    down_copy.start()
    for k in range(sems.shape[1]):
        here = slice(k * tile, (k + 1) * tile)
        for j, out in enumerate((gate_ref, up_ref)):
            copies[2 * k + j].wait()
            out[here, :] = staged[j, :, here].T
    down_copy.wait()


def load(gate_w, up_w, down_w, after):
    units, features = gate_w.shape
    shape = jax.ShapeDtypeStruct((features, units), gate_w.dtype)
    return pl.pallas_call(
        load_kernel,
        out_shape=(shape, shape, jax.ShapeDtypeStruct(down_w.shape, down_w.dtype)),
        in_specs=[pl.BlockSpec(memory_space=pltpu.HBM)] * 3 + [pl.BlockSpec(memory_space=pl.ANY)],
        out_specs=(vmem(),) * 3,
        scratch_shapes=[
            pltpu.VMEM((2, units, features), gate_w.dtype),
            pltpu.SemaphoreType.DMA((2, TURNS)),
            pltpu.SemaphoreType.DMA,
        ],
        cost_estimate=pl.CostEstimate(flops=0, bytes_accessed=6 * units * features, transcendentals=0),
        compiler_params=pltpu.CompilerParams(vmem_limit_bytes=24 << 20),
    )(*(pltpu.with_memory_space_constraint(w, pltpu.HBM) for w in (gate_w, up_w, down_w)), after)


def hidden_kernel(start, last, *refs):
    gate_ref, up_ref, near_here, near_there, far_here, far_there, *refs = refs
    sums, outs = refs[: len(refs) - (1 if last else 2)], refs[-1 if last else -2 :]
    width = far_here.shape[1]
    tile = math.gcd(width, 1024)
    gate, up = (ref[...] for ref in sums) if sums else (0.0, 0.0)
    for first in range(0, width, tile):
        here, there = slice(first, first + tile), slice(start + first, start + first + tile)
        rows = jnp.concatenate([near_here[:, there], far_here[:, here], near_there[:, there], far_there[:, here]])
        gate = gate + jnp.dot(rows, gate_ref[there, :], preferred_element_type=jnp.float32)
        up = up + jnp.dot(rows, up_ref[there, :], preferred_element_type=jnp.float32)
    if last:
        outs[0][...] = (gate / (1.0 + jnp.exp(-gate)) * up).astype(jnp.bfloat16)
    else:
        outs[0][...], outs[1][...] = gate, up


def hidden_units(gate_w, up_w, near, spans):
    features, units = gate_w.shape
    count = 2 * (near[0].shape[0] + spans[0][0].shape[0])
    sums, start = (), 0
    for span in spans:
        width = span[0].shape[1]
        last = start + width == features
        total = jax.ShapeDtypeStruct((count, units), jnp.float32)
        sums = pl.pallas_call(
            functools.partial(hidden_kernel, start, last),
            out_shape=(jax.ShapeDtypeStruct((count, units), jnp.bfloat16),) if last else (total, total),
            in_specs=[vmem()] * (6 + len(sums)),
            out_specs=(vmem(),) * (1 if last else 2),
            cost_estimate=pl.CostEstimate(
                flops=4 * units * count * width, bytes_accessed=4 * units * width, transcendentals=0
            ),
            compiler_params=pltpu.CompilerParams(vmem_limit_bytes=24 << 20),
        )(gate_w, up_w, *near, *span, *sums)
        start += width
    return sums[0]


def down_kernel(spans, hidden_ref, down_ref, *outs):
    half, features = hidden_ref.shape[0] // 2, down_ref.shape[1]
    tile = math.gcd(features, 512)
    for first in range(0, features, tile):
        here = slice(first, first + tile)
        part = jnp.dot(hidden_ref[...], down_ref[:, here], preferred_element_type=jnp.float32)
        for k, out in enumerate(outs):
            begin = 0 if k < len(spans) else half
            rows = [part[begin + first : begin + last] for first, last in spans[k % len(spans)]]
            out[:, here] = jnp.concatenate(rows).astype(out.dtype)


def down(hidden, down_w, spans):
    units, features = down_w.shape
    counts = [sum(last - first for first, last in span) for span in spans]
    return pl.pallas_call(
        functools.partial(down_kernel, spans),
        out_shape=[jax.ShapeDtypeStruct((count, features), jnp.float32) for count in counts]
        + [jax.ShapeDtypeStruct((count, features), jnp.bfloat16) for count in counts],
        in_specs=[vmem()] * 2,
        out_specs=[vmem()] * (2 * len(counts)),
        cost_estimate=pl.CostEstimate(
            flops=2 * hidden.size * features, bytes_accessed=2 * units * features, transcendentals=0
        ),
        compiler_params=pltpu.CompilerParams(vmem_limit_bytes=24 << 20),
    )(hidden, down_w)


def signs_twice():
    index = jnp.arange(BLOCK, dtype=jnp.int32)
    common = index[:, None] & index[None, :]
    for shift in (4, 2, 1):
        common = common ^ (common >> shift)
    signs = (1 - 2 * (common & 1)).astype(jnp.bfloat16)
    return jnp.concatenate([signs, signs])


def rotate_kernel(count, *refs):
    total_ref, *arrived = refs[: count + 1]
    sign_ref, matrix_ref, out_ref = refs[count + 1 :]
    rows, features = total_ref.shape
    value = total_ref[...]
    for piece in arrived:
        value = value + piece[...].astype(jnp.float32)
    value = value * sign_ref[...].astype(jnp.float32)
    value = jnp.concatenate([value[:, b : b + BLOCK] for b in range(0, features, BLOCK)])
    high = value.astype(jnp.bfloat16)
    low = (value - high.astype(jnp.float32)).astype(jnp.bfloat16)
    both = jnp.concatenate([high, low], axis=1)
    turned = jnp.dot(both, matrix_ref[...], preferred_element_type=jnp.float32) * (1.0 / math.sqrt(BLOCK))
    for b in range(features // BLOCK):
        out_ref[:, b * BLOCK : (b + 1) * BLOCK] = turned[b * rows : (b + 1) * rows].astype(jnp.bfloat16)


def rotate(total, arrived, signs):
    return pl.pallas_call(
        functools.partial(rotate_kernel, len(arrived)),
        out_shape=jax.ShapeDtypeStruct(total.shape, jnp.bfloat16),
        in_specs=[vmem()] * (len(arrived) + 3),
        out_specs=vmem(),
        compiler_params=pltpu.CompilerParams(vmem_limit_bytes=16 << 20),
    )(total, *arrived, signs.reshape(1, -1), signs_twice())


def solution(mesh):
    members = mesh.shape["gx"]
    assert members & (members - 1) == 0 and members >= 16

    square = ((4, 2), (2, 4), (6, 6))
    far = []
    mask = members // 2
    while mask > 4:
        far.append((mask, mask))
        mask //= 2
    others = members // 8 - 1

    def swap(value, masks):
        return lax.ppermute(value, "gx", [(i, i ^ masks[i % 2]) for i in range(members)])

    def on_device(tokens, gate_weight, up_weight, down_weight, sign_pattern):
        rows, features = tokens.shape

        away = []
        for masks in far:
            away.append(swap(jnp.concatenate([tokens] + away), masks))
        away = jnp.concatenate(away)
        near = [swap(tokens, m) for m in square]
        away, sign_pattern = lax.optimization_barrier((away, sign_pattern))
        there = [swap(away, m) for m in square[:2]]
        away, near[0] = lax.optimization_barrier((away, near[0]))
        there.append(swap(away, square[2]))
        gate_w, up_w, down_w = load(gate_weight.T, up_weight.T, down_weight, away)
        there[0], *near = lax.optimization_barrier((there[0], *near))
        early = jnp.concatenate([near[1], near[0], near[2], away, there[0], tokens])
        early_there = swap(early, (1, 1))
        gate_w, up_w, early, *there[1:] = lax.optimization_barrier((gate_w, up_w, early, *there[1:]))
        spans = []
        width = features // SPANS
        for k in range(SPANS):
            span = jnp.concatenate([piece[:, k * width : (k + 1) * width] for piece in there[:0:-1]])
            spans.append((span, swap(span, (1, 1))))
        hidden = hidden_units(gate_w, up_w, (early, early_there), spans)

        count = others * rows
        ends = [3 * rows, 3 * rows + count, 3 * rows + 2 * count, 4 * rows + 2 * count]
        ends += [ends[3] + count, ends[3] + 2 * count]
        own_rows = ((ends[2], ends[3]), (0, ends[0]))
        rest_rows = ((ends[0], ends[2]), (ends[4], ends[5]))
        own, diagonal, rest, *sends = down(hidden, down_w, (own_rows, ((ends[3], ends[4]),), rest_rows))
        diagonal = diagonal + swap(sends[1], (1, 1)).astype(jnp.float32)
        diagonal = swap(diagonal.astype(jnp.bfloat16), square[2])
        rest_there, sends[0] = lax.optimization_barrier((swap(sends[2], (1, 1)), sends[0]))
        rest = rest + rest_there.astype(jnp.float32)
        leave = rest[count:].astype(jnp.bfloat16)
        total = rest[:count]
        for piece in (diagonal, swap(leave[:count], square[0]), swap(leave[count:], square[1])):
            total = total + piece.astype(jnp.float32)
        arrived = []
        for masks in reversed(far):
            split = total.shape[0] // 2 // rows * rows
            piece = swap(total[split:].astype(jnp.bfloat16), masks)
            arrived.append(piece[:rows])
            total = total[:split] + piece[rows:].astype(jnp.float32)

        own = own + swap(sends[0], (1, 1)).astype(jnp.float32)
        own = own[: 2 * rows] + swap(own[2 * rows :].astype(jnp.bfloat16), square[0]).astype(jnp.float32)
        arrived.append(swap(own[rows:].astype(jnp.bfloat16), square[1]))
        return rotate(own[:rows], arrived, sign_pattern)

    placed = (P(("groups", "gx"), None), P(None, "gx"), P(None, "gx"), P("gx", None), P())
    return jax.shard_map(
        on_device, mesh=mesh, in_specs=placed, out_specs=P(("groups", "gx"), None), check_vma=False
    )
```

```python
import functools
import math

import jax
import jax.numpy as jnp
from jax import lax
from jax.experimental import pallas as pl
from jax.experimental.pallas import tpu as pltpu
from jax.sharding import PartitionSpec as P

BLOCK = 128
SPANS = 2
PARTS, ORDER = (9, 7), (0, 1)
TURNS = 8
NT = (((1,), (1,)), ((), ()))


def vmem():
    return pl.BlockSpec(memory_space=pltpu.VMEM)


def load_kernel(gate_hbm, up_hbm, down_hbm, _, gate_ref, up_ref, down_ref, staged, sems, down_sem):
    tile = staged.shape[2] // sems.shape[1]
    copies = []
    for k in range(sems.shape[1]):
        here = slice(k * tile, (k + 1) * tile)
        for j, source in enumerate((gate_hbm, up_hbm)):
            copies.append(
                pltpu.make_async_copy(source.at[:, here], staged.at[j, :, here], sems.at[j, k])
            )
            copies[-1].start()
    down_copy = pltpu.make_async_copy(down_hbm, down_ref, down_sem)
    down_copy.start()
    for k in range(sems.shape[1]):
        here = slice(k * tile, (k + 1) * tile)
        for j, out in enumerate((gate_ref, up_ref)):
            copies[2 * k + j].wait()
            out[here, :] = staged[j, :, here].T
    down_copy.wait()


def load(gate_w, up_w, down_w, after):
    units, features = gate_w.shape
    shape = jax.ShapeDtypeStruct((features, units), gate_w.dtype)
    return pl.pallas_call(
        load_kernel,
        out_shape=(shape, shape, jax.ShapeDtypeStruct(down_w.shape, down_w.dtype)),
        in_specs=[pl.BlockSpec(memory_space=pltpu.HBM)] * 3 + [pl.BlockSpec(memory_space=pl.ANY)],
        out_specs=(vmem(),) * 3,
        scratch_shapes=[
            pltpu.VMEM((2, units, features), gate_w.dtype),
            pltpu.SemaphoreType.DMA((2, TURNS)),
            pltpu.SemaphoreType.DMA,
        ],
        cost_estimate=pl.CostEstimate(flops=0, bytes_accessed=6 * units * features, transcendentals=0),
        compiler_params=pltpu.CompilerParams(vmem_limit_bytes=24 << 20),
    )(*(pltpu.with_memory_space_constraint(w, pltpu.HBM) for w in (gate_w, up_w, down_w)), after)


def hidden_kernel(start, last, *refs):
    gate_ref, up_ref, near_here, near_there, far_here, far_there, *refs = refs
    sums, outs = refs[: len(refs) - (1 if last else 2)], refs[-1 if last else -2 :]
    width = far_here.shape[1]
    tile = math.gcd(width, 1024)
    gate, up = (ref[...] for ref in sums) if sums else (0.0, 0.0)
    for first in range(0, width, tile):
        here, there = slice(first, first + tile), slice(start + first, start + first + tile)
        rows = jnp.concatenate([near_here[:, there], far_here[:, here], near_there[:, there], far_there[:, here]])
        gate = gate + jnp.dot(rows, gate_ref[there, :], preferred_element_type=jnp.float32)
        up = up + jnp.dot(rows, up_ref[there, :], preferred_element_type=jnp.float32)
    if last:
        outs[0][...] = (gate / (1.0 + jnp.exp(-gate)) * up).astype(jnp.bfloat16)
    else:
        outs[0][...], outs[1][...] = gate, up


def hidden_units(gate_w, up_w, near, spans):
    features, units = gate_w.shape
    count = 2 * (near[0].shape[0] + spans[0][0].shape[0])
    sums, start = (), 0
    for span in spans:
        width = span[0].shape[1]
        last = start + width == features
        total = jax.ShapeDtypeStruct((count, units), jnp.float32)
        sums = pl.pallas_call(
            functools.partial(hidden_kernel, start, last),
            out_shape=(jax.ShapeDtypeStruct((count, units), jnp.bfloat16),) if last else (total, total),
            in_specs=[vmem()] * (6 + len(sums)),
            out_specs=(vmem(),) * (1 if last else 2),
            cost_estimate=pl.CostEstimate(
                flops=4 * units * count * width, bytes_accessed=4 * units * width, transcendentals=0
            ),
            compiler_params=pltpu.CompilerParams(vmem_limit_bytes=24 << 20),
        )(gate_w, up_w, *near, *span, *sums)
        start += width
    return sums[0]


def down_kernel(spans, hidden_ref, down_ref, *outs):
    half, features = hidden_ref.shape[0] // 2, down_ref.shape[1]
    tile = math.gcd(features, 512)
    for first in range(0, features, tile):
        here = slice(first, first + tile)
        part = jnp.dot(hidden_ref[...], down_ref[:, here], preferred_element_type=jnp.float32)
        for k, out in enumerate(outs):
            begin = 0 if k < len(spans) else half
            rows = [part[begin + first : begin + last] for first, last in spans[k % len(spans)]]
            out[:, here] = jnp.concatenate(rows).astype(out.dtype)


def down(hidden, down_w, spans):
    units, features = down_w.shape
    counts = [sum(last - first for first, last in span) for span in spans]
    return pl.pallas_call(
        functools.partial(down_kernel, spans),
        out_shape=[jax.ShapeDtypeStruct((count, features), jnp.float32) for count in counts]
        + [jax.ShapeDtypeStruct((count, features), jnp.bfloat16) for count in counts],
        in_specs=[vmem()] * 2,
        out_specs=[vmem()] * (2 * len(counts)),
        cost_estimate=pl.CostEstimate(
            flops=2 * hidden.size * features, bytes_accessed=2 * units * features, transcendentals=0
        ),
        compiler_params=pltpu.CompilerParams(vmem_limit_bytes=24 << 20),
    )(hidden, down_w)


def signs_twice():
    index = jnp.arange(BLOCK, dtype=jnp.int32)
    common = index[:, None] & index[None, :]
    for shift in (4, 2, 1):
        common = common ^ (common >> shift)
    signs = (1 - 2 * (common & 1)).astype(jnp.bfloat16)
    return jnp.concatenate([signs, signs])


def rotate_kernel(counts, *refs):
    total_ref, *refs = refs
    value = total_ref[...]
    rows, features = value.shape
    for count in counts:
        parts, refs = refs[:count], refs[count:]
        value = value + jnp.concatenate([part[...] for part in parts], axis=1).astype(jnp.float32)
    sign_ref, matrix_ref, out_ref = refs
    value = value * sign_ref[...].astype(jnp.float32)
    value = jnp.concatenate([value[:, b : b + BLOCK] for b in range(0, features, BLOCK)])
    high = value.astype(jnp.bfloat16)
    low = (value - high.astype(jnp.float32)).astype(jnp.bfloat16)
    both = jnp.concatenate([high, low], axis=1)
    turned = jnp.dot(both, matrix_ref[...], preferred_element_type=jnp.float32) * (1.0 / math.sqrt(BLOCK))
    for b in range(features // BLOCK):
        out_ref[:, b * BLOCK : (b + 1) * BLOCK] = turned[b * rows : (b + 1) * rows].astype(jnp.bfloat16)


def rotate(total, arrived, signs):
    pieces = [piece for parts in arrived for piece in parts]
    return pl.pallas_call(
        functools.partial(rotate_kernel, [len(parts) for parts in arrived]),
        out_shape=jax.ShapeDtypeStruct(total.shape, jnp.bfloat16),
        in_specs=[vmem()] * (len(pieces) + 3),
        out_specs=vmem(),
        compiler_params=pltpu.CompilerParams(vmem_limit_bytes=16 << 20),
    )(total, *pieces, signs.reshape(1, -1), signs_twice())


def solution(mesh):
    members = mesh.shape["gx"]
    assert members & (members - 1) == 0 and members >= 16

    square = ((4, 2), (2, 4), (6, 6))
    far = []
    mask = members // 2
    while mask > 4:
        far.append((mask, mask))
        mask //= 2
    others = members // 8 - 1

    def swap(value, masks):
        return lax.ppermute(value, "gx", [(i, i ^ masks[i % 2]) for i in range(members)])

    def on_device(tokens, gate_weight, up_weight, down_weight, sign_pattern):
        rows, features = tokens.shape

        away = []
        for masks in far:
            away.append(swap(jnp.concatenate([tokens] + away), masks))
        away = jnp.concatenate(away)
        near = [swap(tokens, m) for m in square]
        away, sign_pattern = lax.optimization_barrier((away, sign_pattern))
        there = [swap(away, m) for m in square[:2]]
        away, near[0] = lax.optimization_barrier((away, near[0]))
        there.append(swap(away, square[2]))
        gate_w, up_w, down_w = load(gate_weight.T, up_weight.T, down_weight, away)
        there[0], *near = lax.optimization_barrier((there[0], *near))
        early = jnp.concatenate([near[1], near[0], near[2], away, there[0], tokens])
        early_there = swap(early, (1, 1))
        gate_w, up_w, early, *there[1:] = lax.optimization_barrier((gate_w, up_w, early, *there[1:]))
        spans = []
        width = features // SPANS
        for k in range(SPANS):
            span = jnp.concatenate([piece[:, k * width : (k + 1) * width] for piece in there[:0:-1]])
            spans.append((span, swap(span, (1, 1))))
        hidden = hidden_units(gate_w, up_w, (early, early_there), spans)

        count = others * rows
        ends = [3 * rows, 3 * rows + count, 3 * rows + 2 * count, 4 * rows + 2 * count]
        ends += [ends[3] + count, ends[3] + 2 * count]
        own_rows = ((ends[2], ends[3]), (0, ends[0]))
        rest_rows = ((ends[0], ends[2]), (ends[4], ends[5]))
        own, diagonal, rest, *sends = down(hidden, down_w, (own_rows, ((ends[3], ends[4]),), rest_rows))
        diagonal = diagonal + swap(sends[1], (1, 1)).astype(jnp.float32)
        diagonal = diagonal.astype(jnp.bfloat16)
        rest_there, sends[0] = lax.optimization_barrier((swap(sends[2], (1, 1)), sends[0]))
        rest = rest + rest_there.astype(jnp.float32)
        leave = rest[count:].astype(jnp.bfloat16)
        own = own + swap(sends[0], (1, 1)).astype(jnp.float32)
        own, step = own[: 2 * rows], own[2 * rows :].astype(jnp.bfloat16)
        beside = swap(step, square[0])

        arrived = []
        ends = [features * sum(PARTS[:k]) // sum(PARTS) for k in range(len(PARTS) + 1)]
        for k in ORDER:
            part = slice(ends[k], ends[k + 1])
            pieces = [diagonal[:, part], leave[count:, part], leave[:count, part]]
            if k == ORDER[-1]:
                step, *pieces = lax.optimization_barrier((step, *pieces))
            pieces = [swap(piece, masks) for piece, masks in zip(pieces, square[::-1])]
            if k == ORDER[-1]:
                beside, *pieces = lax.optimization_barrier((beside, *pieces))
            total = rest[:count, part]
            for piece in pieces:
                total = total + piece.astype(jnp.float32)
            arrived.append([])
            for masks in reversed(far):
                split = total.shape[0] // 2 // rows * rows
                piece = swap(total[split:].astype(jnp.bfloat16), masks)
                arrived[-1].append(piece[:rows])
                total = total[:split] + piece[rows:].astype(jnp.float32)
        arrived = list(zip(*(arrived[ORDER.index(k)] for k in range(len(PARTS)))))

        own = own + beside.astype(jnp.float32)
        arrived.append([swap(own[rows:].astype(jnp.bfloat16), square[1])])
        return rotate(own[:rows], arrived, sign_pattern)

    placed = (P(("groups", "gx"), None), P(None, "gx"), P(None, "gx"), P("gx", None), P())
    return jax.shard_map(
        on_device, mesh=mesh, in_specs=placed, out_specs=P(("groups", "gx"), None), check_vma=False
    )
```

```python
import functools
import math

import jax
import jax.numpy as jnp
from jax import lax
from jax.experimental import pallas as pl
from jax.experimental.pallas import tpu as pltpu
from jax.sharding import PartitionSpec as P

BLOCK = 128
SPANS = 2
TURNS = 8
NT = (((1,), (1,)), ((), ()))


def vmem():
    return pl.BlockSpec(memory_space=pltpu.VMEM)


def load_kernel(gate_hbm, up_hbm, down_hbm, _, gate_ref, up_ref, down_ref, staged, sems, down_sem):
    tile = staged.shape[2] // sems.shape[1]
    copies = []
    for k in range(sems.shape[1]):
        here = slice(k * tile, (k + 1) * tile)
        for j, source in enumerate((gate_hbm, up_hbm)):
            copies.append(
                pltpu.make_async_copy(source.at[:, here], staged.at[j, :, here], sems.at[j, k])
            )
            copies[-1].start()
    down_copy = pltpu.make_async_copy(down_hbm, down_ref, down_sem)
    down_copy.start()
    for k in range(sems.shape[1]):
        here = slice(k * tile, (k + 1) * tile)
        for j, out in enumerate((gate_ref, up_ref)):
            copies[2 * k + j].wait()
            out[here, :] = staged[j, :, here].T
    down_copy.wait()


def load(gate_w, up_w, down_w, after):
    units, features = gate_w.shape
    shape = jax.ShapeDtypeStruct((features, units), gate_w.dtype)
    return pl.pallas_call(
        load_kernel,
        out_shape=(shape, shape, jax.ShapeDtypeStruct(down_w.shape, down_w.dtype)),
        in_specs=[pl.BlockSpec(memory_space=pltpu.HBM)] * 3 + [pl.BlockSpec(memory_space=pl.ANY)],
        out_specs=(vmem(),) * 3,
        scratch_shapes=[
            pltpu.VMEM((2, units, features), gate_w.dtype),
            pltpu.SemaphoreType.DMA((2, TURNS)),
            pltpu.SemaphoreType.DMA,
        ],
        cost_estimate=pl.CostEstimate(flops=0, bytes_accessed=6 * units * features, transcendentals=0),
        compiler_params=pltpu.CompilerParams(vmem_limit_bytes=24 << 20),
    )(*(pltpu.with_memory_space_constraint(w, pltpu.HBM) for w in (gate_w, up_w, down_w)), after)


def hidden_kernel(start, last, *refs):
    gate_ref, up_ref, near_here, near_there, far_here, far_there, *refs = refs
    sums, outs = refs[: len(refs) - (1 if last else 2)], refs[-1 if last else -2 :]
    width = far_here.shape[1]
    tile = math.gcd(width, 1024)
    gate, up = (ref[...] for ref in sums) if sums else (0.0, 0.0)
    for first in range(0, width, tile):
        here, there = slice(first, first + tile), slice(start + first, start + first + tile)
        rows = jnp.concatenate([near_here[:, there], far_here[:, here], near_there[:, there], far_there[:, here]])
        gate = gate + jnp.dot(rows, gate_ref[there, :], preferred_element_type=jnp.float32)
        up = up + jnp.dot(rows, up_ref[there, :], preferred_element_type=jnp.float32)
    if last:
        outs[0][...] = (gate / (1.0 + jnp.exp(-gate)) * up).astype(jnp.bfloat16)
    else:
        outs[0][...], outs[1][...] = gate, up


def hidden_units(gate_w, up_w, near, spans):
    features, units = gate_w.shape
    count = 2 * (near[0].shape[0] + spans[0][0].shape[0])
    sums, start = (), 0
    for span in spans:
        width = span[0].shape[1]
        last = start + width == features
        total = jax.ShapeDtypeStruct((count, units), jnp.float32)
        sums = pl.pallas_call(
            functools.partial(hidden_kernel, start, last),
            out_shape=(jax.ShapeDtypeStruct((count, units), jnp.bfloat16),) if last else (total, total),
            in_specs=[vmem()] * (6 + len(sums)),
            out_specs=(vmem(),) * (1 if last else 2),
            cost_estimate=pl.CostEstimate(
                flops=4 * units * count * width, bytes_accessed=4 * units * width, transcendentals=0
            ),
            compiler_params=pltpu.CompilerParams(vmem_limit_bytes=24 << 20),
        )(gate_w, up_w, *near, *span, *sums)
        start += width
    return sums[0]


def down_kernel(spans, hidden_ref, down_ref, *outs):
    half, features = hidden_ref.shape[0] // 2, down_ref.shape[1]
    tile = math.gcd(features, 512)
    for first in range(0, features, tile):
        here = slice(first, first + tile)
        part = jnp.dot(hidden_ref[...], down_ref[:, here], preferred_element_type=jnp.float32)
        for k, out in enumerate(outs):
            begin = 0 if k < len(spans) else half
            rows = [part[begin + first : begin + last] for first, last in spans[k % len(spans)]]
            out[:, here] = jnp.concatenate(rows).astype(out.dtype)


def down(hidden, down_w, spans):
    units, features = down_w.shape
    counts = [sum(last - first for first, last in span) for span in spans]
    return pl.pallas_call(
        functools.partial(down_kernel, spans),
        out_shape=[jax.ShapeDtypeStruct((count, features), jnp.float32) for count in counts]
        + [jax.ShapeDtypeStruct((count, features), jnp.bfloat16) for count in counts],
        in_specs=[vmem()] * 2,
        out_specs=[vmem()] * (2 * len(counts)),
        cost_estimate=pl.CostEstimate(
            flops=2 * hidden.size * features, bytes_accessed=2 * units * features, transcendentals=0
        ),
        compiler_params=pltpu.CompilerParams(vmem_limit_bytes=24 << 20),
    )(hidden, down_w)


def signs_twice():
    index = jnp.arange(BLOCK, dtype=jnp.int32)
    common = index[:, None] & index[None, :]
    for shift in (4, 2, 1):
        common = common ^ (common >> shift)
    signs = (1 - 2 * (common & 1)).astype(jnp.bfloat16)
    return jnp.concatenate([signs, signs])


def rotate_kernel(count, *refs):
    total_ref, *arrived = refs[: count + 1]
    sign_ref, matrix_ref, out_ref = refs[count + 1 :]
    rows, features = total_ref.shape
    value = total_ref[...]
    for piece in arrived:
        value = value + piece[...].astype(jnp.float32)
    value = value * sign_ref[...].astype(jnp.float32)
    value = jnp.concatenate([value[:, b : b + BLOCK] for b in range(0, features, BLOCK)])
    high = value.astype(jnp.bfloat16)
    low = (value - high.astype(jnp.float32)).astype(jnp.bfloat16)
    both = jnp.concatenate([high, low], axis=1)
    turned = jnp.dot(both, matrix_ref[...], preferred_element_type=jnp.float32) * (1.0 / math.sqrt(BLOCK))
    for b in range(features // BLOCK):
        out_ref[:, b * BLOCK : (b + 1) * BLOCK] = turned[b * rows : (b + 1) * rows].astype(jnp.bfloat16)


def rotate(total, arrived, signs):
    return pl.pallas_call(
        functools.partial(rotate_kernel, len(arrived)),
        out_shape=jax.ShapeDtypeStruct(total.shape, jnp.bfloat16),
        in_specs=[vmem()] * (len(arrived) + 3),
        out_specs=vmem(),
        compiler_params=pltpu.CompilerParams(vmem_limit_bytes=16 << 20),
    )(total, *arrived, signs.reshape(1, -1), signs_twice())


def solution(mesh):
    members = mesh.shape["gx"]
    assert members & (members - 1) == 0 and members >= 16

    square = ((4, 2), (2, 4), (6, 6))
    far = []
    mask = members // 2
    while mask > 4:
        far.append((mask, mask))
        mask //= 2
    others = members // 8 - 1

    def swap(value, masks):
        return lax.ppermute(value, "gx", [(i, i ^ masks[i % 2]) for i in range(members)])

    def on_device(tokens, gate_weight, up_weight, down_weight, sign_pattern):
        rows, features = tokens.shape

        away = []
        for masks in far:
            away.append(swap(jnp.concatenate([tokens] + away), masks))
        away = jnp.concatenate(away)
        near = [swap(tokens, m) for m in square]
        away, sign_pattern = lax.optimization_barrier((away, sign_pattern))
        there = [None] * 3
        for k in (2, 0):
            there[k] = swap(away, square[k])
        away, near[0] = lax.optimization_barrier((away, near[0]))
        there[1] = swap(away, square[1])
        gate_w, up_w, down_w = load(gate_weight.T, up_weight.T, down_weight, away)
        there[0], *near = lax.optimization_barrier((there[0], *near))
        early = jnp.concatenate([near[1], near[0], near[2], away, there[0], tokens])
        early_there = swap(early, (1, 1))
        gate_w, up_w, early, *there[1:] = lax.optimization_barrier((gate_w, up_w, early, *there[1:]))
        spans = []
        width = features // SPANS
        for k in range(SPANS):
            span = jnp.concatenate([piece[:, k * width : (k + 1) * width] for piece in there[:0:-1]])
            spans.append((span, swap(span, (1, 1))))
        hidden = hidden_units(gate_w, up_w, (early, early_there), spans)

        count = others * rows
        ends = [3 * rows, 3 * rows + count, 3 * rows + 2 * count, 4 * rows + 2 * count]
        ends += [ends[3] + count, ends[3] + 2 * count]
        own_rows = ((ends[2], ends[3]), (0, ends[0]))
        rest_rows = ((ends[0], ends[2]), (ends[4], ends[5]))
        own, diagonal, rest, *sends = down(hidden, down_w, (own_rows, ((ends[3], ends[4]),), rest_rows))
        diagonal = diagonal + swap(sends[1], (1, 1)).astype(jnp.float32)
        diagonal = swap(diagonal.astype(jnp.bfloat16), square[2])
        rest_there, sends[0] = lax.optimization_barrier((swap(sends[2], (1, 1)), sends[0]))
        rest = rest + rest_there.astype(jnp.float32)
        leave = rest[count:].astype(jnp.bfloat16)
        total = rest[:count]
        for piece in (diagonal, swap(leave[:count], square[0]), swap(leave[count:], square[1])):
            total = total + piece.astype(jnp.float32)
        arrived = []
        for masks in reversed(far):
            split = total.shape[0] // 2 // rows * rows
            piece = swap(total[split:].astype(jnp.bfloat16), masks)
            arrived.append(piece[:rows])
            total = total[:split] + piece[rows:].astype(jnp.float32)

        own = own + swap(sends[0], (1, 1)).astype(jnp.float32)
        own = own[: 2 * rows] + swap(own[2 * rows :].astype(jnp.bfloat16), square[0]).astype(jnp.float32)
        arrived.append(swap(own[rows:].astype(jnp.bfloat16), square[1]))
        return rotate(own[:rows], arrived, sign_pattern)

    placed = (P(("groups", "gx"), None), P(None, "gx"), P(None, "gx"), P("gx", None), P())
    return jax.shard_map(
        on_device, mesh=mesh, in_specs=placed, out_specs=P(("groups", "gx"), None), check_vma=False
    )
```

```python
import functools
import math

import jax
import jax.numpy as jnp
from jax import lax
from jax.experimental import pallas as pl
from jax.experimental.pallas import tpu as pltpu
from jax.sharding import PartitionSpec as P

BLOCK = 128
SPANS = 2
TURNS = 8
NT = (((1,), (1,)), ((), ()))


def vmem():
    return pl.BlockSpec(memory_space=pltpu.VMEM)


def load_kernel(gate_hbm, up_hbm, down_hbm, _, gate_ref, up_ref, down_ref, staged, sems, down_sem):
    tile = staged.shape[2] // sems.shape[1]
    copies = []
    for k in range(sems.shape[1]):
        here = slice(k * tile, (k + 1) * tile)
        for j, source in enumerate((gate_hbm, up_hbm)):
            copies.append(
                pltpu.make_async_copy(source.at[:, here], staged.at[j, :, here], sems.at[j, k])
            )
            copies[-1].start()
    down_copy = pltpu.make_async_copy(down_hbm, down_ref, down_sem)
    down_copy.start()
    for k in range(sems.shape[1]):
        here = slice(k * tile, (k + 1) * tile)
        for j, out in enumerate((gate_ref, up_ref)):
            copies[2 * k + j].wait()
            out[here, :] = staged[j, :, here].T
    down_copy.wait()


def load(gate_w, up_w, down_w, after):
    units, features = gate_w.shape
    shape = jax.ShapeDtypeStruct((features, units), gate_w.dtype)
    return pl.pallas_call(
        load_kernel,
        out_shape=(shape, shape, jax.ShapeDtypeStruct(down_w.shape, down_w.dtype)),
        in_specs=[pl.BlockSpec(memory_space=pltpu.HBM)] * 3 + [pl.BlockSpec(memory_space=pl.ANY)],
        out_specs=(vmem(),) * 3,
        scratch_shapes=[
            pltpu.VMEM((2, units, features), gate_w.dtype),
            pltpu.SemaphoreType.DMA((2, TURNS)),
            pltpu.SemaphoreType.DMA,
        ],
        cost_estimate=pl.CostEstimate(flops=0, bytes_accessed=6 * units * features, transcendentals=0),
        compiler_params=pltpu.CompilerParams(vmem_limit_bytes=24 << 20),
    )(*(pltpu.with_memory_space_constraint(w, pltpu.HBM) for w in (gate_w, up_w, down_w)), after)


def hidden_kernel(start, last, *refs):
    gate_ref, up_ref, near_here, near_there, far_here, far_there, *refs = refs
    sums, outs = refs[: len(refs) - (1 if last else 2)], refs[-1 if last else -2 :]
    width = far_here.shape[1]
    tile = math.gcd(width, 1024)
    gate, up = (ref[...] for ref in sums) if sums else (0.0, 0.0)
    for first in range(0, width, tile):
        here, there = slice(first, first + tile), slice(start + first, start + first + tile)
        rows = jnp.concatenate([near_here[:, there], far_here[:, here], near_there[:, there], far_there[:, here]])
        gate = gate + jnp.dot(rows, gate_ref[there, :], preferred_element_type=jnp.float32)
        up = up + jnp.dot(rows, up_ref[there, :], preferred_element_type=jnp.float32)
    if last:
        outs[0][...] = (gate / (1.0 + jnp.exp(-gate)) * up).astype(jnp.bfloat16)
    else:
        outs[0][...], outs[1][...] = gate, up


def hidden_units(gate_w, up_w, near, spans):
    features, units = gate_w.shape
    count = 2 * (near[0].shape[0] + spans[0][0].shape[0])
    sums, start = (), 0
    for span in spans:
        width = span[0].shape[1]
        last = start + width == features
        total = jax.ShapeDtypeStruct((count, units), jnp.float32)
        sums = pl.pallas_call(
            functools.partial(hidden_kernel, start, last),
            out_shape=(jax.ShapeDtypeStruct((count, units), jnp.bfloat16),) if last else (total, total),
            in_specs=[vmem()] * (6 + len(sums)),
            out_specs=(vmem(),) * (1 if last else 2),
            cost_estimate=pl.CostEstimate(
                flops=4 * units * count * width, bytes_accessed=4 * units * width, transcendentals=0
            ),
            compiler_params=pltpu.CompilerParams(vmem_limit_bytes=24 << 20),
        )(gate_w, up_w, *near, *span, *sums)
        start += width
    return sums[0]


def down_kernel(spans, hidden_ref, down_ref, *outs):
    half, features = hidden_ref.shape[0] // 2, down_ref.shape[1]
    tile = math.gcd(features, 512)
    for first in range(0, features, tile):
        here = slice(first, first + tile)
        part = jnp.dot(hidden_ref[...], down_ref[:, here], preferred_element_type=jnp.float32)
        for k, out in enumerate(outs):
            begin = 0 if k < len(spans) else half
            rows = [part[begin + first : begin + last] for first, last in spans[k % len(spans)]]
            out[:, here] = jnp.concatenate(rows).astype(out.dtype)


def down(hidden, down_w, spans):
    units, features = down_w.shape
    counts = [sum(last - first for first, last in span) for span in spans]
    return pl.pallas_call(
        functools.partial(down_kernel, spans),
        out_shape=[jax.ShapeDtypeStruct((count, features), jnp.float32) for count in counts]
        + [jax.ShapeDtypeStruct((count, features), jnp.bfloat16) for count in counts],
        in_specs=[vmem()] * 2,
        out_specs=[vmem()] * (2 * len(counts)),
        cost_estimate=pl.CostEstimate(
            flops=2 * hidden.size * features, bytes_accessed=2 * units * features, transcendentals=0
        ),
        compiler_params=pltpu.CompilerParams(vmem_limit_bytes=24 << 20),
    )(hidden, down_w)


def signs_twice():
    index = jnp.arange(BLOCK, dtype=jnp.int32)
    common = index[:, None] & index[None, :]
    for shift in (4, 2, 1):
        common = common ^ (common >> shift)
    signs = (1 - 2 * (common & 1)).astype(jnp.bfloat16)
    return jnp.concatenate([signs, signs])


def rotate_kernel(count, *refs):
    total_ref, *arrived = refs[: count + 1]
    sign_ref, matrix_ref, out_ref = refs[count + 1 :]
    rows, features = total_ref.shape
    value = total_ref[...]
    for piece in arrived:
        value = value + piece[...].astype(jnp.float32)
    value = value * sign_ref[...].astype(jnp.float32)
    value = jnp.concatenate([value[:, b : b + BLOCK] for b in range(0, features, BLOCK)])
    high = value.astype(jnp.bfloat16)
    low = (value - high.astype(jnp.float32)).astype(jnp.bfloat16)
    both = jnp.concatenate([high, low], axis=1)
    turned = jnp.dot(both, matrix_ref[...], preferred_element_type=jnp.float32) * (1.0 / math.sqrt(BLOCK))
    for b in range(features // BLOCK):
        out_ref[:, b * BLOCK : (b + 1) * BLOCK] = turned[b * rows : (b + 1) * rows].astype(jnp.bfloat16)


def rotate(total, arrived, signs):
    return pl.pallas_call(
        functools.partial(rotate_kernel, len(arrived)),
        out_shape=jax.ShapeDtypeStruct(total.shape, jnp.bfloat16),
        in_specs=[vmem()] * (len(arrived) + 3),
        out_specs=vmem(),
        compiler_params=pltpu.CompilerParams(vmem_limit_bytes=16 << 20),
    )(total, *arrived, signs.reshape(1, -1), signs_twice())


def solution(mesh):
    members = mesh.shape["gx"]
    assert members & (members - 1) == 0 and members >= 16

    square = ((2, 4), (4, 2), (6, 6))
    far = []
    mask = members // 2
    while mask > 4:
        far.append((mask, mask))
        mask //= 2
    others = members // 8 - 1

    def swap(value, masks):
        return lax.ppermute(value, "gx", [(i, i ^ masks[i % 2]) for i in range(members)])

    def on_device(tokens, gate_weight, up_weight, down_weight, sign_pattern):
        rows, features = tokens.shape

        away = []
        for masks in far:
            away.append(swap(jnp.concatenate([tokens] + away), masks))
        away = jnp.concatenate(away)
        near = [swap(tokens, m) for m in square]
        away, sign_pattern = lax.optimization_barrier((away, sign_pattern))
        there = [swap(away, m) for m in square[:2]]
        away, near[0] = lax.optimization_barrier((away, near[0]))
        there.append(swap(away, square[2]))
        gate_w, up_w, down_w = load(gate_weight.T, up_weight.T, down_weight, away)
        there[0], *near = lax.optimization_barrier((there[0], *near))
        early = jnp.concatenate([near[1], near[0], near[2], away, there[0], tokens])
        early_there = swap(early, (1, 1))
        gate_w, up_w, early, *there[1:] = lax.optimization_barrier((gate_w, up_w, early, *there[1:]))
        spans = []
        width = features // SPANS
        for k in range(SPANS):
            span = jnp.concatenate([piece[:, k * width : (k + 1) * width] for piece in there[:0:-1]])
            spans.append((span, swap(span, (1, 1))))
        hidden = hidden_units(gate_w, up_w, (early, early_there), spans)

        count = others * rows
        ends = [3 * rows, 3 * rows + count, 3 * rows + 2 * count, 4 * rows + 2 * count]
        ends += [ends[3] + count, ends[3] + 2 * count]
        own_rows = ((ends[2], ends[3]), (0, ends[0]))
        rest_rows = ((ends[0], ends[2]), (ends[4], ends[5]))
        own, diagonal, rest, *sends = down(hidden, down_w, (own_rows, ((ends[3], ends[4]),), rest_rows))
        diagonal = diagonal + swap(sends[1], (1, 1)).astype(jnp.float32)
        diagonal = swap(diagonal.astype(jnp.bfloat16), square[2])
        rest_there, sends[0] = lax.optimization_barrier((swap(sends[2], (1, 1)), sends[0]))
        rest = rest + rest_there.astype(jnp.float32)
        leave = rest[count:].astype(jnp.bfloat16)
        total = rest[:count]
        for piece in (diagonal, swap(leave[:count], square[0]), swap(leave[count:], square[1])):
            total = total + piece.astype(jnp.float32)
        arrived = []
        for masks in reversed(far):
            split = total.shape[0] // 2 // rows * rows
            piece = swap(total[split:].astype(jnp.bfloat16), masks)
            arrived.append(piece[:rows])
            total = total[:split] + piece[rows:].astype(jnp.float32)

        own = own + swap(sends[0], (1, 1)).astype(jnp.float32)
        own = own[: 2 * rows] + swap(own[2 * rows :].astype(jnp.bfloat16), square[0]).astype(jnp.float32)
        arrived.append(swap(own[rows:].astype(jnp.bfloat16), square[1]))
        return rotate(own[:rows], arrived, sign_pattern)

    placed = (P(("groups", "gx"), None), P(None, "gx"), P(None, "gx"), P("gx", None), P())
    return jax.shard_map(
        on_device, mesh=mesh, in_specs=placed, out_specs=P(("groups", "gx"), None), check_vma=False
    )
```

```python
import functools
import math

import jax
import jax.numpy as jnp
from jax import lax
from jax.experimental import pallas as pl
from jax.experimental.pallas import tpu as pltpu
from jax.sharding import PartitionSpec as P

BLOCK = 128
SPANS = 2
TURNS = 8
NT = (((1,), (1,)), ((), ()))


def vmem():
    return pl.BlockSpec(memory_space=pltpu.VMEM)


def load_kernel(gate_hbm, up_hbm, down_hbm, _, gate_ref, up_ref, down_ref, staged, sems, down_sem):
    tile = staged.shape[2] // sems.shape[1]
    copies = []
    for k in range(sems.shape[1]):
        here = slice(k * tile, (k + 1) * tile)
        for j, source in enumerate((gate_hbm, up_hbm)):
            copies.append(
                pltpu.make_async_copy(source.at[:, here], staged.at[j, :, here], sems.at[j, k])
            )
            copies[-1].start()
    down_copy = pltpu.make_async_copy(down_hbm, down_ref, down_sem)
    down_copy.start()
    for k in range(sems.shape[1]):
        here = slice(k * tile, (k + 1) * tile)
        for j, out in enumerate((gate_ref, up_ref)):
            copies[2 * k + j].wait()
            out[here, :] = staged[j, :, here].T
    down_copy.wait()


def load(gate_w, up_w, down_w, after):
    units, features = gate_w.shape
    shape = jax.ShapeDtypeStruct((features, units), gate_w.dtype)
    return pl.pallas_call(
        load_kernel,
        out_shape=(shape, shape, jax.ShapeDtypeStruct(down_w.shape, down_w.dtype)),
        in_specs=[pl.BlockSpec(memory_space=pltpu.HBM)] * 3 + [pl.BlockSpec(memory_space=pl.ANY)],
        out_specs=(vmem(),) * 3,
        scratch_shapes=[
            pltpu.VMEM((2, units, features), gate_w.dtype),
            pltpu.SemaphoreType.DMA((2, TURNS)),
            pltpu.SemaphoreType.DMA,
        ],
        cost_estimate=pl.CostEstimate(flops=0, bytes_accessed=6 * units * features, transcendentals=0),
        compiler_params=pltpu.CompilerParams(vmem_limit_bytes=24 << 20),
    )(*(pltpu.with_memory_space_constraint(w, pltpu.HBM) for w in (gate_w, up_w, down_w)), after)


def hidden_kernel(start, last, *refs):
    gate_ref, up_ref, near_here, near_there, far_here, far_there, *refs = refs
    sums, outs = refs[: len(refs) - (1 if last else 2)], refs[-1 if last else -2 :]
    width = far_here.shape[1]
    tile = math.gcd(width, 1024)
    gate, up = (ref[...] for ref in sums) if sums else (0.0, 0.0)
    for first in range(0, width, tile):
        here, there = slice(first, first + tile), slice(start + first, start + first + tile)
        rows = jnp.concatenate([near_here[:, there], far_here[:, here], near_there[:, there], far_there[:, here]])
        gate = gate + jnp.dot(rows, gate_ref[there, :], preferred_element_type=jnp.float32)
        up = up + jnp.dot(rows, up_ref[there, :], preferred_element_type=jnp.float32)
    if last:
        outs[0][...] = (gate / (1.0 + jnp.exp(-gate)) * up).astype(jnp.bfloat16)
    else:
        outs[0][...], outs[1][...] = gate, up


def hidden_units(gate_w, up_w, near, spans):
    features, units = gate_w.shape
    count = 2 * (near[0].shape[0] + spans[0][0].shape[0])
    sums, start = (), 0
    for span in spans:
        width = span[0].shape[1]
        last = start + width == features
        total = jax.ShapeDtypeStruct((count, units), jnp.float32)
        sums = pl.pallas_call(
            functools.partial(hidden_kernel, start, last),
            out_shape=(jax.ShapeDtypeStruct((count, units), jnp.bfloat16),) if last else (total, total),
            in_specs=[vmem()] * (6 + len(sums)),
            out_specs=(vmem(),) * (1 if last else 2),
            cost_estimate=pl.CostEstimate(
                flops=4 * units * count * width, bytes_accessed=4 * units * width, transcendentals=0
            ),
            compiler_params=pltpu.CompilerParams(vmem_limit_bytes=24 << 20),
        )(gate_w, up_w, *near, *span, *sums)
        start += width
    return sums[0]


def down_kernel(spans, hidden_ref, down_ref, *outs):
    half, features = hidden_ref.shape[0] // 2, down_ref.shape[1]
    tile = math.gcd(features, 512)
    for first in range(0, features, tile):
        here = slice(first, first + tile)
        part = jnp.dot(hidden_ref[...], down_ref[:, here], preferred_element_type=jnp.float32)
        for k, out in enumerate(outs):
            begin = 0 if k < len(spans) else half
            rows = [part[begin + first : begin + last] for first, last in spans[k % len(spans)]]
            out[:, here] = jnp.concatenate(rows).astype(out.dtype)


def down(hidden, down_w, spans):
    units, features = down_w.shape
    counts = [sum(last - first for first, last in span) for span in spans]
    return pl.pallas_call(
        functools.partial(down_kernel, spans),
        out_shape=[jax.ShapeDtypeStruct((count, features), jnp.float32) for count in counts]
        + [jax.ShapeDtypeStruct((count, features), jnp.bfloat16) for count in counts],
        in_specs=[vmem()] * 2,
        out_specs=[vmem()] * (2 * len(counts)),
        cost_estimate=pl.CostEstimate(
            flops=2 * hidden.size * features, bytes_accessed=2 * units * features, transcendentals=0
        ),
        compiler_params=pltpu.CompilerParams(vmem_limit_bytes=24 << 20),
    )(hidden, down_w)


def signs_twice():
    index = jnp.arange(BLOCK, dtype=jnp.int32)
    common = index[:, None] & index[None, :]
    for shift in (4, 2, 1):
        common = common ^ (common >> shift)
    signs = (1 - 2 * (common & 1)).astype(jnp.bfloat16)
    return jnp.concatenate([signs, signs])


def rotate_kernel(count, *refs):
    total_ref, *arrived = refs[: count + 1]
    sign_ref, matrix_ref, out_ref = refs[count + 1 :]
    rows, features = total_ref.shape
    value = total_ref[...]
    for piece in arrived:
        value = value + piece[...].astype(jnp.float32)
    value = value * sign_ref[...].astype(jnp.float32)
    value = jnp.concatenate([value[:, b : b + BLOCK] for b in range(0, features, BLOCK)])
    high = value.astype(jnp.bfloat16)
    low = (value - high.astype(jnp.float32)).astype(jnp.bfloat16)
    both = jnp.concatenate([high, low], axis=1)
    turned = jnp.dot(both, matrix_ref[...], preferred_element_type=jnp.float32) * (1.0 / math.sqrt(BLOCK))
    for b in range(features // BLOCK):
        out_ref[:, b * BLOCK : (b + 1) * BLOCK] = turned[b * rows : (b + 1) * rows].astype(jnp.bfloat16)


def rotate(total, arrived, signs):
    return pl.pallas_call(
        functools.partial(rotate_kernel, len(arrived)),
        out_shape=jax.ShapeDtypeStruct(total.shape, jnp.bfloat16),
        in_specs=[vmem()] * (len(arrived) + 3),
        out_specs=vmem(),
        compiler_params=pltpu.CompilerParams(vmem_limit_bytes=16 << 20),
    )(total, *arrived, signs.reshape(1, -1), signs_twice())


def solution(mesh):
    members = mesh.shape["gx"]
    assert members & (members - 1) == 0 and members >= 16

    square = ((4, 2), (2, 4), (6, 6))
    far = []
    mask = members // 2
    while mask > 4:
        far.append((mask, mask))
        mask //= 2
    others = members // 8 - 1

    def swap(value, masks):
        return lax.ppermute(value, "gx", [(i, i ^ masks[i % 2]) for i in range(members)])

    def on_device(tokens, gate_weight, up_weight, down_weight, sign_pattern):
        rows, features = tokens.shape

        away = []
        for masks in far:
            away.append(swap(jnp.concatenate([tokens] + away), masks))
        away = jnp.concatenate(away)
        near = [swap(tokens, m) for m in square]
        away, sign_pattern = lax.optimization_barrier((away, sign_pattern))
        there = [swap(away, m) for m in square[:2]]
        away, near[0] = lax.optimization_barrier((away, near[0]))
        there.append(swap(away, square[2]))
        gate_w, up_w, down_w = load(gate_weight.T, up_weight.T, down_weight, away)
        there[0], *near = lax.optimization_barrier((there[0], *near))
        early = jnp.concatenate([near[1], near[0], near[2], away, there[0], tokens])
        early_there = swap(early, (1, 1))
        gate_w, up_w, early, *there[1:] = lax.optimization_barrier((gate_w, up_w, early, *there[1:]))
        spans = []
        width = features // SPANS
        for k in range(SPANS):
            span = jnp.concatenate([piece[:, k * width : (k + 1) * width] for piece in there[:0:-1]])
            spans.append((span, swap(span, (1, 1))))
        hidden = hidden_units(gate_w, up_w, (early, early_there), spans)

        count = others * rows
        ends = [3 * rows, 3 * rows + count, 3 * rows + 2 * count, 4 * rows + 2 * count]
        ends += [ends[3] + count, ends[3] + 2 * count]
        own_rows = ((ends[2], ends[3]), (0, ends[0]))
        rest_rows = ((ends[0], ends[2]), (ends[4], ends[5]))
        own, diagonal, rest, *sends = down(hidden, down_w, (own_rows, ((ends[3], ends[4]),), rest_rows))
        diagonal = diagonal + swap(sends[1], (1, 1)).astype(jnp.float32)
        diagonal = swap(diagonal.astype(jnp.bfloat16), square[2])
        rest_there, sends[0] = lax.optimization_barrier((swap(sends[2], (1, 1)), sends[0]))
        rest = rest + rest_there.astype(jnp.float32)
        leave = rest[count:].astype(jnp.bfloat16)
        diagonal, own = lax.optimization_barrier((diagonal, own))
        total = rest[:count]
        for piece in (diagonal, swap(leave[:count], square[0]), swap(leave[count:], square[1])):
            total = total + piece.astype(jnp.float32)
        arrived = []
        for masks in reversed(far):
            split = total.shape[0] // 2 // rows * rows
            piece = swap(total[split:].astype(jnp.bfloat16), masks)
            arrived.append(piece[:rows])
            total = total[:split] + piece[rows:].astype(jnp.float32)

        own = own + swap(sends[0], (1, 1)).astype(jnp.float32)
        own = own[: 2 * rows] + swap(own[2 * rows :].astype(jnp.bfloat16), square[0]).astype(jnp.float32)
        arrived.append(swap(own[rows:].astype(jnp.bfloat16), square[1]))
        return rotate(own[:rows], arrived, sign_pattern)

    placed = (P(("groups", "gx"), None), P(None, "gx"), P(None, "gx"), P("gx", None), P())
    return jax.shard_map(
        on_device, mesh=mesh, in_specs=placed, out_specs=P(("groups", "gx"), None), check_vma=False
    )
```

```python
import functools
import math

import jax
import jax.numpy as jnp
from jax import lax
from jax.experimental import pallas as pl
from jax.experimental.pallas import tpu as pltpu
from jax.sharding import PartitionSpec as P

BLOCK = 128
SPANS = 2
TURNS = 8
NT = (((1,), (1,)), ((), ()))


def vmem():
    return pl.BlockSpec(memory_space=pltpu.VMEM)


def load_kernel(gate_hbm, up_hbm, down_hbm, _, gate_ref, up_ref, down_ref, staged, sems, down_sem):
    tile = staged.shape[2] // sems.shape[1]
    copies = []
    for k in range(sems.shape[1]):
        here = slice(k * tile, (k + 1) * tile)
        for j, source in enumerate((gate_hbm, up_hbm)):
            copies.append(
                pltpu.make_async_copy(source.at[:, here], staged.at[j, :, here], sems.at[j, k])
            )
            copies[-1].start()
    down_copy = pltpu.make_async_copy(down_hbm, down_ref, down_sem)
    down_copy.start()
    for k in range(sems.shape[1]):
        here = slice(k * tile, (k + 1) * tile)
        for j, out in enumerate((gate_ref, up_ref)):
            copies[2 * k + j].wait()
            out[here, :] = staged[j, :, here].T
    down_copy.wait()


def load(gate_w, up_w, down_w, after):
    units, features = gate_w.shape
    shape = jax.ShapeDtypeStruct((features, units), gate_w.dtype)
    return pl.pallas_call(
        load_kernel,
        out_shape=(shape, shape, jax.ShapeDtypeStruct(down_w.shape, down_w.dtype)),
        in_specs=[pl.BlockSpec(memory_space=pltpu.HBM)] * 3 + [pl.BlockSpec(memory_space=pl.ANY)],
        out_specs=(vmem(),) * 3,
        scratch_shapes=[
            pltpu.VMEM((2, units, features), gate_w.dtype),
            pltpu.SemaphoreType.DMA((2, TURNS)),
            pltpu.SemaphoreType.DMA,
        ],
        cost_estimate=pl.CostEstimate(flops=0, bytes_accessed=6 * units * features, transcendentals=0),
        compiler_params=pltpu.CompilerParams(vmem_limit_bytes=24 << 20),
    )(*(pltpu.with_memory_space_constraint(w, pltpu.HBM) for w in (gate_w, up_w, down_w)), after)


def hidden_kernel(start, last, *refs):
    gate_ref, up_ref, near_here, near_there, far_here, far_there, *refs = refs
    sums, outs = refs[: len(refs) - (1 if last else 2)], refs[-1 if last else -2 :]
    width = far_here.shape[1]
    tile = math.gcd(width, 1024)
    gate, up = (ref[...] for ref in sums) if sums else (0.0, 0.0)
    for first in range(0, width, tile):
        here, there = slice(first, first + tile), slice(start + first, start + first + tile)
        rows = jnp.concatenate([near_here[:, there], far_here[:, here], near_there[:, there], far_there[:, here]])
        gate = gate + jnp.dot(rows, gate_ref[there, :], preferred_element_type=jnp.float32)
        up = up + jnp.dot(rows, up_ref[there, :], preferred_element_type=jnp.float32)
    if last:
        outs[0][...] = (gate / (1.0 + jnp.exp(-gate)) * up).astype(jnp.bfloat16)
    else:
        outs[0][...], outs[1][...] = gate, up


def hidden_units(gate_w, up_w, near, spans):
    features, units = gate_w.shape
    count = 2 * (near[0].shape[0] + spans[0][0].shape[0])
    sums, start = (), 0
    for span in spans:
        width = span[0].shape[1]
        last = start + width == features
        total = jax.ShapeDtypeStruct((count, units), jnp.float32)
        sums = pl.pallas_call(
            functools.partial(hidden_kernel, start, last),
            out_shape=(jax.ShapeDtypeStruct((count, units), jnp.bfloat16),) if last else (total, total),
            in_specs=[vmem()] * (6 + len(sums)),
            out_specs=(vmem(),) * (1 if last else 2),
            cost_estimate=pl.CostEstimate(
                flops=4 * units * count * width, bytes_accessed=4 * units * width, transcendentals=0
            ),
            compiler_params=pltpu.CompilerParams(vmem_limit_bytes=24 << 20),
        )(gate_w, up_w, *near, *span, *sums)
        start += width
    return sums[0]


def down_kernel(spans, hidden_ref, down_ref, *outs):
    half, features = hidden_ref.shape[0] // 2, down_ref.shape[1]
    tile = math.gcd(features, 512)
    for first in range(0, features, tile):
        here = slice(first, first + tile)
        part = jnp.dot(hidden_ref[...], down_ref[:, here], preferred_element_type=jnp.float32)
        for k, out in enumerate(outs):
            begin = 0 if k < len(spans) else half
            rows = [part[begin + first : begin + last] for first, last in spans[k % len(spans)]]
            out[:, here] = jnp.concatenate(rows).astype(out.dtype)


def down(hidden, down_w, spans):
    units, features = down_w.shape
    counts = [sum(last - first for first, last in span) for span in spans]
    return pl.pallas_call(
        functools.partial(down_kernel, spans),
        out_shape=[jax.ShapeDtypeStruct((count, features), jnp.float32) for count in counts]
        + [jax.ShapeDtypeStruct((count, features), jnp.bfloat16) for count in counts],
        in_specs=[vmem()] * 2,
        out_specs=[vmem()] * (2 * len(counts)),
        cost_estimate=pl.CostEstimate(
            flops=2 * hidden.size * features, bytes_accessed=2 * units * features, transcendentals=0
        ),
        compiler_params=pltpu.CompilerParams(vmem_limit_bytes=24 << 20),
    )(hidden, down_w)


def signs_twice():
    index = jnp.arange(BLOCK, dtype=jnp.int32)
    common = index[:, None] & index[None, :]
    for shift in (4, 2, 1):
        common = common ^ (common >> shift)
    signs = (1 - 2 * (common & 1)).astype(jnp.bfloat16)
    return jnp.concatenate([signs, signs])


def rotate_kernel(count, *refs):
    total_ref, *arrived = refs[: count + 1]
    sign_ref, matrix_ref, out_ref = refs[count + 1 :]
    rows, features = total_ref.shape
    value = total_ref[...]
    for piece in arrived:
        value = value + piece[...].astype(jnp.float32)
    value = value * sign_ref[...].astype(jnp.float32)
    value = jnp.concatenate([value[:, b : b + BLOCK] for b in range(0, features, BLOCK)])
    high = value.astype(jnp.bfloat16)
    low = (value - high.astype(jnp.float32)).astype(jnp.bfloat16)
    both = jnp.concatenate([high, low], axis=1)
    turned = jnp.dot(both, matrix_ref[...], preferred_element_type=jnp.float32) * (1.0 / math.sqrt(BLOCK))
    for b in range(features // BLOCK):
        out_ref[:, b * BLOCK : (b + 1) * BLOCK] = turned[b * rows : (b + 1) * rows].astype(jnp.bfloat16)


def rotate(total, arrived, signs):
    return pl.pallas_call(
        functools.partial(rotate_kernel, len(arrived)),
        out_shape=jax.ShapeDtypeStruct(total.shape, jnp.bfloat16),
        in_specs=[vmem()] * (len(arrived) + 3),
        out_specs=vmem(),
        compiler_params=pltpu.CompilerParams(vmem_limit_bytes=16 << 20),
    )(total, *arrived, signs.reshape(1, -1), signs_twice())


def solution(mesh):
    members = mesh.shape["gx"]
    assert members & (members - 1) == 0 and members >= 16

    square = ((4, 2), (2, 4), (6, 6))
    far = []
    mask = members // 2
    while mask > 4:
        far.append((mask, mask))
        mask //= 2
    others = members // 8 - 1

    def swap(value, masks):
        return lax.ppermute(value, "gx", [(i, i ^ masks[i % 2]) for i in range(members)])

    def on_device(tokens, gate_weight, up_weight, down_weight, sign_pattern):
        rows, features = tokens.shape

        away = []
        for masks in far:
            away.append(swap(jnp.concatenate([tokens] + away), masks))
        away = jnp.concatenate(away)
        near = [swap(tokens, m) for m in square]
        away, sign_pattern = lax.optimization_barrier((away, sign_pattern))
        there = [None] * 3
        for k in (2, 0):
            there[k] = swap(away, square[k])
        away, near[0] = lax.optimization_barrier((away, near[0]))
        there[1] = swap(away, square[1])
        gate_w, up_w, down_w = load(gate_weight.T, up_weight.T, down_weight, away)
        there[0], *near = lax.optimization_barrier((there[0], *near))
        early = jnp.concatenate([near[1], near[0], near[2], away, there[0], tokens])
        early_there = swap(early, (1, 1))
        gate_w, up_w, early, *there[1:] = lax.optimization_barrier((gate_w, up_w, early, *there[1:]))
        spans = []
        width = features // SPANS
        for k in range(SPANS):
            span = jnp.concatenate([piece[:, k * width : (k + 1) * width] for piece in there[:0:-1]])
            spans.append((span, swap(span, (1, 1))))
        hidden = hidden_units(gate_w, up_w, (early, early_there), spans)

        count = others * rows
        ends = [3 * rows, 3 * rows + count, 3 * rows + 2 * count, 4 * rows + 2 * count]
        ends += [ends[3] + count, ends[3] + 2 * count]
        own_rows = ((ends[2], ends[3]), (0, ends[0]))
        rest_rows = ((ends[0], ends[2]), (ends[4], ends[5]))
        own, diagonal, rest, *sends = down(hidden, down_w, (own_rows, ((ends[3], ends[4]),), rest_rows))
        diagonal = diagonal + swap(sends[1], (1, 1)).astype(jnp.float32)
        diagonal = swap(diagonal.astype(jnp.bfloat16), square[2])
        rest_there, sends[0] = lax.optimization_barrier((swap(sends[2], (1, 1)), sends[0]))
        rest = rest + rest_there.astype(jnp.float32)
        leave = rest[count:].astype(jnp.bfloat16)
        own_there, diagonal = lax.optimization_barrier((swap(sends[0], (1, 1)), diagonal))
        total = rest[:count]
        for piece in (diagonal, swap(leave[:count], square[0]), swap(leave[count:], square[1])):
            total = total + piece.astype(jnp.float32)
        arrived = []
        for masks in reversed(far):
            split = total.shape[0] // 2 // rows * rows
            piece = swap(total[split:].astype(jnp.bfloat16), masks)
            arrived.append(piece[:rows])
            total = total[:split] + piece[rows:].astype(jnp.float32)

        own = own + own_there.astype(jnp.float32)
        own = own[: 2 * rows] + swap(own[2 * rows :].astype(jnp.bfloat16), square[0]).astype(jnp.float32)
        arrived.append(swap(own[rows:].astype(jnp.bfloat16), square[1]))
        return rotate(own[:rows], arrived, sign_pattern)

    placed = (P(("groups", "gx"), None), P(None, "gx"), P(None, "gx"), P("gx", None), P())
    return jax.shard_map(
        on_device, mesh=mesh, in_specs=placed, out_specs=P(("groups", "gx"), None), check_vma=False
    )
```

```python
import functools
import math

import jax
import jax.numpy as jnp
from jax import lax
from jax.experimental import pallas as pl
from jax.experimental.pallas import tpu as pltpu
from jax.sharding import PartitionSpec as P

BLOCK = 128
SPANS = 2
TURNS = 8
NT = (((1,), (1,)), ((), ()))


def vmem():
    return pl.BlockSpec(memory_space=pltpu.VMEM)


def load_kernel(gate_hbm, up_hbm, down_hbm, _, gate_ref, up_ref, down_ref, staged, sems, down_sem):
    tile = staged.shape[2] // sems.shape[1]
    copies = []
    for k in range(sems.shape[1]):
        here = slice(k * tile, (k + 1) * tile)
        for j, source in enumerate((gate_hbm, up_hbm)):
            copies.append(
                pltpu.make_async_copy(source.at[:, here], staged.at[j, :, here], sems.at[j, k])
            )
            copies[-1].start()
    down_copy = pltpu.make_async_copy(down_hbm, down_ref, down_sem)
    down_copy.start()
    for k in range(sems.shape[1]):
        here = slice(k * tile, (k + 1) * tile)
        for j, out in enumerate((gate_ref, up_ref)):
            copies[2 * k + j].wait()
            out[here, :] = staged[j, :, here].T
    down_copy.wait()


def load(gate_w, up_w, down_w, after):
    units, features = gate_w.shape
    shape = jax.ShapeDtypeStruct((features, units), gate_w.dtype)
    return pl.pallas_call(
        load_kernel,
        out_shape=(shape, shape, jax.ShapeDtypeStruct(down_w.shape, down_w.dtype)),
        in_specs=[pl.BlockSpec(memory_space=pltpu.HBM)] * 3 + [pl.BlockSpec(memory_space=pl.ANY)],
        out_specs=(vmem(),) * 3,
        scratch_shapes=[
            pltpu.VMEM((2, units, features), gate_w.dtype),
            pltpu.SemaphoreType.DMA((2, TURNS)),
            pltpu.SemaphoreType.DMA,
        ],
        cost_estimate=pl.CostEstimate(flops=0, bytes_accessed=6 * units * features, transcendentals=0),
        compiler_params=pltpu.CompilerParams(vmem_limit_bytes=24 << 20),
    )(*(pltpu.with_memory_space_constraint(w, pltpu.HBM) for w in (gate_w, up_w, down_w)), after)


def hidden_kernel(start, last, *refs):
    gate_ref, up_ref, near_here, near_there, far_here, far_there, *refs = refs
    sums, outs = refs[: len(refs) - (1 if last else 2)], refs[-1 if last else -2 :]
    width = far_here.shape[1]
    tile = math.gcd(width, 1024)
    gate, up = (ref[...] for ref in sums) if sums else (0.0, 0.0)
    for first in range(0, width, tile):
        here, there = slice(first, first + tile), slice(start + first, start + first + tile)
        rows = jnp.concatenate([near_here[:, there], far_here[:, here], near_there[:, there], far_there[:, here]])
        gate = gate + jnp.dot(rows, gate_ref[there, :], preferred_element_type=jnp.float32)
        up = up + jnp.dot(rows, up_ref[there, :], preferred_element_type=jnp.float32)
    if last:
        outs[0][...] = (gate / (1.0 + jnp.exp(-gate)) * up).astype(jnp.bfloat16)
    else:
        outs[0][...], outs[1][...] = gate, up


def hidden_units(gate_w, up_w, near, spans):
    features, units = gate_w.shape
    count = 2 * (near[0].shape[0] + spans[0][0].shape[0])
    sums, start = (), 0
    for span in spans:
        width = span[0].shape[1]
        last = start + width == features
        total = jax.ShapeDtypeStruct((count, units), jnp.float32)
        sums = pl.pallas_call(
            functools.partial(hidden_kernel, start, last),
            out_shape=(jax.ShapeDtypeStruct((count, units), jnp.bfloat16),) if last else (total, total),
            in_specs=[vmem()] * (6 + len(sums)),
            out_specs=(vmem(),) * (1 if last else 2),
            cost_estimate=pl.CostEstimate(
                flops=4 * units * count * width, bytes_accessed=4 * units * width, transcendentals=0
            ),
            compiler_params=pltpu.CompilerParams(vmem_limit_bytes=24 << 20),
        )(gate_w, up_w, *near, *span, *sums)
        start += width
    return sums[0]


def down_kernel(spans, hidden_ref, down_ref, *outs):
    half, features = hidden_ref.shape[0] // 2, down_ref.shape[1]
    tile = math.gcd(features, 512)
    for first in range(0, features, tile):
        here = slice(first, first + tile)
        part = jnp.dot(hidden_ref[...], down_ref[:, here], preferred_element_type=jnp.float32)
        for k, out in enumerate(outs):
            begin = 0 if k < len(spans) else half
            rows = [part[begin + first : begin + last] for first, last in spans[k % len(spans)]]
            out[:, here] = jnp.concatenate(rows).astype(out.dtype)


def down(hidden, down_w, spans):
    units, features = down_w.shape
    counts = [sum(last - first for first, last in span) for span in spans]
    return pl.pallas_call(
        functools.partial(down_kernel, spans),
        out_shape=[jax.ShapeDtypeStruct((count, features), jnp.float32) for count in counts]
        + [jax.ShapeDtypeStruct((count, features), jnp.bfloat16) for count in counts],
        in_specs=[vmem()] * 2,
        out_specs=[vmem()] * (2 * len(counts)),
        cost_estimate=pl.CostEstimate(
            flops=2 * hidden.size * features, bytes_accessed=2 * units * features, transcendentals=0
        ),
        compiler_params=pltpu.CompilerParams(vmem_limit_bytes=24 << 20),
    )(hidden, down_w)


def signs_twice():
    index = jnp.arange(BLOCK, dtype=jnp.int32)
    common = index[:, None] & index[None, :]
    for shift in (4, 2, 1):
        common = common ^ (common >> shift)
    signs = (1 - 2 * (common & 1)).astype(jnp.bfloat16)
    return jnp.concatenate([signs, signs])


def rotate_kernel(count, *refs):
    total_ref, *arrived = refs[: count + 1]
    sign_ref, matrix_ref, out_ref = refs[count + 1 :]
    rows, features = total_ref.shape
    value = total_ref[...]
    for piece in arrived:
        value = value + piece[...].astype(jnp.float32)
    value = value * sign_ref[...].astype(jnp.float32)
    value = jnp.concatenate([value[:, b : b + BLOCK] for b in range(0, features, BLOCK)])
    high = value.astype(jnp.bfloat16)
    low = (value - high.astype(jnp.float32)).astype(jnp.bfloat16)
    both = jnp.concatenate([high, low], axis=1)
    turned = jnp.dot(both, matrix_ref[...], preferred_element_type=jnp.float32) * (1.0 / math.sqrt(BLOCK))
    for b in range(features // BLOCK):
        out_ref[:, b * BLOCK : (b + 1) * BLOCK] = turned[b * rows : (b + 1) * rows].astype(jnp.bfloat16)


def rotate(total, arrived, signs):
    return pl.pallas_call(
        functools.partial(rotate_kernel, len(arrived)),
        out_shape=jax.ShapeDtypeStruct(total.shape, jnp.bfloat16),
        in_specs=[vmem()] * (len(arrived) + 3),
        out_specs=vmem(),
        compiler_params=pltpu.CompilerParams(vmem_limit_bytes=16 << 20),
    )(total, *arrived, signs.reshape(1, -1), signs_twice())


def solution(mesh):
    members = mesh.shape["gx"]
    assert members & (members - 1) == 0 and members >= 16

    square = ((4, 2), (2, 4), (6, 6))
    far = []
    mask = members // 2
    while mask > 4:
        far.append((mask, mask))
        mask //= 2
    others = members // 8 - 1

    def swap(value, masks):
        return lax.ppermute(value, "gx", [(i, i ^ masks[i % 2]) for i in range(members)])

    def on_device(tokens, gate_weight, up_weight, down_weight, sign_pattern):
        rows, features = tokens.shape

        away = []
        for masks in far:
            away.append(swap(jnp.concatenate([tokens] + away), masks))
        away = jnp.concatenate(away)
        near = [swap(tokens, m) for m in square]
        away, sign_pattern = lax.optimization_barrier((away, sign_pattern))
        there = [swap(away, m) for m in square[:2]]
        away, near[0] = lax.optimization_barrier((away, near[0]))
        there.append(swap(away, square[2]))
        gate_w, up_w, down_w = load(gate_weight.T, up_weight.T, down_weight, away)
        there[0], *near = lax.optimization_barrier((there[0], *near))
        early = jnp.concatenate([near[1], near[0], near[2], away, there[0], tokens])
        early_there = swap(early, (1, 1))
        gate_w, up_w, early, *there[1:] = lax.optimization_barrier((gate_w, up_w, early, *there[1:]))
        spans = []
        width = features // SPANS
        for k in range(SPANS):
            span = jnp.concatenate([piece[:, k * width : (k + 1) * width] for piece in there[:0:-1]])
            spans.append((span, swap(span, (1, 1))))
        hidden = hidden_units(gate_w, up_w, (early, early_there), spans)

        count = others * rows
        ends = [3 * rows, 3 * rows + count, 3 * rows + 2 * count, 4 * rows + 2 * count]
        ends += [ends[3] + count, ends[3] + 2 * count]
        own_rows = ((ends[2], ends[3]), (0, ends[0]))
        rest_rows = ((ends[0], ends[2]), (ends[4], ends[5]))
        own, diagonal, rest, *sends = down(hidden, down_w, (own_rows, ((ends[3], ends[4]),), rest_rows))
        diagonal = diagonal + swap(sends[1], (1, 1)).astype(jnp.float32)
        diagonal = swap(diagonal.astype(jnp.bfloat16), square[2])
        rest_there, sends[0] = lax.optimization_barrier((swap(sends[2], (1, 1)), sends[0]))
        rest = rest + rest_there.astype(jnp.float32)
        leave = rest[count:].astype(jnp.bfloat16)
        total = rest[:count]
        for piece in (diagonal, swap(leave[count:], square[1]), swap(leave[:count], square[0])):
            total = total + piece.astype(jnp.float32)
        arrived = []
        for masks in reversed(far):
            split = total.shape[0] // 2 // rows * rows
            piece = swap(total[split:].astype(jnp.bfloat16), masks)
            arrived.append(piece[:rows])
            total = total[:split] + piece[rows:].astype(jnp.float32)

        own = own + swap(sends[0], (1, 1)).astype(jnp.float32)
        own = own[: 2 * rows] + swap(own[2 * rows :].astype(jnp.bfloat16), square[0]).astype(jnp.float32)
        arrived.append(swap(own[rows:].astype(jnp.bfloat16), square[1]))
        return rotate(own[:rows], arrived, sign_pattern)

    placed = (P(("groups", "gx"), None), P(None, "gx"), P(None, "gx"), P("gx", None), P())
    return jax.shard_map(
        on_device, mesh=mesh, in_specs=placed, out_specs=P(("groups", "gx"), None), check_vma=False
    )
```

```python
import functools
import math

import jax
import jax.numpy as jnp
from jax import lax
from jax.experimental import pallas as pl
from jax.experimental.pallas import tpu as pltpu
from jax.sharding import PartitionSpec as P

BLOCK = 128
SPANS = 2
TURNS = 8
NT = (((1,), (1,)), ((), ()))


def vmem():
    return pl.BlockSpec(memory_space=pltpu.VMEM)


def load_kernel(turned, *refs):
    count = len(turned)
    sources, outs = refs[:count], refs[count + 1 : 2 * count + 1]
    staged, sems = refs[2 * count + 1 :]
    tile = staged.shape[1] // (sems.shape[0] - 1)
    copies = []
    for source, out, turn in zip(sources, outs, turned):
        if not turn:
            continue
        for k in range(sems.shape[0] - 1):
            here = slice(k * tile, (k + 1) * tile)
            copies.append((pltpu.make_async_copy(source.at[:, here], staged.at[:, here], sems.at[k]), out, here))
    others = [
        pltpu.make_async_copy(source, out, sems.at[sems.shape[0] - 1])
        for source, out, turn in zip(sources, outs, turned)
        if not turn
    ]
    for copy, _, _ in copies:
        copy.start()
    for copy in others:
        copy.start()
    for copy, out, here in copies:
        copy.wait()
        out[here, :] = staged[:, here].T
    for copy in others:
        copy.wait()


def load(weights, turned, after):
    shapes = [w.shape[::-1] if turn else w.shape for w, turn in zip(weights, turned)]
    size = sum(w.size for w in weights)
    return pl.pallas_call(
        functools.partial(load_kernel, turned),
        out_shape=[jax.ShapeDtypeStruct(shape, weights[0].dtype) for shape in shapes],
        in_specs=[pl.BlockSpec(memory_space=pltpu.HBM)] * len(weights) + [pl.BlockSpec(memory_space=pl.ANY)],
        out_specs=[vmem()] * len(weights),
        scratch_shapes=[
            pltpu.VMEM(weights[0].shape, weights[0].dtype),
            pltpu.SemaphoreType.DMA((TURNS + 1,)),
        ],
        cost_estimate=pl.CostEstimate(flops=0, bytes_accessed=4 * size, transcendentals=0),
        compiler_params=pltpu.CompilerParams(vmem_limit_bytes=16 << 20),
    )(*(pltpu.with_memory_space_constraint(w, pltpu.HBM) for w in weights), after)


def hidden_kernel(start, last, *refs):
    gate_ref, up_ref, near_here, near_there, far_here, far_there, *refs = refs
    sums, outs = refs[: len(refs) - (1 if last else 2)], refs[-1 if last else -2 :]
    width = far_here.shape[1]
    tile = math.gcd(width, 1024)
    gate, up = (ref[...] for ref in sums) if sums else (0.0, 0.0)
    for first in range(0, width, tile):
        here, there = slice(first, first + tile), slice(start + first, start + first + tile)
        rows = jnp.concatenate([near_here[:, there], far_here[:, here], near_there[:, there], far_there[:, here]])
        gate = gate + jnp.dot(rows, gate_ref[there, :], preferred_element_type=jnp.float32)
        up = up + jnp.dot(rows, up_ref[there, :], preferred_element_type=jnp.float32)
    if last:
        outs[0][...] = (gate / (1.0 + jnp.exp(-gate)) * up).astype(jnp.bfloat16)
    else:
        outs[0][...], outs[1][...] = gate, up


def hidden_units(gate_w, up_w, near, spans):
    features, units = gate_w.shape
    count = 2 * (near[0].shape[0] + spans[0][0].shape[0])
    sums, start = (), 0
    for span in spans:
        width = span[0].shape[1]
        last = start + width == features
        total = jax.ShapeDtypeStruct((count, units), jnp.float32)
        sums = pl.pallas_call(
            functools.partial(hidden_kernel, start, last),
            out_shape=(jax.ShapeDtypeStruct((count, units), jnp.bfloat16),) if last else (total, total),
            in_specs=[vmem()] * (6 + len(sums)),
            out_specs=(vmem(),) * (1 if last else 2),
            cost_estimate=pl.CostEstimate(
                flops=4 * units * count * width, bytes_accessed=4 * units * width, transcendentals=0
            ),
            compiler_params=pltpu.CompilerParams(vmem_limit_bytes=24 << 20),
        )(gate_w, up_w, *near, *span, *sums)
        start += width
    return sums[0]


def down_kernel(spans, hidden_ref, down_ref, *outs):
    half, features = hidden_ref.shape[0] // 2, down_ref.shape[1]
    tile = math.gcd(features, 512)
    for first in range(0, features, tile):
        here = slice(first, first + tile)
        part = jnp.dot(hidden_ref[...], down_ref[:, here], preferred_element_type=jnp.float32)
        for k, out in enumerate(outs):
            begin = 0 if k < len(spans) else half
            rows = [part[begin + first : begin + last] for first, last in spans[k % len(spans)]]
            out[:, here] = jnp.concatenate(rows).astype(out.dtype)


def down(hidden, down_w, spans):
    units, features = down_w.shape
    counts = [sum(last - first for first, last in span) for span in spans]
    return pl.pallas_call(
        functools.partial(down_kernel, spans),
        out_shape=[jax.ShapeDtypeStruct((count, features), jnp.float32) for count in counts]
        + [jax.ShapeDtypeStruct((count, features), jnp.bfloat16) for count in counts],
        in_specs=[vmem()] * 2,
        out_specs=[vmem()] * (2 * len(counts)),
        cost_estimate=pl.CostEstimate(
            flops=2 * hidden.size * features, bytes_accessed=2 * units * features, transcendentals=0
        ),
        compiler_params=pltpu.CompilerParams(vmem_limit_bytes=24 << 20),
    )(hidden, down_w)


def signs_twice():
    index = jnp.arange(BLOCK, dtype=jnp.int32)
    common = index[:, None] & index[None, :]
    for shift in (4, 2, 1):
        common = common ^ (common >> shift)
    signs = (1 - 2 * (common & 1)).astype(jnp.bfloat16)
    return jnp.concatenate([signs, signs])


def rotate_kernel(count, *refs):
    total_ref, *arrived = refs[: count + 1]
    sign_ref, matrix_ref, out_ref = refs[count + 1 :]
    rows, features = total_ref.shape
    value = total_ref[...]
    for piece in arrived:
        value = value + piece[...].astype(jnp.float32)
    value = value * sign_ref[...].astype(jnp.float32)
    value = jnp.concatenate([value[:, b : b + BLOCK] for b in range(0, features, BLOCK)])
    high = value.astype(jnp.bfloat16)
    low = (value - high.astype(jnp.float32)).astype(jnp.bfloat16)
    both = jnp.concatenate([high, low], axis=1)
    turned = jnp.dot(both, matrix_ref[...], preferred_element_type=jnp.float32) * (1.0 / math.sqrt(BLOCK))
    for b in range(features // BLOCK):
        out_ref[:, b * BLOCK : (b + 1) * BLOCK] = turned[b * rows : (b + 1) * rows].astype(jnp.bfloat16)


def rotate(total, arrived, signs):
    return pl.pallas_call(
        functools.partial(rotate_kernel, len(arrived)),
        out_shape=jax.ShapeDtypeStruct(total.shape, jnp.bfloat16),
        in_specs=[vmem()] * (len(arrived) + 3),
        out_specs=vmem(),
        compiler_params=pltpu.CompilerParams(vmem_limit_bytes=16 << 20),
    )(total, *arrived, signs.reshape(1, -1), signs_twice())


def solution(mesh):
    members = mesh.shape["gx"]
    assert members & (members - 1) == 0 and members >= 16

    square = ((4, 2), (2, 4), (6, 6))
    far = []
    mask = members // 2
    while mask > 4:
        far.append((mask, mask))
        mask //= 2
    others = members // 8 - 1

    def swap(value, masks):
        return lax.ppermute(value, "gx", [(i, i ^ masks[i % 2]) for i in range(members)])

    def on_device(tokens, gate_weight, up_weight, down_weight, sign_pattern):
        rows, features = tokens.shape

        away = []
        for masks in far:
            away.append(swap(jnp.concatenate([tokens] + away), masks))
        away = jnp.concatenate(away)
        near = [swap(tokens, m) for m in square]
        gate_w = pltpu.with_memory_space_constraint(gate_weight.T, pltpu.HBM)
        (gate_w,) = load((gate_w,), (True,), gate_w)
        away, gate_w = lax.optimization_barrier((away, gate_w))
        there = [swap(away, m) for m in square[:2]]
        away, near[0] = lax.optimization_barrier((away, near[0]))
        there.append(swap(away, square[2]))
        up_w, down_w = load((up_weight.T, down_weight), (True, False), away)
        there[0], *near = lax.optimization_barrier((there[0], *near))
        early = jnp.concatenate([near[1], near[0], near[2], away, there[0], tokens])
        early_there = swap(early, (1, 1))
        gate_w, up_w, early, *there[1:] = lax.optimization_barrier((gate_w, up_w, early, *there[1:]))
        spans = []
        width = features // SPANS
        for k in range(SPANS):
            span = jnp.concatenate([piece[:, k * width : (k + 1) * width] for piece in there[:0:-1]])
            spans.append((span, swap(span, (1, 1))))
        hidden = hidden_units(gate_w, up_w, (early, early_there), spans)

        count = others * rows
        ends = [3 * rows, 3 * rows + count, 3 * rows + 2 * count, 4 * rows + 2 * count]
        ends += [ends[3] + count, ends[3] + 2 * count]
        own_rows = ((ends[2], ends[3]), (0, ends[0]))
        rest_rows = ((ends[0], ends[2]), (ends[4], ends[5]))
        own, diagonal, rest, *sends = down(hidden, down_w, (own_rows, ((ends[3], ends[4]),), rest_rows))
        diagonal = diagonal + swap(sends[1], (1, 1)).astype(jnp.float32)
        diagonal = swap(diagonal.astype(jnp.bfloat16), square[2])
        rest_there, sends[0] = lax.optimization_barrier((swap(sends[2], (1, 1)), sends[0]))
        rest = rest + rest_there.astype(jnp.float32)
        leave = rest[count:].astype(jnp.bfloat16)
        total = rest[:count]
        for piece in (diagonal, swap(leave[:count], square[0]), swap(leave[count:], square[1])):
            total = total + piece.astype(jnp.float32)
        arrived = []
        for masks in reversed(far):
            split = total.shape[0] // 2 // rows * rows
            piece = swap(total[split:].astype(jnp.bfloat16), masks)
            arrived.append(piece[:rows])
            total = total[:split] + piece[rows:].astype(jnp.float32)

        own = own + swap(sends[0], (1, 1)).astype(jnp.float32)
        own = own[: 2 * rows] + swap(own[2 * rows :].astype(jnp.bfloat16), square[0]).astype(jnp.float32)
        arrived.append(swap(own[rows:].astype(jnp.bfloat16), square[1]))
        return rotate(own[:rows], arrived, sign_pattern)

    placed = (P(("groups", "gx"), None), P(None, "gx"), P(None, "gx"), P("gx", None), P())
    return jax.shard_map(
        on_device, mesh=mesh, in_specs=placed, out_specs=P(("groups", "gx"), None), check_vma=False
    )
```

```python
import functools
import math

import jax
import jax.numpy as jnp
from jax import lax
from jax.experimental import pallas as pl
from jax.experimental.pallas import tpu as pltpu
from jax.sharding import PartitionSpec as P

BLOCK = 128
SPANS = 2
TURNS = 8
NT = (((1,), (1,)), ((), ()))


def vmem():
    return pl.BlockSpec(memory_space=pltpu.VMEM)


def load_kernel(turned, *refs):
    count = len(turned)
    sources, outs = refs[:count], refs[count + 1 : 2 * count + 1]
    staged, sems = refs[2 * count + 1 :]
    tile = staged.shape[1] // (sems.shape[0] - 1)
    copies = []
    for source, out, turn in zip(sources, outs, turned):
        if not turn:
            continue
        for k in range(sems.shape[0] - 1):
            here = slice(k * tile, (k + 1) * tile)
            copies.append((pltpu.make_async_copy(source.at[:, here], staged.at[:, here], sems.at[k]), out, here))
    others = [
        pltpu.make_async_copy(source, out, sems.at[sems.shape[0] - 1])
        for source, out, turn in zip(sources, outs, turned)
        if not turn
    ]
    for copy, _, _ in copies:
        copy.start()
    for copy in others:
        copy.start()
    for copy, out, here in copies:
        copy.wait()
        out[here, :] = staged[:, here].T
    for copy in others:
        copy.wait()


def load(weights, turned, after):
    shapes = [w.shape[::-1] if turn else w.shape for w, turn in zip(weights, turned)]
    size = sum(w.size for w in weights)
    return pl.pallas_call(
        functools.partial(load_kernel, turned),
        out_shape=[jax.ShapeDtypeStruct(shape, weights[0].dtype) for shape in shapes],
        in_specs=[pl.BlockSpec(memory_space=pltpu.HBM)] * len(weights) + [pl.BlockSpec(memory_space=pl.ANY)],
        out_specs=[vmem()] * len(weights),
        scratch_shapes=[
            pltpu.VMEM(weights[0].shape, weights[0].dtype),
            pltpu.SemaphoreType.DMA((TURNS + 1,)),
        ],
        cost_estimate=pl.CostEstimate(flops=0, bytes_accessed=4 * size, transcendentals=0),
        compiler_params=pltpu.CompilerParams(vmem_limit_bytes=16 << 20),
    )(*(pltpu.with_memory_space_constraint(w, pltpu.HBM) for w in weights), after)


def hidden_kernel(start, last, *refs):
    gate_ref, up_ref, near_here, near_there, far_here, far_there, *refs = refs
    sums, outs = refs[: len(refs) - (1 if last else 2)], refs[-1 if last else -2 :]
    width = far_here.shape[1]
    tile = math.gcd(width, 1024)
    gate, up = (ref[...] for ref in sums) if sums else (0.0, 0.0)
    for first in range(0, width, tile):
        here, there = slice(first, first + tile), slice(start + first, start + first + tile)
        rows = jnp.concatenate([near_here[:, there], far_here[:, here], near_there[:, there], far_there[:, here]])
        gate = gate + jnp.dot(rows, gate_ref[there, :], preferred_element_type=jnp.float32)
        up = up + jnp.dot(rows, up_ref[there, :], preferred_element_type=jnp.float32)
    if last:
        outs[0][...] = (gate / (1.0 + jnp.exp(-gate)) * up).astype(jnp.bfloat16)
    else:
        outs[0][...], outs[1][...] = gate, up


def hidden_units(gate_w, up_w, near, spans):
    features, units = gate_w.shape
    count = 2 * (near[0].shape[0] + spans[0][0].shape[0])
    sums, start = (), 0
    for span in spans:
        width = span[0].shape[1]
        last = start + width == features
        total = jax.ShapeDtypeStruct((count, units), jnp.float32)
        sums = pl.pallas_call(
            functools.partial(hidden_kernel, start, last),
            out_shape=(jax.ShapeDtypeStruct((count, units), jnp.bfloat16),) if last else (total, total),
            in_specs=[vmem()] * (6 + len(sums)),
            out_specs=(vmem(),) * (1 if last else 2),
            cost_estimate=pl.CostEstimate(
                flops=4 * units * count * width, bytes_accessed=4 * units * width, transcendentals=0
            ),
            compiler_params=pltpu.CompilerParams(vmem_limit_bytes=24 << 20),
        )(gate_w, up_w, *near, *span, *sums)
        start += width
    return sums[0]


def down_kernel(spans, hidden_ref, down_ref, *outs):
    half, features = hidden_ref.shape[0] // 2, down_ref.shape[1]
    tile = math.gcd(features, 512)
    for first in range(0, features, tile):
        here = slice(first, first + tile)
        part = jnp.dot(hidden_ref[...], down_ref[:, here], preferred_element_type=jnp.float32)
        for k, out in enumerate(outs):
            begin = 0 if k < len(spans) else half
            rows = [part[begin + first : begin + last] for first, last in spans[k % len(spans)]]
            out[:, here] = jnp.concatenate(rows).astype(out.dtype)


def down(hidden, down_w, spans):
    units, features = down_w.shape
    counts = [sum(last - first for first, last in span) for span in spans]
    return pl.pallas_call(
        functools.partial(down_kernel, spans),
        out_shape=[jax.ShapeDtypeStruct((count, features), jnp.float32) for count in counts]
        + [jax.ShapeDtypeStruct((count, features), jnp.bfloat16) for count in counts],
        in_specs=[vmem()] * 2,
        out_specs=[vmem()] * (2 * len(counts)),
        cost_estimate=pl.CostEstimate(
            flops=2 * hidden.size * features, bytes_accessed=2 * units * features, transcendentals=0
        ),
        compiler_params=pltpu.CompilerParams(vmem_limit_bytes=24 << 20),
    )(hidden, down_w)


def signs_twice():
    index = jnp.arange(BLOCK, dtype=jnp.int32)
    common = index[:, None] & index[None, :]
    for shift in (4, 2, 1):
        common = common ^ (common >> shift)
    signs = (1 - 2 * (common & 1)).astype(jnp.bfloat16)
    return jnp.concatenate([signs, signs])


def rotate_kernel(count, *refs):
    total_ref, *arrived = refs[: count + 1]
    sign_ref, matrix_ref, out_ref = refs[count + 1 :]
    rows, features = total_ref.shape
    value = total_ref[...]
    for piece in arrived:
        value = value + piece[...].astype(jnp.float32)
    value = value * sign_ref[...].astype(jnp.float32)
    value = jnp.concatenate([value[:, b : b + BLOCK] for b in range(0, features, BLOCK)])
    high = value.astype(jnp.bfloat16)
    low = (value - high.astype(jnp.float32)).astype(jnp.bfloat16)
    both = jnp.concatenate([high, low], axis=1)
    turned = jnp.dot(both, matrix_ref[...], preferred_element_type=jnp.float32) * (1.0 / math.sqrt(BLOCK))
    for b in range(features // BLOCK):
        out_ref[:, b * BLOCK : (b + 1) * BLOCK] = turned[b * rows : (b + 1) * rows].astype(jnp.bfloat16)


def rotate(total, arrived, signs):
    return pl.pallas_call(
        functools.partial(rotate_kernel, len(arrived)),
        out_shape=jax.ShapeDtypeStruct(total.shape, jnp.bfloat16),
        in_specs=[vmem()] * (len(arrived) + 3),
        out_specs=vmem(),
        compiler_params=pltpu.CompilerParams(vmem_limit_bytes=16 << 20),
    )(total, *arrived, signs.reshape(1, -1), signs_twice())


def solution(mesh):
    members = mesh.shape["gx"]
    assert members & (members - 1) == 0 and members >= 16

    square = ((4, 2), (2, 4), (6, 6))
    far = []
    mask = members // 2
    while mask > 8:
        far.append((mask, mask))
        mask //= 2
    far.append((8, 12))
    others = members // 8 - 1

    def swap(value, masks):
        return lax.ppermute(value, "gx", [(i, i ^ masks[i % 2]) for i in range(members)])

    def on_device(tokens, gate_weight, up_weight, down_weight, sign_pattern):
        rows, features = tokens.shape

        away = []
        for masks in far:
            away.append(swap(jnp.concatenate([tokens] + away), masks))
        away = jnp.concatenate(away)
        near = [swap(tokens, m) for m in square]
        gate_w = pltpu.with_memory_space_constraint(gate_weight.T, pltpu.HBM)
        (gate_w,) = load((gate_w,), (True,), gate_w)
        away, gate_w = lax.optimization_barrier((away, gate_w))
        there = [swap(away, m) for m in square[:2]]
        away, near[0] = lax.optimization_barrier((away, near[0]))
        there.append(swap(away, square[2]))
        up_w, down_w = load((up_weight.T, down_weight), (True, False), away)
        there[0], *near = lax.optimization_barrier((there[0], *near))
        early = jnp.concatenate([near[1], near[0], near[2], away, there[0], tokens])
        early_there = swap(early, (1, 1))
        gate_w, up_w, early, *there[1:] = lax.optimization_barrier((gate_w, up_w, early, *there[1:]))
        spans = []
        width = features // SPANS
        for k in range(SPANS):
            span = jnp.concatenate([piece[:, k * width : (k + 1) * width] for piece in there[:0:-1]])
            spans.append((span, swap(span, (1, 1))))
        hidden = hidden_units(gate_w, up_w, (early, early_there), spans)

        count = others * rows
        ends = [3 * rows, 3 * rows + count, 3 * rows + 2 * count, 4 * rows + 2 * count]
        ends += [ends[3] + count, ends[3] + 2 * count]
        own_rows = ((ends[2], ends[3]), (0, ends[0]))
        rest_rows = ((ends[0], ends[2]), (ends[4], ends[5]))
        own, diagonal, rest, *sends = down(hidden, down_w, (own_rows, ((ends[3], ends[4]),), rest_rows))
        diagonal = diagonal + swap(sends[1], (1, 1)).astype(jnp.float32)
        diagonal = swap(diagonal.astype(jnp.bfloat16), square[2])
        rest_there, sends[0] = lax.optimization_barrier((swap(sends[2], (1, 1)), sends[0]))
        rest = rest + rest_there.astype(jnp.float32)
        leave = rest[count:].astype(jnp.bfloat16)
        total = rest[:count]
        for piece in (diagonal, swap(leave[:count], square[0]), swap(leave[count:], square[1])):
            total = total + piece.astype(jnp.float32)
        arrived = []
        for masks in reversed(far):
            split = total.shape[0] // 2 // rows * rows
            piece = swap(total[split:].astype(jnp.bfloat16), masks)
            arrived.append(piece[:rows])
            total = total[:split] + piece[rows:].astype(jnp.float32)

        own = own + swap(sends[0], (1, 1)).astype(jnp.float32)
        own = own[: 2 * rows] + swap(own[2 * rows :].astype(jnp.bfloat16), square[0]).astype(jnp.float32)
        arrived.append(swap(own[rows:].astype(jnp.bfloat16), square[1]))
        return rotate(own[:rows], arrived, sign_pattern)

    placed = (P(("groups", "gx"), None), P(None, "gx"), P(None, "gx"), P("gx", None), P())
    return jax.shard_map(
        on_device, mesh=mesh, in_specs=placed, out_specs=P(("groups", "gx"), None), check_vma=False
    )
```

```python
import functools
import math

import jax
import jax.numpy as jnp
from jax import lax
from jax.experimental import pallas as pl
from jax.experimental.pallas import tpu as pltpu
from jax.sharding import PartitionSpec as P

BLOCK = 128
SPANS = 2
TURNS = 8
NT = (((1,), (1,)), ((), ()))


def vmem():
    return pl.BlockSpec(memory_space=pltpu.VMEM)


def load_kernel(turned, *refs):
    count = len(turned)
    sources, outs = refs[:count], refs[count + 1 : 2 * count + 1]
    staged, sems = refs[2 * count + 1 :]
    tile = staged.shape[1] // (sems.shape[0] - 1)
    copies = []
    for source, out, turn in zip(sources, outs, turned):
        if not turn:
            continue
        for k in range(sems.shape[0] - 1):
            here = slice(k * tile, (k + 1) * tile)
            copies.append((pltpu.make_async_copy(source.at[:, here], staged.at[:, here], sems.at[k]), out, here))
    others = [
        pltpu.make_async_copy(source, out, sems.at[sems.shape[0] - 1])
        for source, out, turn in zip(sources, outs, turned)
        if not turn
    ]
    for copy, _, _ in copies:
        copy.start()
    for copy in others:
        copy.start()
    for copy, out, here in copies:
        copy.wait()
        out[here, :] = staged[:, here].T
    for copy in others:
        copy.wait()


def load(weights, turned, after):
    shapes = [w.shape[::-1] if turn else w.shape for w, turn in zip(weights, turned)]
    size = sum(w.size for w in weights)
    return pl.pallas_call(
        functools.partial(load_kernel, turned),
        out_shape=[jax.ShapeDtypeStruct(shape, weights[0].dtype) for shape in shapes],
        in_specs=[pl.BlockSpec(memory_space=pltpu.HBM)] * len(weights) + [pl.BlockSpec(memory_space=pl.ANY)],
        out_specs=[vmem()] * len(weights),
        scratch_shapes=[
            pltpu.VMEM(weights[0].shape, weights[0].dtype),
            pltpu.SemaphoreType.DMA((TURNS + 1,)),
        ],
        cost_estimate=pl.CostEstimate(flops=0, bytes_accessed=4 * size, transcendentals=0),
        compiler_params=pltpu.CompilerParams(vmem_limit_bytes=16 << 20),
    )(*(pltpu.with_memory_space_constraint(w, pltpu.HBM) for w in weights), after)


def hidden_kernel(start, last, *refs):
    gate_ref, up_ref, near_here, near_there, far_here, far_there, *refs = refs
    sums, outs = refs[: len(refs) - (1 if last else 2)], refs[-1 if last else -2 :]
    width = far_here.shape[1]
    tile = math.gcd(width, 1024)
    gate, up = (ref[...] for ref in sums) if sums else (0.0, 0.0)
    for first in range(0, width, tile):
        here, there = slice(first, first + tile), slice(start + first, start + first + tile)
        rows = jnp.concatenate([near_here[:, there], far_here[:, here], near_there[:, there], far_there[:, here]])
        gate = gate + jnp.dot(rows, gate_ref[there, :], preferred_element_type=jnp.float32)
        up = up + jnp.dot(rows, up_ref[there, :], preferred_element_type=jnp.float32)
    if last:
        outs[0][...] = (gate / (1.0 + jnp.exp(-gate)) * up).astype(jnp.bfloat16)
    else:
        outs[0][...], outs[1][...] = gate, up


def hidden_units(gate_w, up_w, near, spans):
    features, units = gate_w.shape
    count = 2 * (near[0].shape[0] + spans[0][0].shape[0])
    sums, start = (), 0
    for span in spans:
        width = span[0].shape[1]
        last = start + width == features
        total = jax.ShapeDtypeStruct((count, units), jnp.float32)
        sums = pl.pallas_call(
            functools.partial(hidden_kernel, start, last),
            out_shape=(jax.ShapeDtypeStruct((count, units), jnp.bfloat16),) if last else (total, total),
            in_specs=[vmem()] * (6 + len(sums)),
            out_specs=(vmem(),) * (1 if last else 2),
            cost_estimate=pl.CostEstimate(
                flops=4 * units * count * width, bytes_accessed=4 * units * width, transcendentals=0
            ),
            compiler_params=pltpu.CompilerParams(vmem_limit_bytes=24 << 20),
        )(gate_w, up_w, *near, *span, *sums)
        start += width
    return sums[0]


def down_kernel(spans, hidden_ref, down_ref, *outs):
    half, features = hidden_ref.shape[0] // 2, down_ref.shape[1]
    tile = math.gcd(features, 512)
    for first in range(0, features, tile):
        here = slice(first, first + tile)
        part = jnp.dot(hidden_ref[...], down_ref[:, here], preferred_element_type=jnp.float32)
        for k, out in enumerate(outs):
            begin = 0 if k < len(spans) else half
            rows = [part[begin + first : begin + last] for first, last in spans[k % len(spans)]]
            out[:, here] = jnp.concatenate(rows).astype(out.dtype)


def down(hidden, down_w, spans):
    units, features = down_w.shape
    counts = [sum(last - first for first, last in span) for span in spans]
    return pl.pallas_call(
        functools.partial(down_kernel, spans),
        out_shape=[jax.ShapeDtypeStruct((count, features), jnp.float32) for count in counts]
        + [jax.ShapeDtypeStruct((count, features), jnp.bfloat16) for count in counts],
        in_specs=[vmem()] * 2,
        out_specs=[vmem()] * (2 * len(counts)),
        cost_estimate=pl.CostEstimate(
            flops=2 * hidden.size * features, bytes_accessed=2 * units * features, transcendentals=0
        ),
        compiler_params=pltpu.CompilerParams(vmem_limit_bytes=24 << 20),
    )(hidden, down_w)


def signs_twice():
    index = jnp.arange(BLOCK, dtype=jnp.int32)
    common = index[:, None] & index[None, :]
    for shift in (4, 2, 1):
        common = common ^ (common >> shift)
    signs = (1 - 2 * (common & 1)).astype(jnp.bfloat16)
    return jnp.concatenate([signs, signs])


def rotate_kernel(count, *refs):
    total_ref, *arrived = refs[: count + 1]
    sign_ref, matrix_ref, out_ref = refs[count + 1 :]
    rows, features = total_ref.shape
    value = total_ref[...]
    for piece in arrived:
        value = value + piece[...].astype(jnp.float32)
    value = value * sign_ref[...].astype(jnp.float32)
    value = jnp.concatenate([value[:, b : b + BLOCK] for b in range(0, features, BLOCK)])
    high = value.astype(jnp.bfloat16)
    low = (value - high.astype(jnp.float32)).astype(jnp.bfloat16)
    both = jnp.concatenate([high, low], axis=1)
    turned = jnp.dot(both, matrix_ref[...], preferred_element_type=jnp.float32) * (1.0 / math.sqrt(BLOCK))
    for b in range(features // BLOCK):
        out_ref[:, b * BLOCK : (b + 1) * BLOCK] = turned[b * rows : (b + 1) * rows].astype(jnp.bfloat16)


def rotate(total, arrived, signs):
    return pl.pallas_call(
        functools.partial(rotate_kernel, len(arrived)),
        out_shape=jax.ShapeDtypeStruct(total.shape, jnp.bfloat16),
        in_specs=[vmem()] * (len(arrived) + 3),
        out_specs=vmem(),
        compiler_params=pltpu.CompilerParams(vmem_limit_bytes=16 << 20),
    )(total, *arrived, signs.reshape(1, -1), signs_twice())


def solution(mesh):
    members = mesh.shape["gx"]
    assert members & (members - 1) == 0 and members >= 16

    square = ((4, 2), (2, 4), (6, 6))
    far = []
    mask = members // 2
    while mask > 8:
        far.append((mask, mask))
        mask //= 2
    far.append((12, 8))
    others = members // 8 - 1

    def swap(value, masks):
        return lax.ppermute(value, "gx", [(i, i ^ masks[i % 2]) for i in range(members)])

    def on_device(tokens, gate_weight, up_weight, down_weight, sign_pattern):
        rows, features = tokens.shape

        away = []
        for masks in far:
            away.append(swap(jnp.concatenate([tokens] + away), masks))
        away = jnp.concatenate(away)
        near = [swap(tokens, m) for m in square]
        gate_w = pltpu.with_memory_space_constraint(gate_weight.T, pltpu.HBM)
        (gate_w,) = load((gate_w,), (True,), gate_w)
        away, gate_w = lax.optimization_barrier((away, gate_w))
        there = [swap(away, m) for m in square[:2]]
        away, near[0] = lax.optimization_barrier((away, near[0]))
        there.append(swap(away, square[2]))
        up_w, down_w = load((up_weight.T, down_weight), (True, False), away)
        there[0], *near = lax.optimization_barrier((there[0], *near))
        early = jnp.concatenate([near[1], near[0], near[2], away, there[0], tokens])
        early_there = swap(early, (1, 1))
        gate_w, up_w, early, *there[1:] = lax.optimization_barrier((gate_w, up_w, early, *there[1:]))
        spans = []
        width = features // SPANS
        for k in range(SPANS):
            span = jnp.concatenate([piece[:, k * width : (k + 1) * width] for piece in there[:0:-1]])
            spans.append((span, swap(span, (1, 1))))
        hidden = hidden_units(gate_w, up_w, (early, early_there), spans)

        count = others * rows
        ends = [3 * rows, 3 * rows + count, 3 * rows + 2 * count, 4 * rows + 2 * count]
        ends += [ends[3] + count, ends[3] + 2 * count]
        own_rows = ((ends[2], ends[3]), (0, ends[0]))
        rest_rows = ((ends[0], ends[2]), (ends[4], ends[5]))
        own, diagonal, rest, *sends = down(hidden, down_w, (own_rows, ((ends[3], ends[4]),), rest_rows))
        diagonal = diagonal + swap(sends[1], (1, 1)).astype(jnp.float32)
        diagonal = swap(diagonal.astype(jnp.bfloat16), square[2])
        rest_there, sends[0] = lax.optimization_barrier((swap(sends[2], (1, 1)), sends[0]))
        rest = rest + rest_there.astype(jnp.float32)
        leave = rest[count:].astype(jnp.bfloat16)
        total = rest[:count]
        for piece in (diagonal, swap(leave[:count], square[0]), swap(leave[count:], square[1])):
            total = total + piece.astype(jnp.float32)
        arrived = []
        for masks in reversed(far):
            split = total.shape[0] // 2 // rows * rows
            piece = swap(total[split:].astype(jnp.bfloat16), masks)
            arrived.append(piece[:rows])
            total = total[:split] + piece[rows:].astype(jnp.float32)

        own = own + swap(sends[0], (1, 1)).astype(jnp.float32)
        own = own[: 2 * rows] + swap(own[2 * rows :].astype(jnp.bfloat16), square[0]).astype(jnp.float32)
        arrived.append(swap(own[rows:].astype(jnp.bfloat16), square[1]))
        return rotate(own[:rows], arrived, sign_pattern)

    placed = (P(("groups", "gx"), None), P(None, "gx"), P(None, "gx"), P("gx", None), P())
    return jax.shard_map(
        on_device, mesh=mesh, in_specs=placed, out_specs=P(("groups", "gx"), None), check_vma=False
    )
```

```python
import functools
import math

import jax
import jax.numpy as jnp
from jax import lax
from jax.experimental import pallas as pl
from jax.experimental.pallas import tpu as pltpu
from jax.sharding import PartitionSpec as P

BLOCK = 128
SPANS = 2
TURNS = 8
NT = (((1,), (1,)), ((), ()))


def vmem():
    return pl.BlockSpec(memory_space=pltpu.VMEM)


def load_kernel(turned, *refs):
    count = len(turned)
    sources, outs = refs[:count], refs[count + 1 : 2 * count + 1]
    staged, sems = refs[2 * count + 1 :]
    tile = staged.shape[1] // (sems.shape[0] - 1)
    copies = []
    for source, out, turn in zip(sources, outs, turned):
        if not turn:
            continue
        for k in range(sems.shape[0] - 1):
            here = slice(k * tile, (k + 1) * tile)
            copies.append((pltpu.make_async_copy(source.at[:, here], staged.at[:, here], sems.at[k]), out, here))
    others = [
        pltpu.make_async_copy(source, out, sems.at[sems.shape[0] - 1])
        for source, out, turn in zip(sources, outs, turned)
        if not turn
    ]
    for copy, _, _ in copies:
        copy.start()
    for copy in others:
        copy.start()
    for copy, out, here in copies:
        copy.wait()
        out[here, :] = staged[:, here].T
    for copy in others:
        copy.wait()


def load(weights, turned, after):
    shapes = [w.shape[::-1] if turn else w.shape for w, turn in zip(weights, turned)]
    size = sum(w.size for w in weights)
    return pl.pallas_call(
        functools.partial(load_kernel, turned),
        out_shape=[jax.ShapeDtypeStruct(shape, weights[0].dtype) for shape in shapes],
        in_specs=[pl.BlockSpec(memory_space=pltpu.HBM)] * len(weights) + [pl.BlockSpec(memory_space=pl.ANY)],
        out_specs=[vmem()] * len(weights),
        scratch_shapes=[
            pltpu.VMEM(weights[0].shape, weights[0].dtype),
            pltpu.SemaphoreType.DMA((TURNS + 1,)),
        ],
        cost_estimate=pl.CostEstimate(flops=0, bytes_accessed=4 * size, transcendentals=0),
        compiler_params=pltpu.CompilerParams(vmem_limit_bytes=16 << 20),
    )(*(pltpu.with_memory_space_constraint(w, pltpu.HBM) for w in weights), after)


def hidden_kernel(start, last, *refs):
    gate_ref, up_ref, near_here, near_there, far_here, far_there, *refs = refs
    sums, outs = refs[: len(refs) - (1 if last else 2)], refs[-1 if last else -2 :]
    width = far_here.shape[1]
    tile = math.gcd(width, 1024)
    gate, up = (ref[...] for ref in sums) if sums else (0.0, 0.0)
    for first in range(0, width, tile):
        here, there = slice(first, first + tile), slice(start + first, start + first + tile)
        rows = jnp.concatenate([near_here[:, there], far_here[:, here], near_there[:, there], far_there[:, here]])
        gate = gate + jnp.dot(rows, gate_ref[there, :], preferred_element_type=jnp.float32)
        up = up + jnp.dot(rows, up_ref[there, :], preferred_element_type=jnp.float32)
    if last:
        outs[0][...] = (gate / (1.0 + jnp.exp(-gate)) * up).astype(jnp.bfloat16)
    else:
        outs[0][...], outs[1][...] = gate, up


def hidden_units(gate_w, up_w, near, spans):
    features, units = gate_w.shape
    count = 2 * (near[0].shape[0] + spans[0][0].shape[0])
    sums, start = (), 0
    for span in spans:
        width = span[0].shape[1]
        last = start + width == features
        total = jax.ShapeDtypeStruct((count, units), jnp.float32)
        sums = pl.pallas_call(
            functools.partial(hidden_kernel, start, last),
            out_shape=(jax.ShapeDtypeStruct((count, units), jnp.bfloat16),) if last else (total, total),
            in_specs=[vmem()] * (6 + len(sums)),
            out_specs=(vmem(),) * (1 if last else 2),
            cost_estimate=pl.CostEstimate(
                flops=4 * units * count * width, bytes_accessed=4 * units * width, transcendentals=0
            ),
            compiler_params=pltpu.CompilerParams(vmem_limit_bytes=24 << 20),
        )(gate_w, up_w, *near, *span, *sums)
        start += width
    return sums[0]


def down_kernel(spans, hidden_ref, down_ref, *outs):
    half, features = hidden_ref.shape[0] // 2, down_ref.shape[1]
    tile = math.gcd(features, 512)
    for first in range(0, features, tile):
        here = slice(first, first + tile)
        part = jnp.dot(hidden_ref[...], down_ref[:, here], preferred_element_type=jnp.float32)
        for k, out in enumerate(outs):
            begin = 0 if k < len(spans) else half
            rows = [part[begin + first : begin + last] for first, last in spans[k % len(spans)]]
            out[:, here] = jnp.concatenate(rows).astype(out.dtype)


def down(hidden, down_w, spans):
    units, features = down_w.shape
    counts = [sum(last - first for first, last in span) for span in spans]
    return pl.pallas_call(
        functools.partial(down_kernel, spans),
        out_shape=[jax.ShapeDtypeStruct((count, features), jnp.float32) for count in counts]
        + [jax.ShapeDtypeStruct((count, features), jnp.bfloat16) for count in counts],
        in_specs=[vmem()] * 2,
        out_specs=[vmem()] * (2 * len(counts)),
        cost_estimate=pl.CostEstimate(
            flops=2 * hidden.size * features, bytes_accessed=2 * units * features, transcendentals=0
        ),
        compiler_params=pltpu.CompilerParams(vmem_limit_bytes=24 << 20),
    )(hidden, down_w)


def signs_twice():
    index = jnp.arange(BLOCK, dtype=jnp.int32)
    common = index[:, None] & index[None, :]
    for shift in (4, 2, 1):
        common = common ^ (common >> shift)
    signs = (1 - 2 * (common & 1)).astype(jnp.bfloat16)
    return jnp.concatenate([signs, signs])


def rotate_kernel(count, *refs):
    total_ref, *arrived = refs[: count + 1]
    sign_ref, matrix_ref, out_ref = refs[count + 1 :]
    rows, features = total_ref.shape
    value = total_ref[...]
    for piece in arrived:
        value = value + piece[...].astype(jnp.float32)
    value = value * sign_ref[...].astype(jnp.float32)
    value = jnp.concatenate([value[:, b : b + BLOCK] for b in range(0, features, BLOCK)])
    high = value.astype(jnp.bfloat16)
    low = (value - high.astype(jnp.float32)).astype(jnp.bfloat16)
    both = jnp.concatenate([high, low], axis=1)
    turned = jnp.dot(both, matrix_ref[...], preferred_element_type=jnp.float32) * (1.0 / math.sqrt(BLOCK))
    for b in range(features // BLOCK):
        out_ref[:, b * BLOCK : (b + 1) * BLOCK] = turned[b * rows : (b + 1) * rows].astype(jnp.bfloat16)


def rotate(total, arrived, signs):
    return pl.pallas_call(
        functools.partial(rotate_kernel, len(arrived)),
        out_shape=jax.ShapeDtypeStruct(total.shape, jnp.bfloat16),
        in_specs=[vmem()] * (len(arrived) + 3),
        out_specs=vmem(),
        compiler_params=pltpu.CompilerParams(vmem_limit_bytes=16 << 20),
    )(total, *arrived, signs.reshape(1, -1), signs_twice())


def solution(mesh):
    members = mesh.shape["gx"]
    assert members & (members - 1) == 0 and members >= 16

    square = ((4, 2), (2, 4), (6, 6))
    far = []
    mask = members // 2
    while mask > 8:
        far.append((mask, mask))
        mask //= 2
    far.append((12, 8))
    others = members // 8 - 1

    def swap(value, masks):
        return lax.ppermute(value, "gx", [(i, i ^ masks[i % 2]) for i in range(members)])

    def on_device(tokens, gate_weight, up_weight, down_weight, sign_pattern):
        rows, features = tokens.shape

        away = []
        for masks in far:
            away.append(swap(jnp.concatenate([tokens] + away), masks))
        away = jnp.concatenate(away)
        near = [swap(tokens, m) for m in square]
        gate_w = pltpu.with_memory_space_constraint(gate_weight.T, pltpu.HBM)
        (gate_w,) = load((gate_w,), (True,), gate_w)
        away, gate_w = lax.optimization_barrier((away, gate_w))
        there = [None] * 3
        for k in (2, 0):
            there[k] = swap(away, square[k])
        away, near[0] = lax.optimization_barrier((away, near[0]))
        there[1] = swap(away, square[1])
        up_w, down_w = load((up_weight.T, down_weight), (True, False), away)
        there[0], *near = lax.optimization_barrier((there[0], *near))
        early = jnp.concatenate([near[1], near[0], near[2], away, there[0], tokens])
        early_there = swap(early, (1, 1))
        gate_w, up_w, early, *there[1:] = lax.optimization_barrier((gate_w, up_w, early, *there[1:]))
        spans = []
        width = features // SPANS
        for k in range(SPANS):
            span = jnp.concatenate([piece[:, k * width : (k + 1) * width] for piece in there[:0:-1]])
            spans.append((span, swap(span, (1, 1))))
        hidden = hidden_units(gate_w, up_w, (early, early_there), spans)

        count = others * rows
        ends = [3 * rows, 3 * rows + count, 3 * rows + 2 * count, 4 * rows + 2 * count]
        ends += [ends[3] + count, ends[3] + 2 * count]
        own_rows = ((ends[2], ends[3]), (0, ends[0]))
        rest_rows = ((ends[0], ends[2]), (ends[4], ends[5]))
        own, diagonal, rest, *sends = down(hidden, down_w, (own_rows, ((ends[3], ends[4]),), rest_rows))
        diagonal = diagonal + swap(sends[1], (1, 1)).astype(jnp.float32)
        diagonal = swap(diagonal.astype(jnp.bfloat16), square[2])
        rest_there, sends[0] = lax.optimization_barrier((swap(sends[2], (1, 1)), sends[0]))
        rest = rest + rest_there.astype(jnp.float32)
        leave = rest[count:].astype(jnp.bfloat16)
        total = rest[:count]
        for piece in (diagonal, swap(leave[:count], square[0]), swap(leave[count:], square[1])):
            total = total + piece.astype(jnp.float32)
        arrived = []
        for masks in reversed(far):
            split = total.shape[0] // 2 // rows * rows
            piece = swap(total[split:].astype(jnp.bfloat16), masks)
            arrived.append(piece[:rows])
            total = total[:split] + piece[rows:].astype(jnp.float32)

        own = own + swap(sends[0], (1, 1)).astype(jnp.float32)
        own = own[: 2 * rows] + swap(own[2 * rows :].astype(jnp.bfloat16), square[0]).astype(jnp.float32)
        arrived.append(swap(own[rows:].astype(jnp.bfloat16), square[1]))
        return rotate(own[:rows], arrived, sign_pattern)

    placed = (P(("groups", "gx"), None), P(None, "gx"), P(None, "gx"), P("gx", None), P())
    return jax.shard_map(
        on_device, mesh=mesh, in_specs=placed, out_specs=P(("groups", "gx"), None), check_vma=False
    )
```

```python
import functools
import math

import jax
import jax.numpy as jnp
from jax import lax
from jax.experimental import pallas as pl
from jax.experimental.pallas import tpu as pltpu
from jax.sharding import PartitionSpec as P

BLOCK = 128
SPANS = 2
TURNS = 8
NT = (((1,), (1,)), ((), ()))


def vmem():
    return pl.BlockSpec(memory_space=pltpu.VMEM)


def load_kernel(turned, *refs):
    count = len(turned)
    sources, outs = refs[:count], refs[count + 1 : 2 * count + 1]
    staged, sems = refs[2 * count + 1 :]
    tile = staged.shape[1] // (sems.shape[0] - 1)
    copies = []
    for source, out, turn in zip(sources, outs, turned):
        if not turn:
            continue
        for k in range(sems.shape[0] - 1):
            here = slice(k * tile, (k + 1) * tile)
            copies.append((pltpu.make_async_copy(source.at[:, here], staged.at[:, here], sems.at[k]), out, here))
    others = [
        pltpu.make_async_copy(source, out, sems.at[sems.shape[0] - 1])
        for source, out, turn in zip(sources, outs, turned)
        if not turn
    ]
    for copy, _, _ in copies:
        copy.start()
    for copy in others:
        copy.start()
    for copy, out, here in copies:
        copy.wait()
        out[here, :] = staged[:, here].T
    for copy in others:
        copy.wait()


def load(weights, turned, after):
    shapes = [w.shape[::-1] if turn else w.shape for w, turn in zip(weights, turned)]
    size = sum(w.size for w in weights)
    return pl.pallas_call(
        functools.partial(load_kernel, turned),
        out_shape=[jax.ShapeDtypeStruct(shape, weights[0].dtype) for shape in shapes],
        in_specs=[pl.BlockSpec(memory_space=pltpu.HBM)] * len(weights) + [pl.BlockSpec(memory_space=pl.ANY)],
        out_specs=[vmem()] * len(weights),
        scratch_shapes=[
            pltpu.VMEM(weights[0].shape, weights[0].dtype),
            pltpu.SemaphoreType.DMA((TURNS + 1,)),
        ],
        cost_estimate=pl.CostEstimate(flops=0, bytes_accessed=4 * size, transcendentals=0),
        compiler_params=pltpu.CompilerParams(vmem_limit_bytes=16 << 20),
    )(*(pltpu.with_memory_space_constraint(w, pltpu.HBM) for w in weights), after)


def hidden_kernel(start, last, *refs):
    gate_ref, up_ref, near_here, near_there, far_here, far_there, *refs = refs
    sums, outs = refs[: len(refs) - (1 if last else 2)], refs[-1 if last else -2 :]
    width = far_here.shape[1]
    tile = math.gcd(width, 1024)
    gate, up = (ref[...] for ref in sums) if sums else (0.0, 0.0)
    for first in range(0, width, tile):
        here, there = slice(first, first + tile), slice(start + first, start + first + tile)
        rows = jnp.concatenate([near_here[:, there], far_here[:, here], near_there[:, there], far_there[:, here]])
        gate = gate + jnp.dot(rows, gate_ref[there, :], preferred_element_type=jnp.float32)
        up = up + jnp.dot(rows, up_ref[there, :], preferred_element_type=jnp.float32)
    if last:
        outs[0][...] = (gate / (1.0 + jnp.exp(-gate)) * up).astype(jnp.bfloat16)
    else:
        outs[0][...], outs[1][...] = gate, up


def hidden_units(gate_w, up_w, near, spans):
    features, units = gate_w.shape
    count = 2 * (near[0].shape[0] + spans[0][0].shape[0])
    sums, start = (), 0
    for span in spans:
        width = span[0].shape[1]
        last = start + width == features
        total = jax.ShapeDtypeStruct((count, units), jnp.float32)
        sums = pl.pallas_call(
            functools.partial(hidden_kernel, start, last),
            out_shape=(jax.ShapeDtypeStruct((count, units), jnp.bfloat16),) if last else (total, total),
            in_specs=[vmem()] * (6 + len(sums)),
            out_specs=(vmem(),) * (1 if last else 2),
            cost_estimate=pl.CostEstimate(
                flops=4 * units * count * width, bytes_accessed=4 * units * width, transcendentals=0
            ),
            compiler_params=pltpu.CompilerParams(vmem_limit_bytes=24 << 20),
        )(gate_w, up_w, *near, *span, *sums)
        start += width
    return sums[0]


def down_kernel(spans, hidden_ref, down_ref, *outs):
    half, features = hidden_ref.shape[0] // 2, down_ref.shape[1]
    tile = math.gcd(features, 512)
    for first in range(0, features, tile):
        here = slice(first, first + tile)
        part = jnp.dot(hidden_ref[...], down_ref[:, here], preferred_element_type=jnp.float32)
        for k, out in enumerate(outs):
            begin = 0 if k < len(spans) else half
            rows = [part[begin + first : begin + last] for first, last in spans[k % len(spans)]]
            out[:, here] = jnp.concatenate(rows).astype(out.dtype)


def down(hidden, down_w, spans):
    units, features = down_w.shape
    counts = [sum(last - first for first, last in span) for span in spans]
    return pl.pallas_call(
        functools.partial(down_kernel, spans),
        out_shape=[jax.ShapeDtypeStruct((count, features), jnp.float32) for count in counts]
        + [jax.ShapeDtypeStruct((count, features), jnp.bfloat16) for count in counts],
        in_specs=[vmem()] * 2,
        out_specs=[vmem()] * (2 * len(counts)),
        cost_estimate=pl.CostEstimate(
            flops=2 * hidden.size * features, bytes_accessed=2 * units * features, transcendentals=0
        ),
        compiler_params=pltpu.CompilerParams(vmem_limit_bytes=24 << 20),
    )(hidden, down_w)


def signs_twice():
    index = jnp.arange(BLOCK, dtype=jnp.int32)
    common = index[:, None] & index[None, :]
    for shift in (4, 2, 1):
        common = common ^ (common >> shift)
    signs = (1 - 2 * (common & 1)).astype(jnp.bfloat16)
    return jnp.concatenate([signs, signs])


def rotate_kernel(count, *refs):
    total_ref, *arrived = refs[: count + 1]
    sign_ref, matrix_ref, out_ref = refs[count + 1 :]
    rows, features = total_ref.shape
    value = total_ref[...]
    for piece in arrived:
        value = value + piece[...].astype(jnp.float32)
    value = value * sign_ref[...].astype(jnp.float32)
    value = jnp.concatenate([value[:, b : b + BLOCK] for b in range(0, features, BLOCK)])
    high = value.astype(jnp.bfloat16)
    low = (value - high.astype(jnp.float32)).astype(jnp.bfloat16)
    both = jnp.concatenate([high, low], axis=1)
    turned = jnp.dot(both, matrix_ref[...], preferred_element_type=jnp.float32) * (1.0 / math.sqrt(BLOCK))
    for b in range(features // BLOCK):
        out_ref[:, b * BLOCK : (b + 1) * BLOCK] = turned[b * rows : (b + 1) * rows].astype(jnp.bfloat16)


def rotate(total, arrived, signs):
    return pl.pallas_call(
        functools.partial(rotate_kernel, len(arrived)),
        out_shape=jax.ShapeDtypeStruct(total.shape, jnp.bfloat16),
        in_specs=[vmem()] * (len(arrived) + 3),
        out_specs=vmem(),
        compiler_params=pltpu.CompilerParams(vmem_limit_bytes=16 << 20),
    )(total, *arrived, signs.reshape(1, -1), signs_twice())


def solution(mesh):
    members = mesh.shape["gx"]
    assert members & (members - 1) == 0 and members >= 16

    square = ((4, 2), (2, 4), (6, 6))
    far = []
    mask = members // 2
    while mask > 8:
        far.append((mask, mask))
        mask //= 2
    far.append((12, 8))
    others = members // 8 - 1

    def swap(value, masks):
        return lax.ppermute(value, "gx", [(i, i ^ masks[i % 2]) for i in range(members)])

    def on_device(tokens, gate_weight, up_weight, down_weight, sign_pattern):
        rows, features = tokens.shape

        away = []
        for masks in far:
            away.append(swap(jnp.concatenate([tokens] + away), masks))
        away = jnp.concatenate(away)
        near = [swap(tokens, m) for m in square]
        gate_w = pltpu.with_memory_space_constraint(gate_weight.T, pltpu.HBM)
        (gate_w,) = load((gate_w,), (True,), gate_w)
        away, gate_w = lax.optimization_barrier((away, gate_w))
        there = [swap(away, m) for m in square[:2]]
        away, near[0] = lax.optimization_barrier((away, near[0]))
        there.append(swap(away, square[2]))
        up_w, down_w = load((up_weight.T, down_weight), (True, False), away)
        there[0], *near = lax.optimization_barrier((there[0], *near))
        early = jnp.concatenate([near[1], near[0], near[2], away, there[0], tokens])
        early_there = swap(early, (1, 1))
        gate_w, up_w, early, *there[1:] = lax.optimization_barrier((gate_w, up_w, early, *there[1:]))
        spans = []
        width = features // SPANS
        for k in range(SPANS):
            span = jnp.concatenate([piece[:, k * width : (k + 1) * width] for piece in there[:0:-1]])
            spans.append((span, swap(span, (1, 1))))
        hidden = hidden_units(gate_w, up_w, (early, early_there), spans)

        count = others * rows
        ends = [3 * rows, 3 * rows + count, 3 * rows + 2 * count, 4 * rows + 2 * count]
        ends += [ends[3] + count, ends[3] + 2 * count]
        own_rows = ((ends[2], ends[3]), (rows, 2 * rows), (0, rows), (2 * rows, ends[0]))
        rest_rows = ((ends[0], ends[2]), (ends[4], ends[5]))
        own, diagonal, rest, *sends = down(hidden, down_w, (own_rows, ((ends[3], ends[4]),), rest_rows))
        diagonal = diagonal + swap(sends[1], (1, 1)).astype(jnp.float32)
        diagonal = swap(diagonal.astype(jnp.bfloat16), square[2])
        rest_there, sends[0] = lax.optimization_barrier((swap(sends[2], (1, 1)), sends[0]))
        rest = rest + rest_there.astype(jnp.float32)
        leave = rest[count:].astype(jnp.bfloat16)
        total = rest[:count]
        for piece in (diagonal, swap(leave[:count], square[0]), swap(leave[count:], square[1])):
            total = total + piece.astype(jnp.float32)
        arrived = []
        for masks in reversed(far):
            split = total.shape[0] // 2 // rows * rows
            piece = swap(total[split:].astype(jnp.bfloat16), masks)
            arrived.append(piece[:rows])
            total = total[:split] + piece[rows:].astype(jnp.float32)

        own = own + swap(sends[0], (1, 1)).astype(jnp.float32)
        own = own[: 2 * rows] + swap(own[2 * rows :].astype(jnp.bfloat16), square[1]).astype(jnp.float32)
        arrived.append(swap(own[rows:].astype(jnp.bfloat16), square[0]))
        return rotate(own[:rows], arrived, sign_pattern)

    placed = (P(("groups", "gx"), None), P(None, "gx"), P(None, "gx"), P("gx", None), P())
    return jax.shard_map(
        on_device, mesh=mesh, in_specs=placed, out_specs=P(("groups", "gx"), None), check_vma=False
    )
```
